32 devices in a mesh: req: 8 (over z, x), ep: 4 (over y, core).
Axes of the slice: x: 2, y: 2, z: 4, core: 2. Of those that a mesh axis runs over, the one named last changes fastest.
Arguments:
- hidden: bfloat16 [4096, 1536], P(('req', 'ep')), may hold values from -6 to 6
- parents: int32 [64, 64], P(('req', 'ep')), may hold values from 0 to 62, as said below
- path: int32 [64, 64], P(('req', 'ep')), may hold values from -1 to 63, as said below
- cache_len: int32 [64], P(('req', 'ep')), may hold values from 64 to 1024
- page_table: int32 [64, 8], P(('req', 'ep')), may hold values from 0 to 15, as said below
- kv_pool: bfloat16 [512, 128, 512], P(('req', 'ep')), may hold values from -90 to 90
- mig_slot: int32 [32], P(('req', 'ep')), may hold values from 0 to 1
- mig_dest: int32 [32], P(('req', 'ep')), may hold values from 0 to 3, as said below
- attn_gain: bfloat16 [1536], replicated, may hold values from 0.25 to 1.75
- w_qkv: bfloat16 [1536, 2048], replicated, may hold values from -0.15625 to 0.15625
- w_out: bfloat16 [1536, 1536], replicated, may hold values from -0.15625 to 0.15625
- moe_gain: bfloat16 [1536], replicated, may hold values from 0.25 to 1.75
- w_router: bfloat16 [1536, 32], replicated, may hold values from -0.15625 to 0.15625
- expert_ids: int32 [4096, 4], P(('req', 'ep')), may hold values from 0 to 31, all different within a row; in each aligned block of 128 rows (0 to 127, 128 to 255, ...) at most 32 rows name the same one
- w_gate: bfloat16 [32, 1536, 768], P(('req', 'ep')), may hold values from -0.15625 to 0.15625
- w_up: bfloat16 [32, 1536, 768], P(('req', 'ep')), may hold values from -0.15625 to 0.15625
- w_down: bfloat16 [32, 768, 1536], P(('req', 'ep')), may hold values from -0.21875 to 0.21875
Outputs:
- layer_out: bfloat16 [4096, 1536], P(('req', 'ep'))
- compact_kv: bfloat16 [64, 64, 512], P(('req', 'ep'))
The draws below stay inside these ranges and needn't reach their ends.
Inputs may be any that keep to these rules, and one draw needn't show every extreme that they name: parents[r, 0] = 0 marks the root; for i >= 1, parents[r, i] < i. `path`: row r lists a chain of the tree of parents[r] from the root 0 down to some token, each entry the parent of the next, then -1. `page_table`: the 2 requests of one device name each of its 16 pool pages once. `mig_dest`: within each index of req, the entries of its 4 devices form a permutation. `expert_ids`: each row names 4 different experts; among the rows of one device no expert is named by more than 32 rows.
All inputs are finite; a program needn't handle non-finite values.
Results may differ from the reference program's by a relative error of at most 0.015.
Values may be sent and summed in bfloat16 or wider, within the bound.
No kernel may reach another device: no remote copies, remote signals or barrier semaphores. Data moves between devices by JAX's collectives and lax.ppermute only.
A program may use at most 128 MiB of HBM per device.

```python
import math
import jax
import jax.numpy as jnp
import numpy as np
from jax import lax

D = 1536
QUERY_HEADS = 12
KEY_VALUE_HEADS = 2
HEAD_SIZE = 128
EXPERTS = 32
FF = 768
TOPK = 4
DRAFT_TOKENS = 64
PAGE = 128
CONTEXT_LIMIT = 1024
R_DEV = 2
QKVW = 2048
KVW = 512
PAGES_REQ = 8
POOL = 16
REQUEST_COUNT = 64
TOK_DEV = 128
TOKENS = 4096
SPLIT = 1
FFS = 768
CAP = 32
N_REQ = 8
N_EP = 4
DEVICES = 32


def tree_parents(key):
    base = jax.random.fold_in(key, 11)
    steps = jnp.arange(DRAFT_TOKENS, dtype=jnp.int32)
    spread_pick = jax.random.randint(jax.random.fold_in(base, 1), (REQUEST_COUNT, DRAFT_TOKENS), 0, jnp.maximum(steps, 1)[None, :])
    coin_flip = jax.random.randint(jax.random.fold_in(base, 2), (REQUEST_COUNT, DRAFT_TOKENS), 0, 2)
    chained = jnp.maximum(steps - 1, 0)[None, :]
    parents = jnp.where(coin_flip == 1, chained, spread_pick).astype(jnp.int32)
    return parents.at[0, DRAFT_TOKENS - 1].set(DRAFT_TOKENS - 2)


def draw_parents(key, part):
    return tree_parents(key)


def draw_path(key, part):
    parents = tree_parents(key)
    backward = jax.random.randint(jax.random.fold_in(key, 23), (REQUEST_COUNT,), 0, max(1, DRAFT_TOKENS // 4))
    leaves = (DRAFT_TOKENS - 1 - backward).astype(jnp.int32).at[0].set(DRAFT_TOKENS - 1)

    def walk(parent_row, leaf_node):

        def stepper(current, unused_item):
            return (parent_row[current], current)
        unused_last, trail = lax.scan(stepper, leaf_node, None, length=DRAFT_TOKENS)
        depth_count = jnp.sum((trail != 0).astype(jnp.int32))
        columns = jnp.arange(DRAFT_TOKENS, dtype=jnp.int32)
        lookup = jnp.clip(depth_count - columns, 0, DRAFT_TOKENS - 1)
        return jnp.where(columns <= depth_count, trail[lookup], -1).astype(jnp.int32)
    return jax.vmap(walk)(parents, leaves)


def draw_cache_len(key, part):
    drawn = jax.random.randint(jax.random.fold_in(key, 5), (REQUEST_COUNT,), CONTEXT_LIMIT // 16, CONTEXT_LIMIT + 1).astype(jnp.int32)
    return drawn.at[0].set(CONTEXT_LIMIT).at[1].set(CONTEXT_LIMIT // 16)


def draw_page_table(key, part):

    def one_device(index):
        return jax.random.permutation(jax.random.fold_in(key, index + 31), POOL).astype(jnp.int32)
    tables = jax.vmap(one_device)(jnp.arange(N_REQ * N_EP, dtype=jnp.int32))
    return tables.reshape(REQUEST_COUNT, PAGES_REQ)


def draw_mig_dest(key, part):

    def one_group(index):
        return jax.random.permutation(jax.random.fold_in(key, index + 7), N_EP).astype(jnp.int32)
    return jax.vmap(one_group)(jnp.arange(N_REQ, dtype=jnp.int32)).reshape(N_REQ * N_EP)


def draw_kv_pool(key, part):
    shape_all = (N_REQ * N_EP * POOL, PAGE, KVW)
    first_key = jax.random.fold_in(key, 41)
    return jnp.clip(jax.random.normal(first_key, shape_all, jnp.float32), -6.0, 6.0).astype(jnp.bfloat16)


def set_ends(values, rng, smallest, top_value):
    place = [jax.random.randint(jax.random.fold_in(rng, axis), (), 0, length) for axis, length in enumerate(values.shape)]
    longest = values.shape.index(max(values.shape))
    neighbour = place[:longest] + [(place[longest] + 1) % values.shape[longest]] + place[longest + 1:]
    return values.at[tuple(place)].set(smallest).at[tuple(neighbour)].set(top_value)


def level_of(own_key, extent, cuts, low, high):
    def one(axis_at, parts):
        draws = jax.random.uniform(jax.random.fold_in(jax.random.fold_in(own_key, 6), axis_at), (parts,), jnp.float32, low / len(cuts), high / len(cuts))
        return jnp.repeat(jnp.exp(draws), extent[axis_at] // parts).reshape((-1,) + (1,) * (len(extent) - axis_at - 1))

    loudness = one(*cuts[0])
    for cut in cuts[1:]:
        loudness = loudness * one(*cut)
    return loudness


def deal_out(rng, own, number, rows, number_of, top, bound, skew):
    order = jax.random.permutation(rng, number_of)
    packed, usual = portions_of(number_of, rows * top, bound, skew, True), portions_of(number_of, rows * top, bound, skew, False)
    places = jnp.arange(number_of)

    def named(sizes, turn):
        used = int((sizes > 0).sum())
        fixed = max(1, used // 4)
        moved = fixed + (places - fixed + turn * (used - fixed)) % max(1, number_of - fixed)
        return jnp.zeros((number_of,), jnp.int32).at[order[jnp.where(places < fixed, places, moved)]].set(jnp.asarray(sizes, jnp.int32))

    sizes = jnp.where(number % 4 == 0, named(packed, number // 4), named(usual, number - number // 4 - 1))
    mixed = jax.random.permutation(jax.random.fold_in(own, 3), number_of)
    donor, receiver = mixed[0:number_of // 2 * 2:2], mixed[1:number_of // 2 * 2:2]
    room = jnp.minimum(sizes[donor] - 1, bound - sizes[receiver]) // 2
    room = jnp.where((donor == order[0]) | (receiver == order[0]) | (sizes[receiver] == 0), 0, jnp.maximum(room, 0))
    moved = jax.random.randint(jax.random.fold_in(own, 4), (number_of // 2,), 0, 1 << 20) % (room + 1)
    sizes = sizes.at[donor].add(-moved).at[receiver].add(moved)
    members = jnp.searchsorted(jnp.cumsum(sizes), jnp.arange(rows * top), side="right").astype(jnp.int32)
    table = members.reshape(top, rows).T
    table = table[jax.random.permutation(jax.random.fold_in(own, 1), rows)]
    turn = jax.random.randint(jax.random.fold_in(own, 2), (rows, 1), 0, top)
    return jnp.take_along_axis(table, (jnp.arange(top)[None, :] + turn) % top, axis=1)


def portions_of(number_of, total, bound, slope, full):
    loads = [(1 << 20) // math.isqrt(grade ** slope) + 1 for grade in range(1, number_of + 1)]
    largest = bound if full else min(bound, max(-(-total // number_of), total * loads[0] // sum(loads)))
    least = 1 if total - largest >= number_of - 1 else 0
    holding, spare = [largest] + [least] * (number_of - 1), total - largest - least * (number_of - 1)
    while spare > 0:
        free = [i for i in range(1, number_of) if holding[i] < largest] or [i for i in range(1, number_of) if holding[i] < bound]
        whole, left = sum([loads[i] for i in free]), spare
        for i in free:
            more = min(bound - holding[i], max(1, left * loads[i] // whole), spare)
            holding[i] = holding[i] + more
            spare = spare - more
    return np.array(holding)


def gaussian(stream_key, shape, width, bound, split=(), held_as=jnp.bfloat16):
    gain = level_of(stream_key, shape, split, -0.22, 0.18) if split else 1.0
    values = jax.random.normal(stream_key, shape, jnp.float32) * width * gain
    return jnp.minimum(jnp.maximum(values, -bound), bound).astype(held_as)


def setup_inputs(seed: int = 0) -> dict:
    key_of = jax.random.split(jax.random.key(seed), 18)
    hidden = gaussian(key_of[0], (TOKENS, D), 1.0, 6.0, ((0, 32),))
    parents = draw_parents(jax.random.fold_in(key_of[17], 71), 0)
    path = draw_path(jax.random.fold_in(key_of[17], 71), 0)
    cache_len = draw_cache_len(jax.random.fold_in(key_of[17], 71), 0)
    page_table = draw_page_table(jax.random.fold_in(key_of[17], 71), 0)
    kv_pool = draw_kv_pool(jax.random.fold_in(key_of[17], 71), 0)
    mig_slot = set_ends(jax.random.randint(key_of[6], (DEVICES,), 0, R_DEV), jax.random.fold_in(key_of[6], 1), 0, R_DEV - 1).astype(jnp.int32)
    mig_dest = draw_mig_dest(jax.random.fold_in(key_of[17], 71), 0)
    attn_gain = jnp.clip(1.0 + 0.15 * jax.random.normal(key_of[8], (D,), jnp.float32), 0.25, 1.75).astype(jnp.bfloat16)
    w_qkv = gaussian(key_of[9], (D, QKVW), D ** -0.5, 0.15625)
    w_out = gaussian(key_of[10], (QUERY_HEADS * HEAD_SIZE, D), (QUERY_HEADS * HEAD_SIZE) ** -0.5, 0.15625)
    moe_gain = jnp.clip(1.0 + 0.15 * jax.random.normal(key_of[11], (D,), jnp.float32), 0.25, 1.75).astype(jnp.bfloat16)
    w_router = gaussian(key_of[12], (D, EXPERTS), D ** -0.5, 0.15625)
    expert_ids_keys = jax.random.split(jax.random.fold_in(key_of[13], 1), TOKENS // TOK_DEV)
    expert_ids_turns = jax.random.permutation(jax.random.fold_in(key_of[13], 3), TOKENS // TOK_DEV)
    expert_ids = jax.vmap(lambda own, number: deal_out(jax.random.fold_in(key_of[13], 2), own, number, TOK_DEV, EXPERTS, TOPK, CAP, 2))(expert_ids_keys, expert_ids_turns).reshape((TOKENS, TOPK))
    w_gate = gaussian(key_of[14], (EXPERTS * SPLIT, D, FFS), D ** -0.5, 0.15625, ((0, 32),))
    w_up = gaussian(key_of[15], (EXPERTS * SPLIT, D, FFS), D ** -0.5, 0.15625, ((0, 32),))
    w_down = gaussian(key_of[16], (EXPERTS * SPLIT, FFS, D), FF ** -0.5, 0.21875, ((0, 32),))
    return dict(hidden=hidden, parents=parents, path=path, cache_len=cache_len, page_table=page_table, kv_pool=kv_pool, mig_slot=mig_slot, mig_dest=mig_dest, attn_gain=attn_gain, w_qkv=w_qkv, w_out=w_out, moe_gain=moe_gain, w_router=w_router, expert_ids=expert_ids, w_gate=w_gate, w_up=w_up, w_down=w_down)


EPSILON = 1e-06
ROPE_BASE = 1000000.0
PRECISE = lax.Precision.HIGHEST
MASKED = -1e+30

def rms_scale(values, scaling):
    widened = values.astype(jnp.float32)
    spread = lax.optimization_barrier(jnp.mean(widened * widened, axis=-1, keepdims=True))
    return (widened * lax.rsqrt(spread + EPSILON) * scaling.astype(jnp.float32)).astype(jnp.bfloat16)

def ancestry(parent_row):
    length = parent_row.shape[-1]
    indices = jnp.arange(length, dtype=jnp.int32)
    linked = (parent_row[:, None] == indices[None, :]).astype(jnp.float32)
    reached = jnp.minimum(linked + jnp.eye(length, dtype=jnp.float32), 1.0)
    for repeat_index in range(max(1, (length - 1).bit_length())):
        reached = jnp.minimum(jnp.dot(reached, reached, precision=PRECISE), 1.0)
    return reached

def apply_rotary(tensor, token_positions):
    halfway = tensor.shape[-1] // 2
    spectrum = ROPE_BASE ** (-2.0 * jnp.arange(halfway, dtype=jnp.float32) / tensor.shape[-1])
    angles = token_positions[..., None] * spectrum
    cosine = jnp.cos(angles)[..., None, :]
    sine_part = jnp.sin(angles)[..., None, :]
    former = tensor[..., :halfway]
    latter = tensor[..., halfway:]
    return jnp.concatenate([former * cosine - latter * sine_part, latter * cosine + former * sine_part], axis=-1)

def take_rows(source_rows, row_ids):
    return source_rows[row_ids]

def reference(hidden, parents, path, cache_len, page_table, kv_pool, mig_slot, mig_dest, attn_gain, w_qkv, w_out, moe_gain, w_router, expert_ids, w_gate, w_up, w_down):
    device_count = N_REQ * N_EP
    device_ids = jnp.arange(device_count, dtype=jnp.int32)
    target = device_ids // N_EP * N_EP + mig_dest
    source = jnp.zeros((device_count,), jnp.int32).at[target].set(device_ids)
    request_ids = jnp.arange(REQUEST_COUNT, dtype=jnp.int32)
    holder = request_ids // R_DEV
    within = request_ids % R_DEV
    sender = source[holder]
    anchor = jnp.where(within == mig_slot[holder], sender * R_DEV + mig_slot[sender], request_ids)
    lengths = cache_len[anchor]
    page_rows = (anchor // R_DEV)[:, None] * POOL + page_table[anchor]
    tree_reach = jax.vmap(ancestry)(parents)
    tree_depth = lax.optimization_barrier(jnp.sum(tree_reach, axis=-1)) - 1.0
    token_positions = lengths.astype(jnp.float32)[:, None] + tree_depth
    query_width = QUERY_HEADS * HEAD_SIZE
    key_width = KEY_VALUE_HEADS * HEAD_SIZE
    normed = rms_scale(hidden, attn_gain)
    projected_input = jnp.dot(normed, w_qkv, preferred_element_type=jnp.float32).reshape(REQUEST_COUNT, DRAFT_TOKENS, QKVW)
    query_rows = apply_rotary(projected_input[..., :query_width].reshape(REQUEST_COUNT, DRAFT_TOKENS, QUERY_HEADS, HEAD_SIZE), token_positions).astype(jnp.bfloat16)
    newest_keys = apply_rotary(projected_input[..., query_width:query_width + key_width].reshape(REQUEST_COUNT, DRAFT_TOKENS, KEY_VALUE_HEADS, HEAD_SIZE), token_positions).astype(jnp.bfloat16)
    newest_values = projected_input[..., query_width + key_width:].astype(jnp.bfloat16)
    fresh_kv = jnp.concatenate([newest_keys.reshape(REQUEST_COUNT, DRAFT_TOKENS, key_width), newest_values], axis=-1)

    def one_request(operands):
        request_query, request_kv, request_pages, cache_length, reached = operands
        cached = kv_pool[request_pages].reshape(CONTEXT_LIMIT, KVW)
        merged_heads = jnp.concatenate([cached, request_kv], axis=0)
        key_head_rows = merged_heads[:, :key_width].reshape(CONTEXT_LIMIT + DRAFT_TOKENS, KEY_VALUE_HEADS, HEAD_SIZE).astype(jnp.float32)
        value_head_rows = merged_heads[:, key_width:].reshape(CONTEXT_LIMIT + DRAFT_TOKENS, KEY_VALUE_HEADS, HEAD_SIZE).astype(jnp.float32)
        grouped_query = request_query.reshape(DRAFT_TOKENS, KEY_VALUE_HEADS, QUERY_HEADS // KEY_VALUE_HEADS, HEAD_SIZE).astype(jnp.float32)
        scores = jnp.einsum('skgd,lkd->kgsl', grouped_query, key_head_rows, precision=PRECISE) * HEAD_SIZE ** (-0.5)
        in_cache = jnp.broadcast_to(jnp.arange(CONTEXT_LIMIT, dtype=jnp.int32)[None, :] < cache_length, (DRAFT_TOKENS, CONTEXT_LIMIT))
        allowed = jnp.concatenate([in_cache, reached > 0.5], axis=1)
        scores = jnp.where(allowed[None, None], scores, MASKED)
        highest = lax.optimization_barrier(jnp.max(scores, axis=-1, keepdims=True))
        weights = jnp.exp(scores - highest)
        totals = lax.optimization_barrier(jnp.sum(weights, axis=-1, keepdims=True))
        mixed = jnp.einsum('kgsl,lkd->kgsd', weights, value_head_rows, precision=PRECISE) / totals
        return jnp.transpose(mixed, (2, 0, 1, 3)).reshape(DRAFT_TOKENS, query_width)
    attended = lax.map(one_request, (query_rows.reshape(REQUEST_COUNT, DRAFT_TOKENS, query_width), fresh_kv, page_rows, lengths, tree_reach)).astype(jnp.bfloat16)
    projected_out = jnp.dot(attended.reshape(TOKENS, query_width), w_out, preferred_element_type=jnp.float32)
    residual_mid = (hidden.astype(jnp.float32) + projected_out).astype(jnp.bfloat16)
    picked_kv = jax.vmap(take_rows)(fresh_kv, jnp.maximum(path, 0))
    compact_kv = jnp.where((path >= 0)[..., None], picked_kv, jnp.zeros((), jnp.bfloat16))
    normed_moe = rms_scale(residual_mid, moe_gain)
    logits = jnp.dot(normed_moe, w_router, preferred_element_type=jnp.float32)
    chosen = jnp.take_along_axis(logits, expert_ids, axis=1)
    squashed = jax.nn.sigmoid(chosen)
    gate_share = squashed / lax.optimization_barrier(jnp.sum(squashed, axis=1, keepdims=True))
    row_limit = N_REQ * N_EP * CAP

    def expert_step(total_moe, expert):
        matches = expert_ids == expert
        chosen_any = jnp.any(matches, axis=1)
        share = lax.optimization_barrier(jnp.sum(jnp.where(matches, gate_share, 0.0), axis=1))
        picked = jnp.nonzero(chosen_any, size=row_limit, fill_value=0)[0]
        valid = jnp.arange(row_limit, dtype=jnp.int32) < jnp.sum(chosen_any.astype(jnp.int32))
        chosen_rows = normed_moe[picked].astype(jnp.float32)
        start = (expert * SPLIT).astype(jnp.int32)
        gate_block = lax.dynamic_slice_in_dim(w_gate, start, SPLIT, 0).astype(jnp.float32)
        up_block = lax.dynamic_slice_in_dim(w_up, start, SPLIT, 0).astype(jnp.float32)
        down_block = lax.dynamic_slice_in_dim(w_down, start, SPLIT, 0).astype(jnp.float32)
        gate_val = jnp.einsum('nd,sdf->nsf', chosen_rows, gate_block, precision=PRECISE)
        up_val = jnp.einsum('nd,sdf->nsf', chosen_rows, up_block, precision=PRECISE)
        activated = (jnp.maximum(gate_val, 0.0) * up_val).astype(jnp.bfloat16)
        pieces = jnp.einsum('nsf,sfd->nsd', activated.astype(jnp.float32), down_block, precision=PRECISE).astype(jnp.bfloat16)
        expert_rows = lax.optimization_barrier(jnp.sum(pieces.astype(jnp.float32), axis=1))
        weighted = jnp.where(valid[:, None], share[picked][:, None] * expert_rows, 0.0)
        return (total_moe.at[picked].add(weighted), None)
    moe_sum, unused_out = lax.scan(expert_step, jnp.zeros((TOKENS, D), jnp.float32), jnp.arange(EXPERTS, dtype=jnp.int32))
    layer_out = (residual_mid.astype(jnp.float32) + moe_sum).astype(jnp.bfloat16)
    return (layer_out, compact_kv)
```

```python
import functools

import jax
import jax.numpy as jnp
import numpy as np
from jax import lax
from jax.experimental import pallas as pl
from jax.experimental.pallas import tpu as pltpu
from jax.sharding import PartitionSpec as P

QUERY_HEADS = 12
KEY_VALUE_HEADS = 2
HEAD_SIZE = 128
GROUP = QUERY_HEADS // KEY_VALUE_HEADS
CAP = 32
EPSILON = 1e-06
ROPE_BASE = 1000000.0
MASKED = -1e30
MIB = 1024 * 1024
AXES = ("req", "ep")

VMEM = pl.BlockSpec(memory_space=pltpu.VMEM)
SMEM = pl.BlockSpec(memory_space=pltpu.SMEM)
ANY = pl.BlockSpec(memory_space=pl.ANY)


def dot(a, b, dims=((1,), (0,))):
    return lax.dot_general(a, b, (dims, ((), ())), preferred_element_type=jnp.float32)


def rms_scale(values, scaling):
    widened = values.astype(jnp.float32)
    spread = jnp.mean(widened * widened, axis=-1, keepdims=True)
    return (widened * lax.rsqrt(spread + EPSILON) * scaling.astype(jnp.float32)).astype(
        jnp.bfloat16
    )


def attend(queries, cached, fresh, reach, length):
    scale = HEAD_SIZE ** (-0.5)
    key_width = KEY_VALUE_HEADS * HEAD_SIZE
    context = cached.shape[0]
    rows = queries.shape[0] * GROUP
    in_cache = lax.broadcasted_iota(jnp.int32, (rows, context), 1) < length
    in_tree = jnp.concatenate([reach] * GROUP, axis=0) > 0.5
    outs = []
    for kv in range(KEY_VALUE_HEADS):
        cols = slice(kv * HEAD_SIZE, (kv + 1) * HEAD_SIZE)
        vcols = slice(key_width + kv * HEAD_SIZE, key_width + (kv + 1) * HEAD_SIZE)
        heads = [
            queries[:, (kv * GROUP + g) * HEAD_SIZE : (kv * GROUP + g + 1) * HEAD_SIZE]
            for g in range(GROUP)
        ]
        stacked = jnp.concatenate(heads, axis=0)
        first = dot(stacked, cached[:, cols], ((1,), (1,))) * scale
        first = jnp.where(in_cache, first, MASKED)
        second = dot(stacked, fresh[:, cols], ((1,), (1,))) * scale
        second = jnp.where(in_tree, second, MASKED)
        highest = jnp.maximum(
            jnp.max(first, axis=-1, keepdims=True), jnp.max(second, axis=-1, keepdims=True)
        )
        first = jnp.exp(first - highest)
        second = jnp.exp(second - highest)
        total = jnp.sum(first, axis=-1, keepdims=True) + jnp.sum(second, axis=-1, keepdims=True)
        mixed = dot(first.astype(jnp.bfloat16), cached[:, vcols])
        mixed = mixed + dot(second.astype(jnp.bfloat16), fresh[:, vcols])
        mixed = (mixed / total).astype(jnp.bfloat16)
        step = queries.shape[0]
        outs += [mixed[g * step : (g + 1) * step] for g in range(GROUP)]
    return jnp.concatenate(outs, axis=1)


def leaving_kernel(meta, table, pool, out, sems):
    slot = meta[0]
    page = pool.shape[1]
    copies = []
    for i in range(table.shape[1]):
        copies.append(
            pltpu.make_async_copy(
                pool.at[table[slot, i]], out.at[pl.ds(i * page, page)], sems.at[i]
            )
        )
    for copy in copies:
        copy.start()
    for copy in copies:
        copy.wait()


def routes_kernel(base, split, ids_t, table):
    tokens = ids_t.shape[1]
    shown = table.shape[0] // (split * CAP)
    names = lax.broadcasted_iota(jnp.int32, (shown, tokens), 0) + base[0]
    assigned = jnp.zeros((shown, tokens), jnp.bool_)
    for k in range(ids_t.shape[0]):
        assigned = assigned | (ids_t[k : k + 1, :] == names)
    before = lax.broadcasted_iota(jnp.int32, (tokens, tokens), 0) < lax.broadcasted_iota(
        jnp.int32, (tokens, tokens), 1
    )
    ones = assigned.astype(jnp.float32)
    ranks = dot(ones.astype(jnp.bfloat16), before.astype(jnp.float32).astype(jnp.bfloat16))
    slots = jnp.where(assigned, ranks.astype(jnp.int32), -1)
    wanted = lax.broadcasted_iota(jnp.int32, (shown, split * CAP, tokens), 1) % CAP
    hot = jnp.where(slots[:, None, :] == wanted, 1.0, 0.0)
    table[...] = hot.reshape(table.shape).astype(jnp.bfloat16)


def shares_kernel(base, split, experts, normed, w_router, ids, high, low):
    tokens = ids.shape[0]
    width = high.shape[1]
    shown = width // (split * CAP)
    logits = dot(normed[...], w_router[...])
    names = lax.broadcasted_iota(jnp.int32, (tokens, experts), 1)
    assigned = jnp.zeros((tokens, experts), jnp.bool_)
    for k in range(ids.shape[1]):
        assigned = assigned | (ids[:, k : k + 1] == names)
    squashed = jnp.where(assigned, jax.nn.sigmoid(logits), 0.0)
    share = squashed / jnp.sum(squashed, axis=1, keepdims=True)
    before = lax.broadcasted_iota(jnp.int32, (tokens, tokens), 1) < lax.broadcasted_iota(
        jnp.int32, (tokens, tokens), 0
    )
    ones = assigned.astype(jnp.float32).astype(jnp.bfloat16)
    ranks = dot(before.astype(jnp.float32).astype(jnp.bfloat16), ones)
    slots = jnp.where(assigned, ranks, -1.0).astype(jnp.bfloat16)
    spread = (
        lax.broadcasted_iota(jnp.int32, (experts, width), 1) // (split * CAP) + base[0]
        == lax.broadcasted_iota(jnp.int32, (experts, width), 0)
    )
    spread = spread.astype(jnp.float32).astype(jnp.bfloat16)
    wanted = lax.broadcasted_iota(jnp.int32, (tokens, width), 1) % CAP
    hit = dot(slots, spread).astype(jnp.int32) == wanted
    share_high = share.astype(jnp.bfloat16)
    share_low = (share - share_high.astype(jnp.float32)).astype(jnp.bfloat16)
    high[...] = jnp.where(hit, dot(share_high, spread), 0.0).astype(jnp.bfloat16)
    low[...] = jnp.where(hit, dot(share_low, spread), 0.0).astype(jnp.bfloat16)


def front_kernel(
    meta, table, hidden, parents, path, spectrum, gain, w_qkv, w_out, pool,
    queries, fresh, reach, compact, staying, cache, sems,
):
    stay = 1 - meta[0]
    page = pool.shape[1]
    copies = []
    for i in range(table.shape[1]):
        copies.append(
            pltpu.make_async_copy(
                pool.at[table[stay, i]], cache.at[pl.ds(i * page, page)], sems.at[i]
            )
        )
    for copy in copies:
        copy.start()
    requests = meta.shape[0] - 1
    draft = hidden.shape[0] // requests
    query_width = queries.shape[1]
    key_width = KEY_VALUE_HEADS * HEAD_SIZE
    normed = rms_scale(hidden[...], gain[...])
    projected = dot(normed, w_qkv[...])
    names = lax.broadcasted_iota(jnp.int32, (draft, draft), 1)
    itself = names == lax.broadcasted_iota(jnp.int32, (draft, draft), 0)
    turned = lax.broadcasted_iota(jnp.int32, (1, HEAD_SIZE), 1) < HEAD_SIZE // 2
    for r in range(requests):
        rows = slice(r * draft, (r + 1) * draft)
        linked = parents[rows, :] == names
        reached = jnp.where(linked | itself, 1.0, 0.0)
        for _ in range(max(1, (draft - 1).bit_length())):
            half = reached.astype(jnp.bfloat16)
            reached = jnp.minimum(dot(half, half), 1.0)
        depth = jnp.sum(reached, axis=-1, keepdims=True) - 1.0
        angles = (depth + meta[1 + r].astype(jnp.float32)) * spectrum[...]
        cosine = jnp.cos(angles)
        sine = jnp.sin(angles)
        sine = jnp.where(turned, -sine, sine)
        for h in range(QUERY_HEADS + KEY_VALUE_HEADS):
            part = projected[rows, h * HEAD_SIZE : (h + 1) * HEAD_SIZE]
            swapped = jnp.concatenate(
                [part[:, HEAD_SIZE // 2 :], part[:, : HEAD_SIZE // 2]], axis=1
            )
            rotated = (part * cosine + swapped * sine).astype(jnp.bfloat16)
            if h < QUERY_HEADS:
                queries[rows, h * HEAD_SIZE : (h + 1) * HEAD_SIZE] = rotated
            else:
                at = (h - QUERY_HEADS) * HEAD_SIZE
                fresh[rows, at : at + HEAD_SIZE] = rotated
        fresh[rows, key_width:] = projected[rows, query_width + key_width :].astype(jnp.bfloat16)
        reach[rows, :] = reached
        picked = jnp.where(path[rows, :] == names, 1.0, 0.0).astype(jnp.bfloat16)
        compact[rows, :] = dot(picked, fresh[rows, :]).astype(jnp.bfloat16)
    for copy in copies:
        copy.wait()
    own = pl.ds(pl.multiple_of(stay * draft, draft), draft)
    attended = attend(queries[own, :], cache, fresh[own, :], reach[own, :], meta[1 + stay])
    projected_out = dot(attended, w_out[...])
    staying[...] = (hidden[own, :].astype(jnp.float32) + projected_out).astype(jnp.bfloat16)


def arrival_kernel(
    meta, select, hidden, queries, fresh, reach, staying, gain, routes, w_out, *rest,
):
    sources = rest[:-8]
    residual, normed, packed, cache, weights, sem, weight_sem, _ = rest[-8:]
    load = pltpu.make_async_copy(w_out, weights, weight_sem)
    load.start()
    for i, source in enumerate(sources):

        @pl.when(select[0] == i)
        def _(source=source):
            copy = pltpu.make_async_copy(source, cache, sem)
            copy.start()
            copy.wait()

    slot = meta[0]
    draft = staying.shape[0]
    own = pl.ds(pl.multiple_of(slot * draft, draft), draft)
    other = pl.ds(pl.multiple_of((1 - slot) * draft, draft), draft)
    attended = attend(queries[own, :], cache, fresh[own, :], reach[own, :], meta[1 + slot])
    load.wait()
    projected_out = dot(attended, weights[...])
    residual[own, :] = (hidden[own, :].astype(jnp.float32) + projected_out).astype(jnp.bfloat16)
    residual[other, :] = staying[...]
    scaled = rms_scale(residual[...], gain[...])
    normed[...] = scaled
    packed[...] = dot(routes[...], scaled).astype(jnp.bfloat16)


def pack_kernel(routes, normed, packed):
    packed[...] = dot(routes[...], normed[...]).astype(jnp.bfloat16)


def expert_kernel(rows, w_gate, w_up, w_down, out, total):
    step = pl.program_id(0)
    gated = dot(rows[...], w_gate[0])
    upped = dot(rows[...], w_up[0])
    activated = (jnp.maximum(gated, 0.0) * upped).astype(jnp.bfloat16)
    piece = dot(activated, w_down[0])

    @pl.when(step == 0)
    def _():
        total[...] = piece

    @pl.when(step > 0)
    def _():
        total[...] += piece

    @pl.when(step == pl.num_programs(0) - 1)
    def _():
        out[...] = total[...].astype(jnp.bfloat16)


def partial_kernel(high, low, rows, out):
    values = rows[...]
    out[...] = (dot(high[...], values) + dot(low[...], values)).astype(jnp.bfloat16)


def final_kernel(residual, high, low, rows, far, out):
    values = rows[...]
    total = dot(high[...], values) + dot(low[...], values) + far[...].astype(jnp.float32)
    out[...] = (residual[...].astype(jnp.float32) + total).astype(jnp.bfloat16)


def params(mib):
    return pltpu.CompilerParams(vmem_limit_bytes=mib * MIB)


def cost(flops, moved):
    return pl.CostEstimate(flops=int(flops), bytes_accessed=int(moved), transcendentals=0)


def run_experts(rows, w_gate, w_up, w_down):
    count, model = rows.shape
    hidden_units = w_gate.shape[2]
    chunk = 256 if hidden_units % 256 == 0 else hidden_units
    return pl.pallas_call(
        expert_kernel,
        grid=(hidden_units // chunk,),
        in_specs=[
            pl.BlockSpec((count, model), lambda f: (0, 0)),
            pl.BlockSpec((1, model, chunk), lambda f: (0, 0, f)),
            pl.BlockSpec((1, model, chunk), lambda f: (0, 0, f)),
            pl.BlockSpec((1, chunk, model), lambda f: (0, f, 0)),
        ],
        out_specs=pl.BlockSpec((count, model), lambda f: (0, 0)),
        out_shape=jax.ShapeDtypeStruct((count, model), jnp.bfloat16),
        scratch_shapes=[pltpu.VMEM((count, model), jnp.float32)],
        compiler_params=params(50),
        cost_estimate=cost(6 * count * model * hidden_units, 6 * model * hidden_units),
        name="experts",
    )(rows, w_gate, w_up, w_down)


def per_device(
    hidden, parents, path, cache_len, page_table, kv_pool, mig_slot, mig_dest,
    attn_gain, w_qkv, w_out, moe_gain, w_router, expert_ids, w_gate, w_up, w_down,
):
    bf16 = jnp.bfloat16
    requests, draft = parents.shape
    tokens, model = hidden.shape
    req_count = lax.axis_size("req")
    ep_count = lax.axis_size("ep")
    device_count = req_count * ep_count
    half_count = device_count // 2
    experts = w_router.shape[1]
    split = device_count // experts
    pages = page_table.shape[1]
    page, kv_width = kv_pool.shape[1:]
    context = pages * page
    query_width = w_out.shape[0]
    slot_rows = half_count * CAP
    req_index = lax.axis_index("req")
    ep_index = lax.axis_index("ep")
    groups = [[h * half_count + i for i in range(half_count)] for h in range(2)]
    swap = [(i, (i + req_count // 2) % req_count) for i in range(req_count)]
    base = (req_index // (req_count // 2) * (experts // 2)).astype(jnp.int32).reshape(1)

    def within_half(rows):
        return lax.all_to_all(rows, AXES, 0, 0, tiled=True, axis_index_groups=groups)

    leave_len = lax.dynamic_index_in_dim(cache_len, mig_slot[0], 0, keepdims=False)
    note = jnp.stack([mig_dest[0], leave_len])
    notes = lax.all_to_all(
        jnp.broadcast_to(note[None], (ep_count, 2)), "ep", 0, 0, tiled=True
    )
    leaving = pl.pallas_call(
        leaving_kernel,
        in_specs=[SMEM, SMEM, ANY],
        out_specs=ANY,
        out_shape=jax.ShapeDtypeStruct((context, kv_width), bf16),
        scratch_shapes=[pltpu.SemaphoreType.DMA((pages,))],
        cost_estimate=cost(0, 4 * context * kv_width),
        name="leaving",
    )(mig_slot, page_table, kv_pool)
    sibling = lax.ppermute(leaving, "ep", [(i, i ^ 1) for i in range(ep_count)])
    far_ids = lax.ppermute(expert_ids, "req", swap)
    chips = ep_count // 2
    chip = ep_index // 2
    core = ep_index % 2
    arrivals = []
    for k in range(1, chips):
        target = (chip + k) % chips * 2 + core
        payload = jnp.where(mig_dest[0] == target, leaving, sibling)
        moves = [(i, ((i // 2 + k) % chips) * 2 + i % 2) for i in range(ep_count)]
        arrivals.append(lax.ppermute(payload, "ep", moves))
    ep_ids = jnp.arange(ep_count, dtype=jnp.int32)
    for_me = notes[:, 0] == ep_index
    sender = jnp.sum(jnp.where(for_me, ep_ids, 0))
    arrived_len = jnp.sum(jnp.where(for_me, notes[:, 1], 0))
    lengths = jnp.where(jnp.arange(requests) == mig_slot[0], arrived_len, cache_len)
    meta = jnp.concatenate([mig_slot, lengths]).astype(jnp.int32)
    hop = (chip - sender // 2) % chips
    select = jnp.where(
        hop > 0, hop + 1, jnp.where(sender == ep_index, 0, 1)
    ).astype(jnp.int32).reshape(1)

    def routes_of(ids):
        return pl.pallas_call(
            lambda b, i, o: routes_kernel(b, split, i, o),
            in_specs=[SMEM, VMEM],
            out_specs=VMEM,
            out_shape=jax.ShapeDtypeStruct((slot_rows, tokens), bf16),
            name="routes",
        )(base, ids.T)

    routes = routes_of(expert_ids)
    far_routes = routes_of(far_ids)

    frequencies = ROPE_BASE ** (-2.0 * np.arange(HEAD_SIZE // 2) / HEAD_SIZE)
    spectrum = jnp.asarray(np.concatenate([frequencies] * 2)[None].astype(np.float32))
    queries, fresh, reach, compact, staying = pl.pallas_call(
        front_kernel,
        in_specs=[SMEM, SMEM] + [VMEM] * 7 + [ANY],
        out_specs=[VMEM] * 5,
        out_shape=[
            jax.ShapeDtypeStruct((tokens, query_width), bf16),
            jax.ShapeDtypeStruct((tokens, kv_width), bf16),
            jax.ShapeDtypeStruct((tokens, draft), jnp.float32),
            jax.ShapeDtypeStruct((tokens, kv_width), bf16),
            jax.ShapeDtypeStruct((draft, model), bf16),
        ],
        scratch_shapes=[
            pltpu.VMEM((context, kv_width), bf16),
            pltpu.SemaphoreType.DMA((pages,)),
        ],
        compiler_params=params(48),
        cost_estimate=cost(12e9, 24e6),
        name="front",
    )(
        meta, page_table, hidden, parents.reshape(tokens, 1), path.reshape(tokens, 1), spectrum,
        attn_gain.reshape(1, model), w_qkv, w_out, kv_pool,
    )
    sources = [leaving, sibling] + arrivals
    residual, normed, packed = pl.pallas_call(
        arrival_kernel,
        in_specs=[SMEM, SMEM] + [VMEM] * 7 + [ANY] * (1 + len(sources)),
        out_specs=[VMEM] * 3,
        out_shape=[
            jax.ShapeDtypeStruct((tokens, model), bf16),
            jax.ShapeDtypeStruct((tokens, model), bf16),
            jax.ShapeDtypeStruct((slot_rows, model), bf16),
        ],
        scratch_shapes=[
            pltpu.VMEM((context, kv_width), bf16),
            pltpu.VMEM(w_out.shape, bf16),
            pltpu.SemaphoreType.DMA,
            pltpu.SemaphoreType.DMA,
            pltpu.SemaphoreType.DMA,
        ],
        compiler_params=params(48),
        cost_estimate=cost(4e9, 8e6),
        name="arrival",
    )(
        meta, select, hidden, queries, fresh, reach, staying, moe_gain.reshape(1, model),
        routes, w_out, *sources,
    )
    far_normed = lax.ppermute(normed, "req", swap)
    near_rows = within_half(packed)
    far_packed = pl.pallas_call(
        pack_kernel,
        in_specs=[VMEM] * 2,
        out_specs=VMEM,
        out_shape=jax.ShapeDtypeStruct((slot_rows, model), bf16),
        name="pack",
    )(far_routes, far_normed)
    far_rows = within_half(far_packed)

    def shares_of(ids, values):
        return pl.pallas_call(
            lambda b, n, w, i, h, l: shares_kernel(b, split, experts, n, w, i, h, l),
            in_specs=[SMEM] + [VMEM] * 3,
            out_specs=[VMEM] * 2,
            out_shape=[jax.ShapeDtypeStruct((tokens, slot_rows), bf16)] * 2,
            name="shares",
        )(base, values, w_router, ids)

    near_high, near_low = shares_of(expert_ids, normed)
    far_high, far_low = shares_of(far_ids, far_normed)
    near_out = run_experts(near_rows, w_gate, w_up, w_down)
    far_out = run_experts(far_rows, w_gate, w_up, w_down)
    far_back = within_half(far_out)
    far_sum = pl.pallas_call(
        partial_kernel,
        in_specs=[VMEM] * 3,
        out_specs=VMEM,
        out_shape=jax.ShapeDtypeStruct((tokens, model), bf16),
        compiler_params=params(40),
        name="partial",
    )(far_high, far_low, far_back)
    own_far = lax.ppermute(far_sum, "req", swap)
    near_back = within_half(near_out)
    layer_out = pl.pallas_call(
        final_kernel,
        in_specs=[VMEM] * 5,
        out_specs=VMEM,
        out_shape=jax.ShapeDtypeStruct((tokens, model), bf16),
        compiler_params=params(40),
        name="final",
    )(residual, near_high, near_low, near_back, own_far)
    return layer_out, compact.reshape(requests, draft, kv_width)


def solution(mesh):
    rows = P(AXES, None)
    blocks = P(AXES, None, None)
    in_specs = (
        rows, rows, rows, P(AXES), rows, blocks, P(AXES), P(AXES),
        P(), P(), P(), P(), P(), rows, blocks, blocks, blocks,
    )
    return jax.shard_map(
        per_device, mesh=mesh, in_specs=in_specs, out_specs=(rows, blocks), check_vma=False
    )
```

```python
import functools

import jax
import jax.numpy as jnp
import numpy as np
from jax import lax
from jax.experimental import pallas as pl
from jax.experimental.pallas import tpu as pltpu
from jax.sharding import PartitionSpec as P

QUERY_HEADS = 12
KEY_VALUE_HEADS = 2
HEAD_SIZE = 128
GROUP = QUERY_HEADS // KEY_VALUE_HEADS
CAP = 32
EPSILON = 1e-06
ROPE_BASE = 1000000.0
MASKED = -1e30
MIB = 1024 * 1024
NOTE = 16
LIMIT = 60
NOTE_BASE = 32
AXES = ("req", "ep")

VMEM = pl.BlockSpec(memory_space=pltpu.VMEM)
SMEM = pl.BlockSpec(memory_space=pltpu.SMEM)
ANY = pl.BlockSpec(memory_space=pl.ANY)


def dot(a, b, dims=((1,), (0,))):
    return lax.dot_general(a, b, (dims, ((), ())), preferred_element_type=jnp.float32)


def rms_scale(values, scaling):
    widened = values.astype(jnp.float32)
    spread = jnp.mean(widened * widened, axis=-1, keepdims=True)
    return (widened * lax.rsqrt(spread + EPSILON) * scaling.astype(jnp.float32)).astype(
        jnp.bfloat16
    )


def attend(queries, cached, fresh, reach, length):
    scale = HEAD_SIZE ** (-0.5)
    key_width = KEY_VALUE_HEADS * HEAD_SIZE
    context = cached.shape[0]
    rows = queries.shape[0] * GROUP
    in_cache = lax.broadcasted_iota(jnp.int32, (rows, context), 1) < length
    in_tree = jnp.concatenate([reach] * GROUP, axis=0) > 0.5
    outs = []
    for kv in range(KEY_VALUE_HEADS):
        cols = slice(kv * HEAD_SIZE, (kv + 1) * HEAD_SIZE)
        vcols = slice(key_width + kv * HEAD_SIZE, key_width + (kv + 1) * HEAD_SIZE)
        heads = [
            queries[:, (kv * GROUP + g) * HEAD_SIZE : (kv * GROUP + g + 1) * HEAD_SIZE]
            for g in range(GROUP)
        ]
        stacked = jnp.concatenate(heads, axis=0)
        first = dot(stacked, cached[:, cols], ((1,), (1,))) * scale
        first = jnp.where(in_cache, first, MASKED)
        second = dot(stacked, fresh[:, cols], ((1,), (1,))) * scale
        second = jnp.where(in_tree, second, MASKED)
        highest = jnp.maximum(
            jnp.max(first, axis=-1, keepdims=True), jnp.max(second, axis=-1, keepdims=True)
        )
        first = jnp.exp(first - highest)
        second = jnp.exp(second - highest)
        total = jnp.sum(first, axis=-1, keepdims=True) + jnp.sum(second, axis=-1, keepdims=True)
        mixed = dot(first.astype(jnp.bfloat16), cached[:, vcols])
        mixed = mixed + dot(second.astype(jnp.bfloat16), fresh[:, vcols])
        mixed = (mixed / total).astype(jnp.bfloat16)
        step = queries.shape[0]
        outs += [mixed[g * step : (g + 1) * step] for g in range(GROUP)]
    return jnp.concatenate(outs, axis=1)


def load_pages(table, row, pool, target, sems):
    page = pool.shape[1]
    copies = [
        pltpu.make_async_copy(
            pool.at[table[row, i]], target.at[pl.ds(i * page, page)], sems.at[i]
        )
        for i in range(table.shape[1])
    ]
    for copy in copies:
        copy.start()
    return copies


def leaving_kernel(slot, dest, lengths, table, pool, out, sems):
    copies = load_pages(table, slot[0], pool, out, sems)
    length = lengths[slot[0]]
    context = out.shape[0] - NOTE
    note = jnp.zeros((NOTE, 128), jnp.float32)
    for at, value in enumerate((dest[0], length // NOTE_BASE, length % NOTE_BASE)):
        filled = note + value.astype(jnp.float32)
        out[context:, at * 128 : (at + 1) * 128] = filled.astype(jnp.bfloat16)
    out[context:, 3 * 128 :] = jnp.zeros((NOTE, out.shape[1] - 3 * 128), jnp.bfloat16)
    for copy in copies:
        copy.wait()


def slots_of(ids_t, first, shown):
    tokens = ids_t.shape[1]
    names = lax.broadcasted_iota(jnp.int32, (shown, tokens), 0) + first
    assigned = jnp.zeros((shown, tokens), jnp.bool_)
    for k in range(ids_t.shape[0]):
        assigned = assigned | (ids_t[k : k + 1, :] == names)
    before = lax.broadcasted_iota(jnp.int32, (tokens, tokens), 0) < lax.broadcasted_iota(
        jnp.int32, (tokens, tokens), 1
    )
    ranks = dot(one_hot(assigned), one_hot(before))
    return assigned, jnp.where(assigned, ranks, -1.0)


def one_hot(flags):
    return jnp.where(flags, 1.0, 0.0).astype(jnp.bfloat16)


def flipped(values):
    size = values.shape[1]
    same = lax.broadcasted_iota(jnp.int32, (size, size), 0) == lax.broadcasted_iota(
        jnp.int32, (size, size), 1
    )
    if values.shape[0] == 1:
        return jnp.sum(jnp.where(same, values, 0.0), axis=1, keepdims=True)
    return dot(one_hot(same), values.astype(jnp.bfloat16), ((1,), (1,)))


def routes_kernel(split, base, slot, ids_t, table, ordered):
    ids = ids_t[...]
    tokens = ids.shape[1]
    turned = jnp.concatenate([ids[:, tokens // 2 :], ids[:, : tokens // 2]], axis=1)
    ids = jnp.where(slot[0] == 0, turned, ids)
    ordered[...] = ids
    shown = table.shape[0] // (split * CAP)
    _, slots = slots_of(ids, base[0], shown)
    wanted = lax.broadcasted_iota(jnp.int32, (shown, split * CAP, tokens), 1) % CAP
    hot = jnp.where(slots.astype(jnp.int32)[:, None, :] == wanted, 1.0, 0.0)
    table[...] = hot.reshape(table.shape).astype(jnp.bfloat16)


def shares_kernel(split, base, staying, moved, w_router_t, ids_t, high, low):
    tokens = ids_t.shape[1]
    experts = w_router_t.shape[0]
    width = high.shape[1]
    both = jnp.concatenate([staying[...], moved[...]], axis=0)
    logits = dot(both, w_router_t[...], ((1,), (1,)))
    _, slots_t = slots_of(ids_t, 0, experts)
    slots = flipped(slots_t)
    squashed = jnp.where(slots >= 0.0, jax.nn.sigmoid(logits), 0.0)
    share = squashed / jnp.sum(squashed, axis=1, keepdims=True)
    spread = one_hot(
        lax.broadcasted_iota(jnp.int32, (experts, width), 1) // (split * CAP) + base[0]
        == lax.broadcasted_iota(jnp.int32, (experts, width), 0)
    )
    wanted = lax.broadcasted_iota(jnp.int32, (tokens, width), 1) % CAP
    hit = dot(slots.astype(jnp.bfloat16), spread).astype(jnp.int32) == wanted
    share_high = share.astype(jnp.bfloat16)
    share_low = (share - share_high.astype(jnp.float32)).astype(jnp.bfloat16)
    high[...] = jnp.where(hit, dot(share_high, spread), 0.0).astype(jnp.bfloat16)
    low[...] = jnp.where(hit, dot(share_low, spread), 0.0).astype(jnp.bfloat16)


def rotate(projected, depth, length, spectrum, query_width):
    angles = (depth + length) * spectrum
    cosine = jnp.cos(angles)
    sine = jnp.sin(angles)
    first_half = lax.broadcasted_iota(jnp.int32, (1, HEAD_SIZE), 1) < HEAD_SIZE // 2
    sine = jnp.where(first_half, -sine, sine)
    key_width = KEY_VALUE_HEADS * HEAD_SIZE
    turned = []
    for h in range(QUERY_HEADS + KEY_VALUE_HEADS):
        part = projected[:, h * HEAD_SIZE : (h + 1) * HEAD_SIZE]
        swapped = jnp.concatenate([part[:, HEAD_SIZE // 2 :], part[:, : HEAD_SIZE // 2]], axis=1)
        turned.append((part * cosine + swapped * sine).astype(jnp.bfloat16))
    values = projected[:, query_width + key_width :].astype(jnp.bfloat16)
    return (
        jnp.concatenate(turned[:QUERY_HEADS], axis=1),
        jnp.concatenate(turned[QUERY_HEADS:] + [values], axis=1),
    )


def front_kernel(
    slot, lengths, table, hidden, parents, path, spectrum, gain, moe_gain, w_qkv, w_out, pool,
    moved_projected, moved_reach, moved_picked, compact, staying, staying_normed, cache, sems,
):
    stay = 1 - slot[0]
    copies = load_pages(table, stay, pool, cache, sems)
    draft = parents.shape[1]
    query_width = w_out.shape[0]
    rows = [
        hidden[pl.ds(pl.multiple_of(r * draft, draft), draft), :] for r in (stay, slot[0])
    ]
    normed = rms_scale(jnp.concatenate(rows, axis=0), gain[...])
    projected = dot(normed, w_qkv[...])
    names = lax.broadcasted_iota(jnp.int32, (draft, draft), 1)
    itself = names == lax.broadcasted_iota(jnp.int32, (draft, draft), 0)
    trees = []
    for r in (stay, slot[0]):
        above = flipped(parents[pl.ds(r, 1), :].astype(jnp.float32)).astype(jnp.int32)
        reached = jnp.where((above == names) | itself, 1.0, 0.0)
        for _ in range(max(1, (draft - 1).bit_length())):
            half = reached.astype(jnp.bfloat16)
            reached = jnp.minimum(dot(half, half), 1.0)
        trees.append(reached)
    picks = [
        one_hot(flipped(path[pl.ds(r, 1), :].astype(jnp.float32)).astype(jnp.int32) == names)
        for r in (stay, slot[0])
    ]
    moved_projected[...] = projected[draft:]
    moved_reach[...] = trees[1]
    moved_picked[...] = picks[1]
    depth = jnp.sum(trees[0], axis=-1, keepdims=True) - 1.0
    length = lengths[stay]
    queries, fresh = rotate(
        projected[:draft], depth, length.astype(jnp.float32), spectrum[...], query_width
    )
    compact[...] = dot(picks[0], fresh).astype(jnp.bfloat16)
    for copy in copies:
        copy.wait()
    attended = attend(queries, cache, fresh, trees[0], length)
    kept = (rows[0].astype(jnp.float32) + dot(attended, w_out[...])).astype(jnp.bfloat16)
    staying[...] = kept
    staying_normed[...] = rms_scale(kept, moe_gain[...])


def arrival_kernel(
    slot, me, hidden, projected, reach, picked, staying_compact, spectrum, gain, w_out, *rest,
):
    sources = rest[:-7]
    moved, moved_normed, compact, caches, weights, sems, weight_sem = rest[-7:]
    loads = [
        pltpu.make_async_copy(source, caches.at[i], sems.at[i])
        for i, source in enumerate(sources)
    ]
    for load in loads:
        load.start()
    weight_load = pltpu.make_async_copy(w_out, weights, weight_sem)
    weight_load.start()
    draft = projected.shape[0]
    query_width = w_out.shape[0]
    depth = jnp.sum(reach[...], axis=-1, keepdims=True) - 1.0
    for load in loads:
        load.wait()
    context = caches.shape[1] - NOTE

    def noted(i, at):
        values = caches[i, context:, at * 128 : (at + 1) * 128]
        return jnp.max(values.astype(jnp.float32)).astype(jnp.int32)

    chosen = jnp.int32(0)
    length = jnp.int32(0)
    for i in range(len(sources)):
        mine = noted(i, 0) == me[0]
        chosen = jnp.where(mine, i, chosen)
        length = jnp.where(mine, noted(i, 1) * NOTE_BASE + noted(i, 2), length)
    queries, fresh = rotate(
        projected[...], depth, length.astype(jnp.float32), spectrum[...], query_width
    )
    attended = attend(
        queries, caches.at[chosen, pl.ds(0, context)], fresh, reach[...], length
    )
    weight_load.wait()
    own = pl.ds(pl.multiple_of(slot[0] * draft, draft), draft)
    other = pl.ds(pl.multiple_of((1 - slot[0]) * draft, draft), draft)
    kept = hidden[own, :].astype(jnp.float32) + dot(attended, weights[...])
    kept = kept.astype(jnp.bfloat16)
    moved[...] = kept
    moved_normed[...] = rms_scale(kept, gain[...])
    compact[own, :] = dot(picked[...], fresh).astype(jnp.bfloat16)
    compact[other, :] = staying_compact[...]


def pack_kernel(routes, staying, moved, packed):
    both = jnp.concatenate([staying[...], moved[...]], axis=0)
    packed[...] = dot(routes[...], both).astype(jnp.bfloat16)


def expert_kernel(rows, w_gate, w_up, w_down, out, total):
    step = pl.program_id(0)
    gated = dot(rows[...], w_gate[0])
    upped = dot(rows[...], w_up[0])
    activated = (jnp.maximum(gated, 0.0) * upped).astype(jnp.bfloat16)
    piece = dot(activated, w_down[0])

    @pl.when(step == 0)
    def _():
        total[...] = piece

    @pl.when(step > 0)
    def _():
        total[...] += piece

    @pl.when(step == pl.num_programs(0) - 1)
    def _():
        out[...] = total[...].astype(jnp.bfloat16)


def partial_kernel(high, low, rows, out):
    values = rows[...]
    out[...] = (dot(high[...], values) + dot(low[...], values)).astype(jnp.bfloat16)


def final_kernel(slot, staying, moved, high, low, rows, far, out):
    values = rows[...]
    total = dot(high[...], values) + dot(low[...], values) + far[...].astype(jnp.float32)
    draft = staying.shape[0]
    stay = pl.ds(pl.multiple_of((1 - slot[0]) * draft, draft), draft)
    move = pl.ds(pl.multiple_of(slot[0] * draft, draft), draft)
    out[stay, :] = (staying[...].astype(jnp.float32) + total[:draft]).astype(jnp.bfloat16)
    out[move, :] = (moved[...].astype(jnp.float32) + total[draft:]).astype(jnp.bfloat16)


def params(mib):
    return pltpu.CompilerParams(vmem_limit_bytes=mib * MIB)


def cost(flops, moved):
    return pl.CostEstimate(flops=int(flops), bytes_accessed=int(moved), transcendentals=0)


def run_experts(rows, w_gate, w_up, w_down):
    count, model = rows.shape
    hidden_units = w_gate.shape[2]
    chunk = 256 if hidden_units % 256 == 0 else hidden_units
    return pl.pallas_call(
        expert_kernel,
        grid=(hidden_units // chunk,),
        in_specs=[
            pl.BlockSpec((count, model), lambda f: (0, 0)),
            pl.BlockSpec((1, model, chunk), lambda f: (0, 0, f)),
            pl.BlockSpec((1, model, chunk), lambda f: (0, 0, f)),
            pl.BlockSpec((1, chunk, model), lambda f: (0, f, 0)),
        ],
        out_specs=pl.BlockSpec((count, model), lambda f: (0, 0)),
        out_shape=jax.ShapeDtypeStruct((count, model), jnp.bfloat16),
        scratch_shapes=[pltpu.VMEM((count, model), jnp.float32)],
        compiler_params=params(LIMIT),
        cost_estimate=cost(6 * count * model * hidden_units, 6 * model * hidden_units),
        name="experts",
    )(rows, w_gate, w_up, w_down)


def per_device(
    hidden, parents, path, cache_len, page_table, kv_pool, mig_slot, mig_dest,
    attn_gain, w_qkv, w_out, moe_gain, w_router, expert_ids, w_gate, w_up, w_down,
):
    bf16 = jnp.bfloat16
    requests, draft = parents.shape
    tokens, model = hidden.shape
    req_count = lax.axis_size("req")
    ep_count = lax.axis_size("ep")
    device_count = req_count * ep_count
    half_count = device_count // 2
    experts = w_router.shape[1]
    split = device_count // experts
    pages = page_table.shape[1]
    page, kv_width = kv_pool.shape[1:]
    context = pages * page
    query_width = w_out.shape[0]
    slot_rows = half_count * CAP
    req_index = lax.axis_index("req")
    ep_index = lax.axis_index("ep")
    groups = [[h * half_count + i for i in range(half_count)] for h in range(2)]
    inner = req_count // 4
    swap = [(i, (3 - i // inner) * inner + i % inner) for i in range(req_count)]
    base = (req_index // (req_count // 2) * (experts // 2)).astype(jnp.int32).reshape(1)

    def within_half(rows):
        return lax.all_to_all(rows, AXES, 0, 0, tiled=True, axis_index_groups=groups)

    leaving = pl.pallas_call(
        leaving_kernel,
        in_specs=[SMEM] * 4 + [ANY],
        out_specs=VMEM,
        out_shape=jax.ShapeDtypeStruct((context + NOTE, kv_width), bf16),
        scratch_shapes=[pltpu.SemaphoreType.DMA((pages,))],
        compiler_params=params(LIMIT),
        cost_estimate=cost(0, 4 * context * kv_width),
        name="leaving",
    )(mig_slot, mig_dest, cache_len, page_table, kv_pool)
    sibling = lax.ppermute(leaving, "ep", [(i, i ^ 1) for i in range(ep_count)])
    chips = ep_count // 2
    chip = ep_index // 2
    core = ep_index % 2
    arrivals = []
    for k in range(1, chips):
        target = (chip + k) % chips * 2 + core
        payload = jnp.where(mig_dest[0] == target, leaving, sibling)
        moves = [(i, ((i // 2 + k) % chips) * 2 + i % 2) for i in range(ep_count)]
        arrivals.append(lax.ppermute(payload, "ep", moves))
    me = ep_index.astype(jnp.int32).reshape(1)

    def routes_of(slot, names):
        return pl.pallas_call(
            functools.partial(routes_kernel, split),
            in_specs=[SMEM, SMEM, VMEM],
            out_specs=[VMEM] * 2,
            out_shape=[
                jax.ShapeDtypeStruct((slot_rows, tokens), bf16),
                jax.ShapeDtypeStruct(names.shape, jnp.int32),
            ],
            compiler_params=params(LIMIT),
            cost_estimate=cost(1e8, 1e6),
            name="routes",
        )(base, slot, names)

    routes, ids = routes_of(mig_slot, expert_ids.T)
    far_ids = lax.ppermute(ids, "req", swap)
    far_routes, _ = routes_of(jnp.ones((1,), jnp.int32), far_ids)

    frequencies = ROPE_BASE ** (-2.0 * np.arange(HEAD_SIZE // 2) / HEAD_SIZE)
    spectrum = jnp.asarray(np.concatenate([frequencies] * 2)[None].astype(np.float32))
    row_gain = attn_gain.reshape(1, model)
    row_moe_gain = moe_gain.reshape(1, model)
    projected, reach, picked, staying_compact, staying, staying_normed = pl.pallas_call(
        front_kernel,
        in_specs=[SMEM] * 3 + [VMEM] * 8 + [ANY],
        out_specs=[VMEM] * 6,
        out_shape=[
            jax.ShapeDtypeStruct((draft, w_qkv.shape[1]), jnp.float32),
            jax.ShapeDtypeStruct((draft, draft), jnp.float32),
            jax.ShapeDtypeStruct((draft, draft), bf16),
            jax.ShapeDtypeStruct((draft, kv_width), bf16),
            jax.ShapeDtypeStruct((draft, model), bf16),
            jax.ShapeDtypeStruct((draft, model), bf16),
        ],
        scratch_shapes=[
            pltpu.VMEM((context, kv_width), bf16),
            pltpu.SemaphoreType.DMA((pages,)),
        ],
        compiler_params=params(LIMIT),
        cost_estimate=cost(3e9, 3e6),
        name="front",
    )(
        mig_slot, cache_len, page_table, hidden, parents, path, spectrum, row_gain,
        row_moe_gain, w_qkv, w_out, kv_pool,
    )
    far_staying = lax.ppermute(staying_normed, "req", swap)
    projected, routes, far_routes = lax.optimization_barrier((projected, routes, far_routes))
    sources = [leaving, sibling] + arrivals
    moved, moved_normed, compact = pl.pallas_call(
        arrival_kernel,
        in_specs=[SMEM] * 2 + [VMEM] * 7 + [ANY] * (1 + len(sources)),
        out_specs=[VMEM] * 3,
        out_shape=[
            jax.ShapeDtypeStruct((draft, model), bf16),
            jax.ShapeDtypeStruct((draft, model), bf16),
            jax.ShapeDtypeStruct((tokens, kv_width), bf16),
        ],
        scratch_shapes=[
            pltpu.VMEM((len(sources), context + NOTE, kv_width), bf16),
            pltpu.VMEM(w_out.shape, bf16),
            pltpu.SemaphoreType.DMA((len(sources),)),
            pltpu.SemaphoreType.DMA,
        ],
        compiler_params=params(LIMIT),
        cost_estimate=cost(4e9, 8e6),
        name="arrival",
    )(
        mig_slot, me, hidden, projected, reach, picked, staying_compact, spectrum,
        row_moe_gain, w_out, *sources,
    )
    far_moved = lax.ppermute(moved_normed, "req", swap)

    def pack(table, first, second):
        return pl.pallas_call(
            pack_kernel,
            in_specs=[VMEM] * 3,
            out_specs=VMEM,
            out_shape=jax.ShapeDtypeStruct((slot_rows, model), bf16),
            compiler_params=params(LIMIT),
            cost_estimate=cost(3e8, 2e6),
            name="pack",
        )(table, first, second)

    packed = pack(routes, staying_normed, moved_normed)
    far_packed = pack(far_routes, far_staying, far_moved)
    packed, far_packed = lax.optimization_barrier((packed, far_packed))
    far_rows = within_half(far_packed)
    near_rows = within_half(packed)

    def shares_of(names, first, second):
        return pl.pallas_call(
            functools.partial(shares_kernel, split),
            in_specs=[SMEM] + [VMEM] * 4,
            out_specs=[VMEM] * 2,
            out_shape=[jax.ShapeDtypeStruct((tokens, slot_rows), bf16)] * 2,
            compiler_params=params(LIMIT),
            cost_estimate=cost(3e8, 1e6),
            name="shares",
        )(base, first, second, w_router.T, names)

    near_high, near_low = shares_of(ids, staying_normed, moved_normed)
    far_high, far_low = shares_of(far_ids, far_staying, far_moved)
    near_out = run_experts(near_rows, w_gate, w_up, w_down)
    far_out = run_experts(far_rows, w_gate, w_up, w_down)
    far_out, near_high, near_low, far_high, far_low = lax.optimization_barrier(
        (far_out, near_high, near_low, far_high, far_low)
    )
    far_back = within_half(far_out)
    far_sum = pl.pallas_call(
        partial_kernel,
        in_specs=[VMEM] * 3,
        out_specs=VMEM,
        out_shape=jax.ShapeDtypeStruct((tokens, model), bf16),
        compiler_params=params(LIMIT),
        name="partial",
    )(far_high, far_low, far_back)
    own_far = lax.ppermute(far_sum, "req", swap)
    near_back = within_half(near_out)
    layer_out = pl.pallas_call(
        final_kernel,
        in_specs=[SMEM] + [VMEM] * 6,
        out_specs=VMEM,
        out_shape=jax.ShapeDtypeStruct((tokens, model), bf16),
        compiler_params=params(LIMIT),
        name="final",
    )(mig_slot, staying, moved, near_high, near_low, near_back, own_far)
    return layer_out, compact.reshape(requests, draft, kv_width)


def solution(mesh):
    rows = P(AXES, None)
    blocks = P(AXES, None, None)
    in_specs = (
        rows, rows, rows, P(AXES), rows, blocks, P(AXES), P(AXES),
        P(), P(), P(), P(), P(), rows, blocks, blocks, blocks,
    )
    return jax.shard_map(
        per_device, mesh=mesh, in_specs=in_specs, out_specs=(rows, blocks), check_vma=False
    )
```

```python
import functools

import jax
import jax.numpy as jnp
import numpy as np
from jax import lax
from jax.experimental import pallas as pl
from jax.experimental.pallas import tpu as pltpu
from jax.sharding import PartitionSpec as P

QUERY_HEADS = 12
KEY_VALUE_HEADS = 2
HEAD_SIZE = 128
GROUP = QUERY_HEADS // KEY_VALUE_HEADS
CAP = 32
EPSILON = 1e-06
ROPE_BASE = 1000000.0
MASKED = -1e30
LOG2E = 1.4426950408889634
MIB = 1024 * 1024
NOTE = 16
NOTE_BASE = 32
AXES = ("req", "ep")

VMEM = pl.BlockSpec(memory_space=pltpu.VMEM)
SMEM = pl.BlockSpec(memory_space=pltpu.SMEM)
ANY = pl.BlockSpec(memory_space=pl.ANY)
HBM = pl.BlockSpec(memory_space=pltpu.HBM)


def in_hbm(*values):
    return [pltpu.with_memory_space_constraint(value, pltpu.HBM) for value in values]


def in_vmem(*values):
    return [pltpu.with_memory_space_constraint(value, pltpu.VMEM) for value in values]


def load_all(pairs, sems):
    copies = [
        pltpu.make_async_copy(source, target, sems.at[i])
        for i, (source, target) in enumerate(pairs)
    ]
    for copy in copies:
        copy.start()
    return copies


def finish(copies):
    for copy in copies:
        copy.wait()


def dot(a, b, dims=((1,), (0,))):
    return lax.dot_general(a, b, (dims, ((), ())), preferred_element_type=jnp.float32)


def rms_scale(values, scaling):
    widened = values.astype(jnp.float32)
    spread = jnp.mean(widened * widened, axis=-1, keepdims=True)
    return (widened * lax.rsqrt(spread + EPSILON) * scaling.astype(jnp.float32)).astype(
        jnp.bfloat16
    )


def attend(queries, cached, fresh, reach, length):
    scale = HEAD_SIZE ** (-0.5) * LOG2E
    key_width = KEY_VALUE_HEADS * HEAD_SIZE
    context = cached.shape[0]
    in_cache = lax.broadcasted_iota(jnp.int32, (1, context), 1) < length
    cache_bias = jnp.where(in_cache, 0.0, MASKED)
    tree_bias = jnp.concatenate([jnp.where(reach > 0.5, 0.0, MASKED)] * GROUP, axis=0)
    outs = []
    for kv in range(KEY_VALUE_HEADS):
        cols = slice(kv * HEAD_SIZE, (kv + 1) * HEAD_SIZE)
        vcols = slice(key_width + kv * HEAD_SIZE, key_width + (kv + 1) * HEAD_SIZE)
        heads = [
            queries[:, (kv * GROUP + g) * HEAD_SIZE : (kv * GROUP + g + 1) * HEAD_SIZE]
            for g in range(GROUP)
        ]
        stacked = jnp.concatenate(heads, axis=0)
        first = dot(stacked, cached[:, cols], ((1,), (1,))) * scale + cache_bias
        second = dot(stacked, fresh[:, cols], ((1,), (1,))) * scale + tree_bias
        highest = jnp.maximum(
            jnp.max(first, axis=-1, keepdims=True), jnp.max(second, axis=-1, keepdims=True)
        )
        first = jnp.exp2(first - highest)
        second = jnp.exp2(second - highest)
        total = jnp.sum(first, axis=-1, keepdims=True) + jnp.sum(second, axis=-1, keepdims=True)
        mixed = dot(first.astype(jnp.bfloat16), cached[:, vcols])
        mixed = mixed + dot(second.astype(jnp.bfloat16), fresh[:, vcols])
        mixed = (mixed / total).astype(jnp.bfloat16)
        step = queries.shape[0]
        outs += [mixed[g * step : (g + 1) * step] for g in range(GROUP)]
    return jnp.concatenate(outs, axis=1)


def load_pages(table, row, pool, target, sems):
    page = pool.shape[1]
    copies = [
        pltpu.make_async_copy(
            pool.at[table[row, i]], target.at[pl.ds(i * page, page)], sems.at[i]
        )
        for i in range(table.shape[1])
    ]
    for copy in copies:
        copy.start()
    return copies


def leaving_kernel(slot, dest, lengths, table, pool, first, second, pages, note, sems, out_sems):
    loads = load_pages(table, slot[0], pool, pages, sems)
    length = lengths[slot[0]]
    half = second.shape[0]
    page = 2 * half // len(loads)
    blank = jnp.zeros((NOTE, 128), jnp.float32)
    for at, value in enumerate((dest[0], length // NOTE_BASE, length % NOTE_BASE)):
        filled = blank + value.astype(jnp.float32)
        note[:, at * 128 : (at + 1) * 128] = filled.astype(jnp.bfloat16)
    note[:, 3 * 128 :] = jnp.zeros((NOTE, note.shape[1] - 3 * 128), jnp.bfloat16)
    stores = [pltpu.make_async_copy(note, first.at[pl.ds(half, NOTE)], out_sems.at[len(loads)])]
    stores[0].start()
    for i, load in enumerate(loads):
        load.wait()
        target = first if i * page < half else second
        stores.append(
            pltpu.make_async_copy(
                pages.at[pl.ds(i * page, page)],
                target.at[pl.ds(i * page % half, page)],
                out_sems.at[i],
            )
        )
        stores[-1].start()
    finish(stores)


def slots_of(ids_t, first, shown):
    tokens = ids_t.shape[1]
    names = lax.broadcasted_iota(jnp.int32, (shown, tokens), 0) + first
    assigned = jnp.zeros((shown, tokens), jnp.bool_)
    for k in range(ids_t.shape[0]):
        assigned = assigned | (ids_t[k : k + 1, :] == names)
    before = lax.broadcasted_iota(jnp.int32, (tokens, tokens), 0) < lax.broadcasted_iota(
        jnp.int32, (tokens, tokens), 1
    )
    ranks = dot(one_hot(assigned), one_hot(before))
    return assigned, jnp.where(assigned, ranks, -1.0)


def one_hot(flags):
    return jnp.where(flags, 1.0, 0.0).astype(jnp.bfloat16)


def flipped(values):
    size = values.shape[1]
    same = lax.broadcasted_iota(jnp.int32, (size, size), 0) == lax.broadcasted_iota(
        jnp.int32, (size, size), 1
    )
    if values.shape[0] == 1:
        return jnp.sum(jnp.where(same, values, 0.0), axis=1, keepdims=True)
    return dot(one_hot(same), values.astype(jnp.bfloat16), ((1,), (1,)))


def write_routes(split, first, ids, table):
    shown = table.shape[0] // (split * CAP)
    _, slots = slots_of(ids, first, shown)
    wanted = lax.broadcasted_iota(jnp.int32, (shown, split * CAP, ids.shape[1]), 1) % CAP
    hot = jnp.where(slots.astype(jnp.int32)[:, None, :] == wanted, 1.0, 0.0)
    table[...] = hot.reshape(table.shape).astype(jnp.bfloat16)


def travel_order(slot, ids):
    half = ids.shape[1] // 2
    return jnp.where(slot == 0, jnp.concatenate([ids[:, half:], ids[:, :half]], axis=1), ids)


def routes_kernel(split, base, slot, ids_t, table, ordered, names, sems):
    finish(load_all(((ids_t, names),), sems))
    ids = travel_order(slot[0], names[...])
    ordered[...] = ids
    write_routes(split, base[0], ids, table)


def far_routes_kernel(split, base, parcel, table, ordered):
    draft = parcel.shape[0] - NOTE
    ids = parcel[draft:, : ordered.shape[1]].astype(jnp.float32).astype(jnp.int32)
    ids = ids[: ordered.shape[0]]
    ordered[...] = ids
    write_routes(split, base[0], ids, table)


def shares_kernel(split, base, w_router_t, *rest):
    inputs, out, (weights, names, done, sems, out_sem) = rest[:6], rest[6], rest[7:]
    finish(
        load_all(
            ((w_router_t, weights), (inputs[4], names.at[0]), (inputs[5], names.at[1])), sems
        )
    )
    experts = weights.shape[0]
    tokens, width = done.shape[2:]
    spread = one_hot(
        lax.broadcasted_iota(jnp.int32, (experts, width), 1) // (split * CAP) + base[0]
        == lax.broadcasted_iota(jnp.int32, (experts, width), 0)
    )
    wanted = lax.broadcasted_iota(jnp.int32, (tokens, width), 1) % CAP
    for i in range(2):
        staying, moved = inputs[2 * i : 2 * i + 2]
        rows = jnp.concatenate([staying[: moved.shape[0], :], moved[...]], axis=0)
        logits = dot(rows, weights[...], ((1,), (1,)))
        _, slots_t = slots_of(names.at[i], 0, experts)
        slots = flipped(slots_t)
        squashed = jnp.where(slots >= 0.0, jax.nn.sigmoid(logits), 0.0)
        share = squashed / jnp.sum(squashed, axis=1, keepdims=True)
        hit = dot(slots.astype(jnp.bfloat16), spread).astype(jnp.int32) == wanted
        high = share.astype(jnp.bfloat16)
        low = (share - high.astype(jnp.float32)).astype(jnp.bfloat16)
        done[i, 0] = jnp.where(hit, dot(high, spread), 0.0).astype(jnp.bfloat16)
        done[i, 1] = jnp.where(hit, dot(low, spread), 0.0).astype(jnp.bfloat16)
    finish(load_all(((done, out),), out_sem))


def rotate(projected, depth, length, spectrum, query_width):
    angles = (depth + length) * spectrum
    cosine = jnp.cos(angles)
    sine = jnp.sin(angles)
    first_half = lax.broadcasted_iota(jnp.int32, (1, HEAD_SIZE), 1) < HEAD_SIZE // 2
    sine = jnp.where(first_half, -sine, sine)
    key_width = KEY_VALUE_HEADS * HEAD_SIZE
    turned = []
    for h in range(QUERY_HEADS + KEY_VALUE_HEADS):
        part = projected[:, h * HEAD_SIZE : (h + 1) * HEAD_SIZE]
        swapped = jnp.concatenate([part[:, HEAD_SIZE // 2 :], part[:, : HEAD_SIZE // 2]], axis=1)
        turned.append((part * cosine + swapped * sine).astype(jnp.bfloat16))
    values = projected[:, query_width + key_width :].astype(jnp.bfloat16)
    return (
        jnp.concatenate(turned[:QUERY_HEADS], axis=1),
        jnp.concatenate(turned[QUERY_HEADS:] + [values], axis=1),
    )


def front_kernel(
    slot, lengths, table, hidden, parents, path, spectrum, gain, moe_gain, ids_t, w_qkv, w_out,
    pool, moved_projected, moved_reach, moved_picked, compact, staying, parcel,
    weights, tokens, lines, trees, table_row, gains, names_t, w_in, cache, sems, page_sems,
):
    stay = 1 - slot[0]
    loads = load_all(
        (
            (hidden, tokens), (gain, gains.at[0]), (w_qkv, w_in), (moe_gain, gains.at[1]),
            (parents, lines), (path, trees), (spectrum, table_row),
            (ids_t, names_t), (w_out, weights),
        ),
        sems,
    )
    pages = load_pages(table, stay, pool, cache, page_sems)
    draft = parents.shape[1]
    query_width = w_out.shape[0]
    finish(loads[:3])
    rows = [
        tokens[pl.ds(pl.multiple_of(r * draft, draft), draft), :] for r in (stay, slot[0])
    ]
    normed = rms_scale(jnp.concatenate(rows, axis=0), gains[0])
    projected = dot(normed, w_in[...])
    names = lax.broadcasted_iota(jnp.int32, (draft, draft), 1)
    itself = names == lax.broadcasted_iota(jnp.int32, (draft, draft), 0)
    finish(loads[3:8])
    reaches = []
    for r in (stay, slot[0]):
        above = flipped(lines[pl.ds(r, 1), :].astype(jnp.float32)).astype(jnp.int32)
        reached = jnp.where((above == names) | itself, 1.0, 0.0)
        for _ in range(max(1, (draft - 1).bit_length())):
            half = reached.astype(jnp.bfloat16)
            reached = jnp.minimum(dot(half, half), 1.0)
        reaches.append(reached)
    picks = [
        one_hot(flipped(trees[pl.ds(r, 1), :].astype(jnp.float32)).astype(jnp.int32) == names)
        for r in (stay, slot[0])
    ]
    moved_projected[...] = projected[draft:]
    moved_reach[...] = reaches[1]
    moved_picked[...] = picks[1]
    depth = jnp.sum(reaches[0], axis=-1, keepdims=True) - 1.0
    length = lengths[stay]
    queries, fresh = rotate(
        projected[:draft], depth, length.astype(jnp.float32), table_row[...], query_width
    )
    compact[...] = dot(picks[0], fresh).astype(jnp.bfloat16)
    finish(pages)
    attended = attend(queries, cache, fresh, reaches[0], length)
    finish(loads[8:])
    kept = (rows[0].astype(jnp.float32) + dot(attended, weights[...])).astype(jnp.bfloat16)
    staying[...] = kept
    parcel[:draft, :] = rms_scale(kept, gains[1])
    ids = travel_order(slot[0], names_t[...]).astype(jnp.float32)
    blank = jnp.zeros((NOTE - ids.shape[0], ids.shape[1]), jnp.float32)
    parcel[draft:, :] = jnp.zeros((NOTE, parcel.shape[1]), jnp.bfloat16)
    parcel[draft:, : ids.shape[1]] = jnp.concatenate([ids, blank], axis=0).astype(jnp.bfloat16)


def arrival_kernel(
    slot, me, projected, reach, picked, staying_compact, hidden, spectrum, gain, w_out, *rest,
):
    sources = rest[:-11]
    sources = list(zip(sources[0::2], sources[1::2]))
    moved, moved_normed, compact, cache, notes, weights, rows, table_row, gains, sems, note_sems = (
        rest[-11:]
    )
    half = cache.shape[0] // 2
    draft = projected.shape[0]
    query_width = weights.shape[0]
    note_loads = load_all(
        [(first.at[pl.ds(half, NOTE)], notes.at[i]) for i, (first, _) in enumerate(sources)],
        note_sems,
    )
    own = pl.ds(pl.multiple_of(slot[0] * draft, draft), draft)
    other = pl.ds(pl.multiple_of((1 - slot[0]) * draft, draft), draft)
    loads = load_all(
        ((hidden.at[own], rows), (spectrum, table_row), (gain, gains), (w_out, weights)),
        sems.at[pl.ds(2, 4)],
    )
    depth = jnp.sum(reach[...], axis=-1, keepdims=True) - 1.0
    finish(note_loads)

    def noted(i, at):
        values = notes[i, :, at * 128 : (at + 1) * 128]
        return jnp.max(values.astype(jnp.float32)).astype(jnp.int32)

    def cache_loads(pair):
        return [
            pltpu.make_async_copy(pair[0].at[pl.ds(0, half)], cache.at[pl.ds(0, half)], sems.at[0]),
            pltpu.make_async_copy(pair[1], cache.at[pl.ds(half, half)], sems.at[1]),
        ]

    length = jnp.int32(0)
    for i, pair in enumerate(sources):
        mine = noted(i, 0) == me[0]
        length = jnp.where(mine, noted(i, 1) * NOTE_BASE + noted(i, 2), length)

        @pl.when(mine)
        def _(pair=pair):
            for copy in cache_loads(pair):
                copy.start()

    finish(loads[:3])
    queries, fresh = rotate(
        projected[...], depth, length.astype(jnp.float32), table_row[...], query_width
    )
    finish(cache_loads(sources[0]))
    attended = attend(queries, cache, fresh, reach[...], length)
    finish(loads[3:])
    kept = rows[...].astype(jnp.float32) + dot(attended, weights[...])
    kept = kept.astype(jnp.bfloat16)
    moved[...] = kept
    moved_normed[...] = rms_scale(kept, gains[...])
    compact[own, :] = dot(picked[...], fresh).astype(jnp.bfloat16)
    compact[other, :] = staying_compact[...]


def pack_kernel(routes, staying, moved, out, rows, sems):
    both = jnp.concatenate([staying[: moved.shape[0], :], moved[...]], axis=0)
    group = rows.shape[0] // 2
    stores = []
    for i in range(2):
        span = pl.ds(i * group, group)
        rows[span] = dot(routes[i * group : (i + 1) * group, :], both).astype(jnp.bfloat16)
        stores += load_all(((rows.at[span], out.at[span]),), sems.at[pl.ds(i, 1)])
    finish(stores)


def expert_kernel(arrived, w_gate, w_up, w_down, out, gates, ups, downs, act, done, sems):
    count, model = out.shape
    hidden_units = gates.shape[1]
    chunk = 256 if hidden_units % 256 == 0 else hidden_units
    wide = 512 if model % 512 == 0 else model
    block = 256 if count % 256 == 0 else count
    chunks = [pl.ds(i * chunk, chunk) for i in range(hidden_units // chunk)]
    wides = [pl.ds(i * wide, wide) for i in range(model // wide)]
    loads = []
    for i, cols in enumerate(chunks):
        pairs = ((w_gate.at[0, :, cols], gates.at[:, cols]), (w_up.at[0, :, cols], ups.at[:, cols]))
        loads.append(load_all(pairs, sems.at[i]))
    down_loads = [
        load_all(((w_down.at[0, :, cols], downs.at[:, cols]),), sems.at[len(chunks) + i])
        for i, cols in enumerate(wides)
    ]
    blocks = [slice(i * block, (i + 1) * block) for i in range(count // block)]
    for load, cols in zip(loads, chunks):
        finish(load)
        for span in blocks:
            rows = arrived[span, :]
            gated = dot(rows, gates[:, cols])
            upped = dot(rows, ups[:, cols])
            act[span, cols] = (jnp.maximum(gated, 0.0) * upped).astype(jnp.bfloat16)
    stores = []
    for i, cols in enumerate(wides):
        finish(down_loads[i])
        for span in blocks:
            done[span, cols] = dot(act[span, :], downs[:, cols]).astype(jnp.bfloat16)
        stores += load_all(((done.at[:, cols], out.at[:, cols]),), sems.at[len(chunks) + i])
    finish(stores)


def partial_kernel(shares, rows, out, pair, sems):
    finish(load_all(((shares.at[1], pair),), sems))
    values = rows[...]
    out[...] = (dot(pair[0], values) + dot(pair[1], values)).astype(jnp.bfloat16)


def final_kernel(slot, shares, staying, moved, far, rows, out, pair, sems):
    finish(load_all(((shares.at[0], pair),), sems))
    draft = staying.shape[0]
    values = rows[...]
    total = dot(pair[0], values) + dot(pair[1], values) + far[...].astype(jnp.float32)
    for at, kept, part in (
        (1 - slot[0], staying, total[:draft]), (slot[0], moved, total[draft:])
    ):
        at = pl.ds(pl.multiple_of(at * draft, draft), draft)
        out[at, :] = (kept[...].astype(jnp.float32) + part).astype(jnp.bfloat16)


def params(mib, rows=512):
    return pltpu.CompilerParams(vmem_limit_bytes=min(60, mib * max(rows, 512) // 512) * MIB)


def cost(flops, moved):
    return pl.CostEstimate(flops=int(flops), bytes_accessed=int(moved), transcendentals=0)


def run_experts(arrived, w_gate, w_up, w_down):
    count, model = arrived.shape
    hidden_units = w_gate.shape[2]
    return pl.pallas_call(
        expert_kernel,
        in_specs=[VMEM] + [HBM] * 3,
        out_specs=HBM,
        out_shape=pltpu.HBM((count, model), jnp.bfloat16),
        scratch_shapes=[
            pltpu.VMEM((model, hidden_units), jnp.bfloat16),
            pltpu.VMEM((model, hidden_units), jnp.bfloat16),
            pltpu.VMEM((hidden_units, model), jnp.bfloat16),
            pltpu.VMEM((count, hidden_units), jnp.bfloat16),
            pltpu.VMEM((count, model), jnp.bfloat16),
            pltpu.SemaphoreType.DMA((8, 2)),
        ],
        compiler_params=params(16 + 3 * count * model // MIB),
        cost_estimate=cost(6 * count * model * hidden_units, 6 * model * hidden_units),
        name="experts",
    )(*in_vmem(arrived), *in_hbm(w_gate, w_up, w_down))


def per_device(
    hidden, parents, path, cache_len, page_table, kv_pool, mig_slot, mig_dest,
    attn_gain, w_qkv, w_out, moe_gain, w_router, expert_ids, w_gate, w_up, w_down,
):
    bf16 = jnp.bfloat16
    requests, draft = parents.shape
    tokens, model = hidden.shape
    req_count = lax.axis_size("req")
    ep_count = lax.axis_size("ep")
    device_count = req_count * ep_count
    half_count = device_count // 2
    experts = w_router.shape[1]
    split = device_count // experts
    pages = page_table.shape[1]
    page, kv_width = kv_pool.shape[1:]
    context = pages * page
    query_width = w_out.shape[0]
    slot_rows = half_count * CAP
    req_index = lax.axis_index("req")
    ep_index = lax.axis_index("ep")
    groups = [[h * half_count + i for i in range(half_count)] for h in range(2)]
    inner = req_count // 4
    swap = [(i, (3 - i // inner) * inner + i % inner) for i in range(req_count)]
    base = (req_index // (req_count // 2) * (experts // 2)).astype(jnp.int32).reshape(1)

    def within_half(rows):
        return lax.all_to_all(rows, AXES, 0, 0, tiled=True, axis_index_groups=groups)

    f32 = jnp.float32
    half_cache = context // 2
    leaving = pl.pallas_call(
        leaving_kernel,
        in_specs=[SMEM] * 4 + [HBM],
        out_specs=[HBM] * 2,
        out_shape=[
            pltpu.HBM((half_cache + NOTE, kv_width), bf16),
            pltpu.HBM((half_cache, kv_width), bf16),
        ],
        scratch_shapes=[
            pltpu.VMEM((context, kv_width), bf16),
            pltpu.VMEM((NOTE, kv_width), bf16),
            pltpu.SemaphoreType.DMA((pages,)),
            pltpu.SemaphoreType.DMA((pages + 1,)),
        ],
        compiler_params=params(60),
        cost_estimate=cost(0, 4 * context * kv_width),
        name="leaving",
    )(mig_slot, mig_dest, cache_len, page_table, *in_hbm(kv_pool))
    chips = ep_count // 2
    chip = ep_index // 2
    core = ep_index % 2
    pairs = [(i, i ^ 1) for i in range(ep_count)]
    sibling = [lax.ppermute(part, "ep", pairs) for part in leaving]
    sources = [*leaving, *sibling]
    payloads = []
    for k in range(1, chips):
        target = (chip + k) % chips * 2 + core
        moves = [(i, ((i // 2 + k) % chips) * 2 + i % 2) for i in range(ep_count)]
        for mine, other in zip(leaving, sibling):
            payload = jnp.where(mig_dest[0] == target, mine, other)
            payloads.append(payload)
            sources.append(lax.ppermute(payload, "ep", moves))
    me = ep_index.astype(jnp.int32).reshape(1)

    route_shapes = [
        pltpu.VMEM((slot_rows, tokens), bf16),
        pltpu.HBM((expert_ids.shape[1], tokens), jnp.int32),
    ]
    frequencies = ROPE_BASE ** (-2.0 * np.arange(HEAD_SIZE // 2) / HEAD_SIZE)
    spectrum = jnp.asarray(np.concatenate([frequencies] * 2)[None].astype(np.float32))
    row_gain = attn_gain.reshape(1, model)
    row_moe_gain = moe_gain.reshape(1, model)
    hidden, *_ = lax.optimization_barrier((hidden, *payloads))
    projected, reach, picked, staying_compact, staying, parcel = pl.pallas_call(
        front_kernel,
        in_specs=[SMEM] * 3 + [HBM] * 10,
        out_specs=[VMEM] * 6,
        out_shape=[
            pltpu.VMEM((draft, w_qkv.shape[1]), f32),
            pltpu.VMEM((draft, draft), f32),
            pltpu.VMEM((draft, draft), bf16),
            pltpu.VMEM((draft, kv_width), bf16),
            pltpu.VMEM((draft, model), bf16),
            pltpu.VMEM((draft + NOTE, model), bf16),
        ],
        scratch_shapes=[
            pltpu.VMEM(w_out.shape, bf16),
            pltpu.VMEM((tokens, model), bf16),
            pltpu.VMEM(parents.shape, jnp.int32),
            pltpu.VMEM(path.shape, jnp.int32),
            pltpu.VMEM(spectrum.shape, f32),
            pltpu.VMEM((2, 1, model), bf16),
            pltpu.VMEM((expert_ids.shape[1], tokens), jnp.int32),
            pltpu.VMEM(w_qkv.shape, bf16),
            pltpu.VMEM((context, kv_width), bf16),
            pltpu.SemaphoreType.DMA((9,)),
            pltpu.SemaphoreType.DMA((pages,)),
        ],
        compiler_params=params(36),
        cost_estimate=cost(3e9, 3e6),
        name="front",
    )(
        mig_slot, cache_len, page_table,
        *in_hbm(
            hidden, parents, path, spectrum, row_gain, row_moe_gain, expert_ids.T, w_qkv, w_out,
            kv_pool,
        ),
    )
    far_parcel = lax.ppermute(parcel, "req", swap)
    names_t, _ = lax.optimization_barrier((expert_ids.T, projected))
    routes, ids = pl.pallas_call(
        functools.partial(routes_kernel, split),
        in_specs=[SMEM, SMEM, HBM],
        out_specs=[VMEM] * 2,
        out_shape=route_shapes,
        scratch_shapes=[
            pltpu.VMEM((expert_ids.shape[1], tokens), jnp.int32),
            pltpu.SemaphoreType.DMA((1,)),
        ],
        compiler_params=params(6, slot_rows),
        cost_estimate=cost(1e8, 1e6),
        name="routes",
    )(base, mig_slot, *in_hbm(names_t))
    far_parcel, routes, *sources = lax.optimization_barrier((far_parcel, routes, *sources))
    moved, moved_normed, compact = pl.pallas_call(
        arrival_kernel,
        in_specs=[SMEM] * 2 + [VMEM] * 4 + [HBM] * (4 + len(sources)),
        out_specs=[VMEM] * 3,
        out_shape=[
            pltpu.VMEM((draft, model), bf16),
            pltpu.VMEM((draft, model), bf16),
            jax.ShapeDtypeStruct((tokens, kv_width), bf16),
        ],
        scratch_shapes=[
            pltpu.VMEM((context, kv_width), bf16),
            pltpu.VMEM((len(sources) // 2, NOTE, kv_width), bf16),
            pltpu.VMEM(w_out.shape, bf16),
            pltpu.VMEM((draft, model), bf16),
            pltpu.VMEM(spectrum.shape, f32),
            pltpu.VMEM((1, model), bf16),
            pltpu.SemaphoreType.DMA((6,)),
            pltpu.SemaphoreType.DMA((len(sources) // 2,)),
        ],
        compiler_params=params(24),
        cost_estimate=cost(4e9, 8e6),
        name="arrival",
    )(
        mig_slot, me, *in_vmem(projected, reach, picked, staying_compact),
        *in_hbm(hidden, spectrum, row_moe_gain, w_out, *sources),
    )
    far_moved = lax.ppermute(moved_normed, "req", swap)
    far_routes, far_ids = pl.pallas_call(
        functools.partial(far_routes_kernel, split),
        in_specs=[SMEM, VMEM],
        out_specs=[VMEM] * 2,
        out_shape=route_shapes,
        compiler_params=params(6, slot_rows),
        cost_estimate=cost(1e8, 1e6),
        name="far_routes",
    )(base, *in_vmem(far_parcel))

    def pack(table, first, second):
        return pl.pallas_call(
            pack_kernel,
            in_specs=[VMEM] * 3,
            out_specs=HBM,
            out_shape=pltpu.HBM((slot_rows, model), bf16),
            scratch_shapes=[
                pltpu.VMEM((slot_rows, model), bf16),
                pltpu.SemaphoreType.DMA((2,)),
            ],
            compiler_params=params(10, slot_rows),
            cost_estimate=cost(3e8, 2e6),
            name="pack",
        )(*in_vmem(table, first, second))

    near_packed = pack(routes, parcel, moved_normed)
    far_packed = pack(far_routes, far_parcel, far_moved)
    far_rows = within_half(far_packed)
    near_packed, far_rows = lax.optimization_barrier((near_packed, far_rows))
    near_rows = within_half(near_packed)
    shares = pl.pallas_call(
        functools.partial(shares_kernel, split),
        in_specs=[SMEM, HBM] + [VMEM] * 4 + [HBM] * 2,
        out_specs=HBM,
        out_shape=pltpu.HBM((2, 2, tokens, slot_rows), bf16),
        scratch_shapes=[
            pltpu.VMEM((experts, model), bf16),
            pltpu.VMEM((2,) + ids.shape, jnp.int32),
            pltpu.VMEM((2, 2, tokens, slot_rows), bf16),
            pltpu.SemaphoreType.DMA((3,)),
            pltpu.SemaphoreType.DMA((1,)),
        ],
        compiler_params=params(10, slot_rows),
        cost_estimate=cost(3e8, 1e6),
        name="shares",
    )(
        base, *in_hbm(w_router.T), *in_vmem(parcel, moved_normed, far_parcel, far_moved),
        *in_hbm(ids, far_ids),
    )
    far_out = run_experts(far_rows, w_gate, w_up, w_down)
    far_out, near_rows, shares = lax.optimization_barrier((far_out, near_rows, shares))
    far_back = within_half(far_out)
    near_out = run_experts(near_rows, w_gate, w_up, w_down)
    near_out, far_back = lax.optimization_barrier((near_out, far_back))
    far_sum = pl.pallas_call(
        partial_kernel,
        in_specs=[HBM, VMEM],
        out_specs=VMEM,
        out_shape=pltpu.VMEM((tokens, model), bf16),
        scratch_shapes=[
            pltpu.VMEM((2, tokens, slot_rows), bf16),
            pltpu.SemaphoreType.DMA((1,)),
        ],
        compiler_params=params(8, slot_rows),
        cost_estimate=cost(4e8, 2e6),
        name="partial",
    )(*in_hbm(shares), *in_vmem(far_back))
    own_far = lax.ppermute(far_sum, "req", swap)
    near_back = within_half(near_out)
    layer_out = pl.pallas_call(
        final_kernel,
        in_specs=[SMEM, HBM] + [VMEM] * 4,
        out_specs=VMEM,
        out_shape=jax.ShapeDtypeStruct((tokens, model), bf16),
        scratch_shapes=[
            pltpu.VMEM((2, tokens, slot_rows), bf16),
            pltpu.SemaphoreType.DMA((1,)),
        ],
        compiler_params=params(10, slot_rows),
        cost_estimate=cost(4e8, 2e6),
        name="final",
    )(mig_slot, *in_hbm(shares), *in_vmem(staying, moved, own_far, near_back))
    return layer_out, compact.reshape(requests, draft, kv_width)


def solution(mesh):
    rows = P(AXES, None)
    blocks = P(AXES, None, None)
    in_specs = (
        rows, rows, rows, P(AXES), rows, blocks, P(AXES), P(AXES),
        P(), P(), P(), P(), P(), rows, blocks, blocks, blocks,
    )
    return jax.shard_map(
        per_device, mesh=mesh, in_specs=in_specs, out_specs=(rows, blocks), check_vma=False
    )
```

```python
import functools

import jax
import jax.numpy as jnp
import numpy as np
from jax import lax
from jax.experimental import pallas as pl
from jax.experimental.pallas import tpu as pltpu
from jax.sharding import PartitionSpec as P

QUERY_HEADS = 12
KEY_VALUE_HEADS = 2
HEAD_SIZE = 128
GROUP = QUERY_HEADS // KEY_VALUE_HEADS
CAP = 32
EPSILON = 1e-06
ROPE_BASE = 1000000.0
MASKED = -1e30
LOG2E = 1.4426950408889634
MIB = 1024 * 1024
NOTE = 16
NOTE_BASE = 32
AXES = ("req", "ep")

VMEM = pl.BlockSpec(memory_space=pltpu.VMEM)
SMEM = pl.BlockSpec(memory_space=pltpu.SMEM)
ANY = pl.BlockSpec(memory_space=pl.ANY)
HBM = pl.BlockSpec(memory_space=pltpu.HBM)


def in_hbm(*values):
    return [pltpu.with_memory_space_constraint(value, pltpu.HBM) for value in values]


def in_vmem(*values):
    return [pltpu.with_memory_space_constraint(value, pltpu.VMEM) for value in values]


def load_all(pairs, sems):
    copies = [
        pltpu.make_async_copy(source, target, sems.at[i])
        for i, (source, target) in enumerate(pairs)
    ]
    for copy in copies:
        copy.start()
    return copies


def finish(copies):
    for copy in copies:
        copy.wait()


def dot(a, b, dims=((1,), (0,))):
    return lax.dot_general(a, b, (dims, ((), ())), preferred_element_type=jnp.float32)


def rms_scale(values, scaling):
    widened = values.astype(jnp.float32)
    spread = jnp.mean(widened * widened, axis=-1, keepdims=True)
    return (widened * lax.rsqrt(spread + EPSILON) * scaling.astype(jnp.float32)).astype(
        jnp.bfloat16
    )


def attend(queries, cached, fresh, reach, length):
    scale = HEAD_SIZE ** (-0.5) * LOG2E
    key_width = KEY_VALUE_HEADS * HEAD_SIZE
    context = cached.shape[0]
    in_cache = lax.broadcasted_iota(jnp.int32, (1, context), 1) < length
    cache_bias = jnp.where(in_cache, 0.0, MASKED)
    tree_bias = jnp.concatenate([jnp.where(reach > 0.5, 0.0, MASKED)] * GROUP, axis=0)
    outs = []
    for kv in range(KEY_VALUE_HEADS):
        cols = slice(kv * HEAD_SIZE, (kv + 1) * HEAD_SIZE)
        vcols = slice(key_width + kv * HEAD_SIZE, key_width + (kv + 1) * HEAD_SIZE)
        heads = [
            queries[:, (kv * GROUP + g) * HEAD_SIZE : (kv * GROUP + g + 1) * HEAD_SIZE]
            for g in range(GROUP)
        ]
        stacked = jnp.concatenate(heads, axis=0)
        first = dot(stacked, cached[:, cols], ((1,), (1,))) * scale + cache_bias
        second = dot(stacked, fresh[:, cols], ((1,), (1,))) * scale + tree_bias
        highest = jnp.maximum(
            jnp.max(first, axis=-1, keepdims=True), jnp.max(second, axis=-1, keepdims=True)
        )
        first = jnp.exp2(first - highest)
        second = jnp.exp2(second - highest)
        total = jnp.sum(first, axis=-1, keepdims=True) + jnp.sum(second, axis=-1, keepdims=True)
        mixed = dot(first.astype(jnp.bfloat16), cached[:, vcols])
        mixed = mixed + dot(second.astype(jnp.bfloat16), fresh[:, vcols])
        mixed = (mixed / total).astype(jnp.bfloat16)
        step = queries.shape[0]
        outs += [mixed[g * step : (g + 1) * step] for g in range(GROUP)]
    return jnp.concatenate(outs, axis=1)


def load_pages(table, row, pool, target, sems):
    page = pool.shape[1]
    copies = [
        pltpu.make_async_copy(
            pool.at[table[row, i]], target.at[pl.ds(i * page, page)], sems.at[i]
        )
        for i in range(table.shape[1])
    ]
    for copy in copies:
        copy.start()
    return copies


def leaving_kernel(slot, dest, lengths, table, pool, first, second, sems):
    half, page = second.shape[0], pool.shape[1]
    loads = []
    for i in range(table.shape[1]):
        target = first if i * page < half else second
        span = pl.ds(i * page % half, page)
        loads.append(
            pltpu.make_async_copy(pool.at[table[slot[0], i]], target.at[span], sems.at[i])
        )
        loads[-1].start()
    length = lengths[slot[0]]
    row = lax.broadcasted_iota(jnp.int32, (NOTE, first.shape[1]), 0)
    lane = lax.broadcasted_iota(jnp.int32, (NOTE, first.shape[1]), 1)
    note = jnp.zeros((NOTE, first.shape[1]), jnp.int32)
    parts = (dest[0] * 4 * half, length // NOTE_BASE * NOTE_BASE, length % NOTE_BASE)
    for at, value in enumerate(parts):
        note = jnp.where((row == 0) & (lane == at), value, note)
    first[half:, :] = note.astype(jnp.float32).astype(jnp.bfloat16)
    finish(loads)


def slots_of(ids_t, first, shown):
    tokens = ids_t.shape[1]
    names = lax.broadcasted_iota(jnp.int32, (shown, tokens), 0) + first
    assigned = jnp.zeros((shown, tokens), jnp.bool_)
    for k in range(ids_t.shape[0]):
        assigned = assigned | (ids_t[k : k + 1, :] == names)
    before = lax.broadcasted_iota(jnp.int32, (tokens, tokens), 0) < lax.broadcasted_iota(
        jnp.int32, (tokens, tokens), 1
    )
    ranks = dot(one_hot(assigned), one_hot(before))
    return assigned, jnp.where(assigned, ranks, -1.0)


def one_hot(flags):
    return jnp.where(flags, 1.0, 0.0).astype(jnp.bfloat16)


def flipped(values):
    size = values.shape[1]
    same = lax.broadcasted_iota(jnp.int32, (size, size), 0) == lax.broadcasted_iota(
        jnp.int32, (size, size), 1
    )
    if values.shape[0] == 1:
        return jnp.sum(jnp.where(same, values, 0.0), axis=1, keepdims=True)
    return dot(one_hot(same), values.astype(jnp.bfloat16), ((1,), (1,)))


def write_routes(split, first, ids, table):
    shown = table.shape[0] // (split * CAP)
    _, slots = slots_of(ids, first, shown)
    wanted = lax.broadcasted_iota(jnp.int32, (shown, split * CAP, ids.shape[1]), 1) % CAP
    hot = jnp.where(slots.astype(jnp.int32)[:, None, :] == wanted, 1.0, 0.0)
    table[...] = hot.reshape(table.shape).astype(jnp.bfloat16)


def travel_order(slot, ids):
    half = ids.shape[1] // 2
    return jnp.where(slot == 0, jnp.concatenate([ids[:, half:], ids[:, :half]], axis=1), ids)


def routes_kernel(split, base, slot, ids_t, table, ordered, names, sems):
    finish(load_all(((ids_t, names),), sems))
    ids = travel_order(slot[0], names[...])
    ordered[...] = ids
    write_routes(split, base[0], ids, table)


def far_routes_kernel(split, base, parcel, table, ordered):
    draft = parcel.shape[0] - NOTE
    ids = parcel[draft:, : ordered.shape[1]].astype(jnp.float32).astype(jnp.int32)
    ids = ids[: ordered.shape[0]]
    ordered[...] = ids
    write_routes(split, base[0], ids, table)


def shares_kernel(split, base, w_router_t, *rest):
    inputs, out, (weights, names, done, sems, out_sem) = rest[:6], rest[6], rest[7:]
    finish(
        load_all(
            ((w_router_t, weights), (inputs[4], names.at[0]), (inputs[5], names.at[1])), sems
        )
    )
    experts = weights.shape[0]
    tokens, width = done.shape[2:]
    spread = one_hot(
        lax.broadcasted_iota(jnp.int32, (experts, width), 1) // (split * CAP) + base[0]
        == lax.broadcasted_iota(jnp.int32, (experts, width), 0)
    )
    wanted = lax.broadcasted_iota(jnp.int32, (tokens, width), 1) % CAP
    for i in range(2):
        staying, moved = inputs[2 * i : 2 * i + 2]
        rows = jnp.concatenate([staying[: moved.shape[0], :], moved[...]], axis=0)
        logits = dot(rows, weights[...], ((1,), (1,)))
        _, slots_t = slots_of(names.at[i], 0, experts)
        slots = flipped(slots_t)
        squashed = jnp.where(slots >= 0.0, jax.nn.sigmoid(logits), 0.0)
        share = squashed / jnp.sum(squashed, axis=1, keepdims=True)
        hit = dot(slots.astype(jnp.bfloat16), spread).astype(jnp.int32) == wanted
        high = share.astype(jnp.bfloat16)
        low = (share - high.astype(jnp.float32)).astype(jnp.bfloat16)
        done[i, 0] = jnp.where(hit, dot(high, spread), 0.0).astype(jnp.bfloat16)
        done[i, 1] = jnp.where(hit, dot(low, spread), 0.0).astype(jnp.bfloat16)
    finish(load_all(((done, out),), out_sem))


def rotate(projected, depth, length, spectrum, query_width):
    angles = (depth + length) * spectrum
    cosine = jnp.cos(angles)
    sine = jnp.sin(angles)
    first_half = lax.broadcasted_iota(jnp.int32, (1, HEAD_SIZE), 1) < HEAD_SIZE // 2
    sine = jnp.where(first_half, -sine, sine)
    key_width = KEY_VALUE_HEADS * HEAD_SIZE
    turned = []
    for h in range(QUERY_HEADS + KEY_VALUE_HEADS):
        part = projected[:, h * HEAD_SIZE : (h + 1) * HEAD_SIZE]
        swapped = jnp.concatenate([part[:, HEAD_SIZE // 2 :], part[:, : HEAD_SIZE // 2]], axis=1)
        turned.append((part * cosine + swapped * sine).astype(jnp.bfloat16))
    values = projected[:, query_width + key_width :].astype(jnp.bfloat16)
    return (
        jnp.concatenate(turned[:QUERY_HEADS], axis=1),
        jnp.concatenate(turned[QUERY_HEADS:] + [values], axis=1),
    )


def front_kernel(
    slot, lengths, table, hidden, parents, path, spectrum, gain, moe_gain, ids_t, w_qkv, w_out,
    pool, moved_projected, moved_reach, moved_picked, compact, staying, parcel,
    weights, tokens, lines, trees, table_row, gains, names_t, w_in, cache, kept_lines, sems,
    page_sems, out_sem,
):
    stay = 1 - slot[0]
    loads = load_all(
        (
            (hidden, tokens), (gain, gains.at[0]), (w_qkv, w_in), (moe_gain, gains.at[1]),
            (parents, lines), (path, trees), (spectrum, table_row),
            (ids_t, names_t), (w_out, weights),
        ),
        sems,
    )
    pages = load_pages(table, stay, pool, cache, page_sems)
    draft = parents.shape[1]
    query_width = w_out.shape[0]
    finish(loads[:3])
    rows = [
        tokens[pl.ds(pl.multiple_of(r * draft, draft), draft), :] for r in (stay, slot[0])
    ]
    normed = rms_scale(jnp.concatenate(rows, axis=0), gains[0])
    projected = dot(normed, w_in[...])
    names = lax.broadcasted_iota(jnp.int32, (draft, draft), 1)
    itself = names == lax.broadcasted_iota(jnp.int32, (draft, draft), 0)
    finish(loads[3:8])
    reaches = []
    for r in (stay, slot[0]):
        above = flipped(lines[pl.ds(r, 1), :].astype(jnp.float32)).astype(jnp.int32)
        reached = jnp.where((above == names) | itself, 1.0, 0.0)
        for _ in range(max(1, (draft - 1).bit_length())):
            half = reached.astype(jnp.bfloat16)
            reached = jnp.minimum(dot(half, half), 1.0)
        reaches.append(reached)
    picks = [
        one_hot(flipped(trees[pl.ds(r, 1), :].astype(jnp.float32)).astype(jnp.int32) == names)
        for r in (stay, slot[0])
    ]
    kept_lines[...] = projected[draft:]
    store = load_all(((kept_lines, moved_projected),), out_sem)
    moved_reach[...] = reaches[1]
    moved_picked[...] = picks[1]
    depth = jnp.sum(reaches[0], axis=-1, keepdims=True) - 1.0
    length = lengths[stay]
    queries, fresh = rotate(
        projected[:draft], depth, length.astype(jnp.float32), table_row[...], query_width
    )
    compact[...] = dot(picks[0], fresh).astype(jnp.bfloat16)
    finish(pages)
    attended = attend(queries, cache, fresh, reaches[0], length)
    finish(loads[8:])
    kept = (rows[0].astype(jnp.float32) + dot(attended, weights[...])).astype(jnp.bfloat16)
    staying[...] = kept
    parcel[:draft, :] = rms_scale(kept, gains[1])
    finish(store)
    ids = travel_order(slot[0], names_t[...]).astype(jnp.float32)
    blank = jnp.zeros((NOTE - ids.shape[0], ids.shape[1]), jnp.float32)
    parcel[draft:, :] = jnp.zeros((NOTE, parcel.shape[1]), jnp.bfloat16)
    parcel[draft:, : ids.shape[1]] = jnp.concatenate([ids, blank], axis=0).astype(jnp.bfloat16)


def early_kernel(
    slot, me, reach, picked, staying_compact, projected, spectrum, *rest,
):
    sources = rest[:-14]
    (
        pick, stacked, mixed, tops, totals, compact,
        cache, notes, lines, table_row, fresh, note_sems, sems, cache_sem,
    ) = rest[-14:]
    half = cache.shape[0]
    draft = projected.shape[0]
    note_loads = load_all(
        [
            (first.at[pl.ds(half, NOTE), pl.ds(0, 128)], notes.at[i])
            for i, first in enumerate(sources)
        ],
        note_sems,
    )
    loads = load_all(((projected, lines), (spectrum, table_row)), sems)
    depth = jnp.sum(reach[...], axis=-1, keepdims=True) - 1.0
    finish(note_loads)
    chosen = jnp.int32(0)
    length = jnp.int32(0)
    for i, source in enumerate(sources):
        code = jnp.sum(notes[i].astype(jnp.float32)).astype(jnp.int32)
        mine = code // (4 * half) == me[0]
        chosen = jnp.where(mine, i, chosen)
        length = jnp.where(mine, code % (4 * half), length)

        @pl.when(mine)
        def _(source=source):
            pltpu.make_async_copy(source.at[pl.ds(0, half)], cache, cache_sem).start()

    pick[0] = chosen
    pick[1] = length
    finish(loads)
    query_width = QUERY_HEADS * HEAD_SIZE
    queries, rows = rotate(
        lines[...], depth, length.astype(jnp.float32), table_row[...], query_width
    )
    fresh[...] = rows
    own = pl.ds(pl.multiple_of(slot[0] * draft, draft), draft)
    other = pl.ds(pl.multiple_of((1 - slot[0]) * draft, draft), draft)
    compact[own, :] = dot(picked[...], rows).astype(jnp.bfloat16)
    compact[other, :] = staying_compact[...]
    pltpu.make_async_copy(sources[0].at[pl.ds(0, half)], cache, cache_sem).wait()
    scale = HEAD_SIZE ** (-0.5) * LOG2E
    key_width = KEY_VALUE_HEADS * HEAD_SIZE
    in_cache = lax.broadcasted_iota(jnp.int32, (1, half), 1) < length
    cache_bias = jnp.where(in_cache, 0.0, MASKED)
    tree_bias = jnp.concatenate([jnp.where(reach[...] > 0.5, 0.0, MASKED)] * GROUP, axis=0)
    for kv in range(KEY_VALUE_HEADS):
        cols = slice(kv * HEAD_SIZE, (kv + 1) * HEAD_SIZE)
        vcols = slice(key_width + kv * HEAD_SIZE, key_width + (kv + 1) * HEAD_SIZE)
        heads = [
            queries[:, (kv * GROUP + g) * HEAD_SIZE : (kv * GROUP + g + 1) * HEAD_SIZE]
            for g in range(GROUP)
        ]
        asked = jnp.concatenate(heads, axis=0)
        stacked[kv] = asked
        first = dot(asked, cache[:, cols], ((1,), (1,))) * scale + cache_bias
        second = dot(asked, fresh[:, cols], ((1,), (1,))) * scale + tree_bias
        top = jnp.maximum(
            jnp.max(first, axis=-1, keepdims=True), jnp.max(second, axis=-1, keepdims=True)
        )
        first = jnp.exp2(first - top)
        second = jnp.exp2(second - top)
        tops[kv] = top
        totals[kv] = jnp.sum(first, axis=-1, keepdims=True) + jnp.sum(
            second, axis=-1, keepdims=True
        )
        mixed[kv] = dot(first.astype(jnp.bfloat16), cache[:, vcols]) + dot(
            second.astype(jnp.bfloat16), fresh[:, vcols]
        )


def arrival_kernel(
    slot, pick, stacked, mixed, tops, totals, hidden, gain, w_out, *rest,
):
    sources = rest[:-8]
    moved, moved_normed, cache, weights, rows, gains, sems, cache_sem = rest[-8:]
    half = cache.shape[0]
    draft = rows.shape[0]
    for i, source in enumerate(sources):

        @pl.when(pick[0] == i)
        def _(source=source):
            pltpu.make_async_copy(source, cache, cache_sem).start()

    own = pl.ds(pl.multiple_of(slot[0] * draft, draft), draft)
    loads = load_all(((hidden.at[own], rows), (gain, gains), (w_out, weights)), sems)
    scale = HEAD_SIZE ** (-0.5) * LOG2E
    key_width = KEY_VALUE_HEADS * HEAD_SIZE
    in_cache = lax.broadcasted_iota(jnp.int32, (1, half), 1) + half < pick[1]
    bias = jnp.where(in_cache, 0.0, MASKED)
    pltpu.make_async_copy(sources[0], cache, cache_sem).wait()
    outs = []
    for kv in range(KEY_VALUE_HEADS):
        cols = slice(kv * HEAD_SIZE, (kv + 1) * HEAD_SIZE)
        vcols = slice(key_width + kv * HEAD_SIZE, key_width + (kv + 1) * HEAD_SIZE)
        scores = dot(stacked[kv], cache[:, cols], ((1,), (1,))) * scale + bias
        top = jnp.maximum(jnp.max(scores, axis=-1, keepdims=True), tops[kv])
        weight = jnp.exp2(scores - top)
        factor = jnp.exp2(tops[kv] - top)
        total = totals[kv] * factor + jnp.sum(weight, axis=-1, keepdims=True)
        blend = mixed[kv] * factor + dot(weight.astype(jnp.bfloat16), cache[:, vcols])
        blend = (blend / total).astype(jnp.bfloat16)
        outs += [blend[g * draft : (g + 1) * draft] for g in range(GROUP)]
    attended = jnp.concatenate(outs, axis=1)
    finish(loads)
    kept = rows[...].astype(jnp.float32) + dot(attended, weights[...])
    kept = kept.astype(jnp.bfloat16)
    moved[...] = kept
    moved_normed[...] = rms_scale(kept, gains[...])


def pack_kernel(routes, staying, moved, out, rows, sems):
    both = jnp.concatenate([staying[: moved.shape[0], :], moved[...]], axis=0)
    group = rows.shape[0] // 2
    stores = []
    for i in range(2):
        span = pl.ds(i * group, group)
        rows[span] = dot(routes[i * group : (i + 1) * group, :], both).astype(jnp.bfloat16)
        stores += load_all(((rows.at[span], out.at[span]),), sems.at[pl.ds(i, 1)])
    finish(stores)


def expert_kernel(arrived, w_gate, w_up, w_down, out, gates, ups, downs, act, done, sems):
    count, model = out.shape
    hidden_units = gates.shape[1]
    chunk = 256 if hidden_units % 256 == 0 else hidden_units
    wide = 512 if model % 512 == 0 else model
    block = 256 if count % 256 == 0 else count
    chunks = [pl.ds(i * chunk, chunk) for i in range(hidden_units // chunk)]
    wides = [pl.ds(i * wide, wide) for i in range(model // wide)]
    loads = []
    for i, cols in enumerate(chunks):
        pairs = ((w_gate.at[0, :, cols], gates.at[:, cols]), (w_up.at[0, :, cols], ups.at[:, cols]))
        loads.append(load_all(pairs, sems.at[i]))
    down_loads = [
        load_all(((w_down.at[0, :, cols], downs.at[:, cols]),), sems.at[len(chunks) + i])
        for i, cols in enumerate(wides)
    ]
    blocks = [slice(i * block, (i + 1) * block) for i in range(count // block)]
    for load, cols in zip(loads, chunks):
        finish(load)
        for span in blocks:
            rows = arrived[span, :]
            gated = dot(rows, gates[:, cols])
            upped = dot(rows, ups[:, cols])
            act[span, cols] = (jnp.maximum(gated, 0.0) * upped).astype(jnp.bfloat16)
    stores = []
    for i, cols in enumerate(wides):
        finish(down_loads[i])
        for span in blocks:
            done[span, cols] = dot(act[span, :], downs[:, cols]).astype(jnp.bfloat16)
        stores += load_all(((done.at[:, cols], out.at[:, cols]),), sems.at[len(chunks) + i])
    finish(stores)


def partial_kernel(shares, rows, out, pair, sems):
    finish(load_all(((shares.at[1], pair),), sems))
    values = rows[...]
    out[...] = (dot(pair[0], values) + dot(pair[1], values)).astype(jnp.bfloat16)


def final_kernel(slot, shares, staying, moved, far, rows, out, pair, sems):
    finish(load_all(((shares.at[0], pair),), sems))
    draft = staying.shape[0]
    values = rows[...]
    total = dot(pair[0], values) + dot(pair[1], values) + far[...].astype(jnp.float32)
    for at, kept, part in (
        (1 - slot[0], staying, total[:draft]), (slot[0], moved, total[draft:])
    ):
        at = pl.ds(pl.multiple_of(at * draft, draft), draft)
        out[at, :] = (kept[...].astype(jnp.float32) + part).astype(jnp.bfloat16)


def params(mib, rows=512):
    return pltpu.CompilerParams(vmem_limit_bytes=min(60, mib * max(rows, 512) // 512) * MIB)


def cost(flops, moved):
    return pl.CostEstimate(flops=int(flops), bytes_accessed=int(moved), transcendentals=0)


def run_experts(arrived, w_gate, w_up, w_down):
    count, model = arrived.shape
    hidden_units = w_gate.shape[2]
    return pl.pallas_call(
        expert_kernel,
        in_specs=[VMEM] + [HBM] * 3,
        out_specs=HBM,
        out_shape=pltpu.HBM((count, model), jnp.bfloat16),
        scratch_shapes=[
            pltpu.VMEM((model, hidden_units), jnp.bfloat16),
            pltpu.VMEM((model, hidden_units), jnp.bfloat16),
            pltpu.VMEM((hidden_units, model), jnp.bfloat16),
            pltpu.VMEM((count, hidden_units), jnp.bfloat16),
            pltpu.VMEM((count, model), jnp.bfloat16),
            pltpu.SemaphoreType.DMA((8, 2)),
        ],
        compiler_params=params(16 + 3 * count * model // MIB),
        cost_estimate=cost(6 * count * model * hidden_units, 6 * model * hidden_units),
        name="experts",
    )(*in_vmem(arrived), *in_hbm(w_gate, w_up, w_down))


def per_device(
    hidden, parents, path, cache_len, page_table, kv_pool, mig_slot, mig_dest,
    attn_gain, w_qkv, w_out, moe_gain, w_router, expert_ids, w_gate, w_up, w_down,
):
    bf16 = jnp.bfloat16
    requests, draft = parents.shape
    tokens, model = hidden.shape
    req_count = lax.axis_size("req")
    ep_count = lax.axis_size("ep")
    device_count = req_count * ep_count
    half_count = device_count // 2
    experts = w_router.shape[1]
    split = device_count // experts
    pages = page_table.shape[1]
    page, kv_width = kv_pool.shape[1:]
    context = pages * page
    query_width = w_out.shape[0]
    slot_rows = half_count * CAP
    req_index = lax.axis_index("req")
    ep_index = lax.axis_index("ep")
    groups = [[h * half_count + i for i in range(half_count)] for h in range(2)]
    inner = req_count // 4
    swap = [(i, (3 - i // inner) * inner + i % inner) for i in range(req_count)]
    base = (req_index // (req_count // 2) * (experts // 2)).astype(jnp.int32).reshape(1)

    def within_half(rows):
        return lax.all_to_all(rows, AXES, 0, 0, tiled=True, axis_index_groups=groups)

    f32 = jnp.float32
    half_cache = context // 2
    leaving = pl.pallas_call(
        leaving_kernel,
        in_specs=[SMEM] * 4 + [HBM],
        out_specs=[VMEM] * 2,
        out_shape=[
            pltpu.VMEM((half_cache + NOTE, kv_width), bf16),
            pltpu.VMEM((half_cache, kv_width), bf16),
        ],
        scratch_shapes=[pltpu.SemaphoreType.DMA((pages,))],
        compiler_params=params(58),
        cost_estimate=cost(0, 4 * context * kv_width),
        name="leaving",
    )(mig_slot, mig_dest, cache_len, page_table, *in_hbm(kv_pool))
    chips = ep_count // 2
    chip = ep_index // 2
    core = ep_index % 2
    pairs = [(i, i ^ 1) for i in range(ep_count)]
    sibling = [lax.ppermute(part, "ep", pairs) for part in leaving]
    sources = [*leaving, *sibling]
    payloads = []
    for k in range(1, chips):
        target = (chip + k) % chips * 2 + core
        moves = [(i, ((i // 2 + k) % chips) * 2 + i % 2) for i in range(ep_count)]
        for mine, other in zip(leaving, sibling):
            payload = jnp.where(mig_dest[0] == target, mine, other)
            payloads.append(payload)
            sources.append(lax.ppermute(payload, "ep", moves))
    me = ep_index.astype(jnp.int32).reshape(1)

    route_shapes = [
        pltpu.VMEM((slot_rows, tokens), bf16),
        pltpu.HBM((expert_ids.shape[1], tokens), jnp.int32),
    ]
    frequencies = ROPE_BASE ** (-2.0 * np.arange(HEAD_SIZE // 2) / HEAD_SIZE)
    spectrum = jnp.asarray(np.concatenate([frequencies] * 2)[None].astype(np.float32))
    row_gain = attn_gain.reshape(1, model)
    row_moe_gain = moe_gain.reshape(1, model)
    hidden, *_ = lax.optimization_barrier((hidden, *payloads))
    projected, reach, picked, staying_compact, staying, parcel = pl.pallas_call(
        front_kernel,
        in_specs=[SMEM] * 3 + [HBM] * 10,
        out_specs=[HBM] + [VMEM] * 5,
        out_shape=[
            pltpu.HBM((draft, w_qkv.shape[1]), f32),
            pltpu.VMEM((draft, draft), f32),
            pltpu.VMEM((draft, draft), bf16),
            pltpu.VMEM((draft, kv_width), bf16),
            pltpu.VMEM((draft, model), bf16),
            pltpu.VMEM((draft + NOTE, model), bf16),
        ],
        scratch_shapes=[
            pltpu.VMEM(w_out.shape, bf16),
            pltpu.VMEM((tokens, model), bf16),
            pltpu.VMEM(parents.shape, jnp.int32),
            pltpu.VMEM(path.shape, jnp.int32),
            pltpu.VMEM(spectrum.shape, f32),
            pltpu.VMEM((2, 1, model), bf16),
            pltpu.VMEM((expert_ids.shape[1], tokens), jnp.int32),
            pltpu.VMEM(w_qkv.shape, bf16),
            pltpu.VMEM((context, kv_width), bf16),
            pltpu.VMEM((draft, w_qkv.shape[1]), f32),
            pltpu.SemaphoreType.DMA((9,)),
            pltpu.SemaphoreType.DMA((pages,)),
            pltpu.SemaphoreType.DMA((1,)),
        ],
        compiler_params=params(36),
        cost_estimate=cost(3e9, 3e6),
        name="front",
    )(
        mig_slot, cache_len, page_table,
        *in_hbm(
            hidden, parents, path, spectrum, row_gain, row_moe_gain, expert_ids.T, w_qkv, w_out,
            kv_pool,
        ),
    )
    far_parcel = lax.ppermute(parcel, "req", swap)
    names_t, _ = lax.optimization_barrier((expert_ids.T, projected))
    routes, ids = pl.pallas_call(
        functools.partial(routes_kernel, split),
        in_specs=[SMEM, SMEM, HBM],
        out_specs=[VMEM] * 2,
        out_shape=route_shapes,
        scratch_shapes=[
            pltpu.VMEM((expert_ids.shape[1], tokens), jnp.int32),
            pltpu.SemaphoreType.DMA((1,)),
        ],
        compiler_params=params(6, slot_rows),
        cost_estimate=cost(1e8, 1e6),
        name="routes",
    )(base, mig_slot, *in_hbm(names_t))
    early, late = sources[0::2], sources[1::2]
    rows = GROUP * draft
    pick, stacked, mixed, tops, totals, compact = pl.pallas_call(
        early_kernel,
        in_specs=[SMEM] * 2 + [VMEM] * 3 + [HBM] * 2 + [ANY] * len(early),
        out_specs=[SMEM] + [VMEM] * 5,
        out_shape=[
            jax.ShapeDtypeStruct((2,), jnp.int32),
            pltpu.VMEM((KEY_VALUE_HEADS, rows, HEAD_SIZE), bf16),
            pltpu.VMEM((KEY_VALUE_HEADS, rows, HEAD_SIZE), f32),
            pltpu.VMEM((KEY_VALUE_HEADS, rows, 1), f32),
            pltpu.VMEM((KEY_VALUE_HEADS, rows, 1), f32),
            jax.ShapeDtypeStruct((tokens, kv_width), bf16),
        ],
        scratch_shapes=[
            pltpu.VMEM((half_cache, kv_width), bf16),
            pltpu.VMEM((len(early), NOTE, 128), bf16),
            pltpu.VMEM(projected.shape, f32),
            pltpu.VMEM(spectrum.shape, f32),
            pltpu.VMEM((draft, kv_width), bf16),
            pltpu.SemaphoreType.DMA((len(early),)),
            pltpu.SemaphoreType.DMA((2,)),
            pltpu.SemaphoreType.DMA,
        ],
        compiler_params=params(16),
        cost_estimate=cost(1e9, 2e6),
        name="early",
    )(
        mig_slot, me, *in_vmem(reach, picked, staying_compact), *in_hbm(projected, spectrum),
        *early,
    )
    far_parcel, routes, pick, *late = lax.optimization_barrier((far_parcel, routes, pick, *late))
    moved, moved_normed = pl.pallas_call(
        arrival_kernel,
        in_specs=[SMEM] * 2 + [VMEM] * 4 + [HBM] * 3 + [ANY] * len(late),
        out_specs=[VMEM] * 2,
        out_shape=[pltpu.VMEM((draft, model), bf16)] * 2,
        scratch_shapes=[
            pltpu.VMEM((half_cache, kv_width), bf16),
            pltpu.VMEM(w_out.shape, bf16),
            pltpu.VMEM((draft, model), bf16),
            pltpu.VMEM((1, model), bf16),
            pltpu.SemaphoreType.DMA((3,)),
            pltpu.SemaphoreType.DMA,
        ],
        compiler_params=params(16),
        cost_estimate=cost(2e9, 8e6),
        name="arrival",
    )(
        mig_slot, pick, *in_vmem(stacked, mixed, tops, totals),
        *in_hbm(hidden, row_moe_gain, w_out), *late,
    )
    far_moved = lax.ppermute(moved_normed, "req", swap)
    far_routes, far_ids = pl.pallas_call(
        functools.partial(far_routes_kernel, split),
        in_specs=[SMEM, VMEM],
        out_specs=[VMEM] * 2,
        out_shape=route_shapes,
        compiler_params=params(6, slot_rows),
        cost_estimate=cost(1e8, 1e6),
        name="far_routes",
    )(base, *in_vmem(far_parcel))

    def pack(table, first, second):
        return pl.pallas_call(
            pack_kernel,
            in_specs=[VMEM] * 3,
            out_specs=HBM,
            out_shape=pltpu.HBM((slot_rows, model), bf16),
            scratch_shapes=[
                pltpu.VMEM((slot_rows, model), bf16),
                pltpu.SemaphoreType.DMA((2,)),
            ],
            compiler_params=params(10, slot_rows),
            cost_estimate=cost(3e8, 2e6),
            name="pack",
        )(*in_vmem(table, first, second))

    near_packed = pack(routes, parcel, moved_normed)
    far_packed = pack(far_routes, far_parcel, far_moved)
    far_rows = within_half(far_packed)
    near_packed, far_rows = lax.optimization_barrier((near_packed, far_rows))
    near_rows = within_half(near_packed)
    shares = pl.pallas_call(
        functools.partial(shares_kernel, split),
        in_specs=[SMEM, HBM] + [VMEM] * 4 + [HBM] * 2,
        out_specs=HBM,
        out_shape=pltpu.HBM((2, 2, tokens, slot_rows), bf16),
        scratch_shapes=[
            pltpu.VMEM((experts, model), bf16),
            pltpu.VMEM((2,) + ids.shape, jnp.int32),
            pltpu.VMEM((2, 2, tokens, slot_rows), bf16),
            pltpu.SemaphoreType.DMA((3,)),
            pltpu.SemaphoreType.DMA((1,)),
        ],
        compiler_params=params(10, slot_rows),
        cost_estimate=cost(3e8, 1e6),
        name="shares",
    )(
        base, *in_hbm(w_router.T), *in_vmem(parcel, moved_normed, far_parcel, far_moved),
        *in_hbm(ids, far_ids),
    )
    far_out = run_experts(far_rows, w_gate, w_up, w_down)
    far_out, near_rows, shares = lax.optimization_barrier((far_out, near_rows, shares))
    far_back = within_half(far_out)
    near_out = run_experts(near_rows, w_gate, w_up, w_down)
    near_out, far_back = lax.optimization_barrier((near_out, far_back))
    far_sum = pl.pallas_call(
        partial_kernel,
        in_specs=[HBM, VMEM],
        out_specs=VMEM,
        out_shape=pltpu.VMEM((tokens, model), bf16),
        scratch_shapes=[
            pltpu.VMEM((2, tokens, slot_rows), bf16),
            pltpu.SemaphoreType.DMA((1,)),
        ],
        compiler_params=params(8, slot_rows),
        cost_estimate=cost(4e8, 2e6),
        name="partial",
    )(*in_hbm(shares), *in_vmem(far_back))
    own_far = lax.ppermute(far_sum, "req", swap)
    near_back = within_half(near_out)
    layer_out = pl.pallas_call(
        final_kernel,
        in_specs=[SMEM, HBM] + [VMEM] * 4,
        out_specs=VMEM,
        out_shape=jax.ShapeDtypeStruct((tokens, model), bf16),
        scratch_shapes=[
            pltpu.VMEM((2, tokens, slot_rows), bf16),
            pltpu.SemaphoreType.DMA((1,)),
        ],
        compiler_params=params(10, slot_rows),
        cost_estimate=cost(4e8, 2e6),
        name="final",
    )(mig_slot, *in_hbm(shares), *in_vmem(staying, moved, own_far, near_back))
    return layer_out, compact.reshape(requests, draft, kv_width)


def solution(mesh):
    rows = P(AXES, None)
    blocks = P(AXES, None, None)
    in_specs = (
        rows, rows, rows, P(AXES), rows, blocks, P(AXES), P(AXES),
        P(), P(), P(), P(), P(), rows, blocks, blocks, blocks,
    )
    return jax.shard_map(
        per_device, mesh=mesh, in_specs=in_specs, out_specs=(rows, blocks), check_vma=False
    )
```

```python
import functools

import jax
import jax.numpy as jnp
import numpy as np
from jax import lax
from jax.experimental import pallas as pl
from jax.experimental.pallas import tpu as pltpu
from jax.sharding import PartitionSpec as P

QUERY_HEADS = 12
KEY_VALUE_HEADS = 2
HEAD_SIZE = 128
GROUP = QUERY_HEADS // KEY_VALUE_HEADS
CAP = 32
EPSILON = 1e-06
ROPE_BASE = 1000000.0
MASKED = -1e30
LOG2E = 1.4426950408889634
MIB = 1024 * 1024
NOTE = 16
NOTE_BASE = 32
AXES = ("req", "ep")

VMEM = pl.BlockSpec(memory_space=pltpu.VMEM)
SMEM = pl.BlockSpec(memory_space=pltpu.SMEM)
ANY = pl.BlockSpec(memory_space=pl.ANY)
HBM = pl.BlockSpec(memory_space=pltpu.HBM)


def in_hbm(*values):
    return [pltpu.with_memory_space_constraint(value, pltpu.HBM) for value in values]


def in_vmem(*values):
    return [pltpu.with_memory_space_constraint(value, pltpu.VMEM) for value in values]


def load_all(pairs, sems):
    copies = [
        pltpu.make_async_copy(source, target, sems.at[i])
        for i, (source, target) in enumerate(pairs)
    ]
    for copy in copies:
        copy.start()
    return copies


def finish(copies):
    for copy in copies:
        copy.wait()


def dot(a, b, dims=((1,), (0,))):
    return lax.dot_general(a, b, (dims, ((), ())), preferred_element_type=jnp.float32)


def rms_scale(values, scaling):
    widened = values.astype(jnp.float32)
    spread = jnp.mean(widened * widened, axis=-1, keepdims=True)
    return (widened * lax.rsqrt(spread + EPSILON) * scaling.astype(jnp.float32)).astype(
        jnp.bfloat16
    )


def attend(queries, cached, fresh, reach, length):
    scale = HEAD_SIZE ** (-0.5) * LOG2E
    key_width = KEY_VALUE_HEADS * HEAD_SIZE
    context = cached.shape[0]
    in_cache = lax.broadcasted_iota(jnp.int32, (1, context), 1) < length
    cache_bias = jnp.where(in_cache, 0.0, MASKED)
    tree_bias = jnp.concatenate([jnp.where(reach > 0.5, 0.0, MASKED)] * GROUP, axis=0)
    outs = []
    for kv in range(KEY_VALUE_HEADS):
        cols = slice(kv * HEAD_SIZE, (kv + 1) * HEAD_SIZE)
        vcols = slice(key_width + kv * HEAD_SIZE, key_width + (kv + 1) * HEAD_SIZE)
        heads = [
            queries[:, (kv * GROUP + g) * HEAD_SIZE : (kv * GROUP + g + 1) * HEAD_SIZE]
            for g in range(GROUP)
        ]
        stacked = jnp.concatenate(heads, axis=0)
        first = dot(stacked, cached[:, cols], ((1,), (1,))) * scale + cache_bias
        second = dot(stacked, fresh[:, cols], ((1,), (1,))) * scale + tree_bias
        highest = jnp.maximum(
            jnp.max(first, axis=-1, keepdims=True), jnp.max(second, axis=-1, keepdims=True)
        )
        first = jnp.exp2(first - highest)
        second = jnp.exp2(second - highest)
        total = jnp.sum(first, axis=-1, keepdims=True) + jnp.sum(second, axis=-1, keepdims=True)
        mixed = dot(first.astype(jnp.bfloat16), cached[:, vcols])
        mixed = mixed + dot(second.astype(jnp.bfloat16), fresh[:, vcols])
        mixed = (mixed / total).astype(jnp.bfloat16)
        step = queries.shape[0]
        outs += [mixed[g * step : (g + 1) * step] for g in range(GROUP)]
    return jnp.concatenate(outs, axis=1)


def load_pages(table, row, pool, target, sems):
    page = pool.shape[1]
    copies = [
        pltpu.make_async_copy(
            pool.at[table[row, i]], target.at[pl.ds(i * page, page)], sems.at[i]
        )
        for i in range(table.shape[1])
    ]
    for copy in copies:
        copy.start()
    return copies


def leaving_kernel(slot, dest, lengths, table, pool, first, second, sems):
    half, page = second.shape[0], pool.shape[1]
    loads = []
    for i in range(table.shape[1]):
        target = first if i * page < half else second
        span = pl.ds(i * page % half, page)
        loads.append(
            pltpu.make_async_copy(pool.at[table[slot[0], i]], target.at[span], sems.at[i])
        )
        loads[-1].start()
    length = lengths[slot[0]]
    row = lax.broadcasted_iota(jnp.int32, (NOTE, first.shape[1]), 0)
    lane = lax.broadcasted_iota(jnp.int32, (NOTE, first.shape[1]), 1)
    note = jnp.zeros((NOTE, first.shape[1]), jnp.int32)
    parts = (dest[0] * 4 * half, length // NOTE_BASE * NOTE_BASE, length % NOTE_BASE)
    for at, value in enumerate(parts):
        note = jnp.where((row == 0) & (lane == at), value, note)
    first[half:, :] = note.astype(jnp.float32).astype(jnp.bfloat16)
    finish(loads)


def slots_of(ids_t, first, shown):
    tokens = ids_t.shape[1]
    names = lax.broadcasted_iota(jnp.int32, (shown, tokens), 0) + first
    assigned = jnp.zeros((shown, tokens), jnp.bool_)
    for k in range(ids_t.shape[0]):
        assigned = assigned | (ids_t[k : k + 1, :] == names)
    before = lax.broadcasted_iota(jnp.int32, (tokens, tokens), 0) < lax.broadcasted_iota(
        jnp.int32, (tokens, tokens), 1
    )
    ranks = dot(one_hot(assigned), one_hot(before))
    return assigned, jnp.where(assigned, ranks, -1.0)


def one_hot(flags):
    return jnp.where(flags, 1.0, 0.0).astype(jnp.bfloat16)


def flipped(values):
    size = values.shape[1]
    same = lax.broadcasted_iota(jnp.int32, (size, size), 0) == lax.broadcasted_iota(
        jnp.int32, (size, size), 1
    )
    if values.shape[0] == 1:
        return jnp.sum(jnp.where(same, values, 0.0), axis=1, keepdims=True)
    return dot(one_hot(same), values.astype(jnp.bfloat16), ((1,), (1,)))


def write_routes(split, first, ids, table):
    shown = table.shape[0] // (split * CAP)
    _, slots = slots_of(ids, first, shown)
    wanted = lax.broadcasted_iota(jnp.int32, (shown, split * CAP, ids.shape[1]), 1) % CAP
    hot = jnp.where(slots.astype(jnp.int32)[:, None, :] == wanted, 1.0, 0.0)
    table[...] = hot.reshape(table.shape).astype(jnp.bfloat16)


def travel_order(slot, ids):
    half = ids.shape[1] // 2
    return jnp.where(slot == 0, jnp.concatenate([ids[:, half:], ids[:, :half]], axis=1), ids)


def routes_kernel(split, base, slot, ids_t, table, ordered, names, sems):
    finish(load_all(((ids_t, names),), sems))
    ids = travel_order(slot[0], names[...])
    ordered[...] = ids
    write_routes(split, base[0], ids, table)


def far_routes_kernel(split, base, parcel, table, ordered):
    draft = parcel.shape[0] - NOTE
    ids = parcel[draft:, : ordered.shape[1]].astype(jnp.float32).astype(jnp.int32)
    ids = ids[: ordered.shape[0]]
    ordered[...] = ids
    write_routes(split, base[0], ids, table)


def shares_kernel(split, base, w_router_t, *rest):
    inputs, out, (weights, names, done, sems, out_sem) = rest[:6], rest[6], rest[7:]
    finish(
        load_all(
            ((w_router_t, weights), (inputs[4], names.at[0]), (inputs[5], names.at[1])), sems
        )
    )
    experts = weights.shape[0]
    tokens, width = done.shape[2:]
    spread = one_hot(
        lax.broadcasted_iota(jnp.int32, (experts, width), 1) // (split * CAP) + base[0]
        == lax.broadcasted_iota(jnp.int32, (experts, width), 0)
    )
    wanted = lax.broadcasted_iota(jnp.int32, (tokens, width), 1) % CAP
    for i in range(2):
        staying, moved = inputs[2 * i : 2 * i + 2]
        rows = jnp.concatenate([staying[: moved.shape[0], :], moved[...]], axis=0)
        logits = dot(rows, weights[...], ((1,), (1,)))
        _, slots_t = slots_of(names.at[i], 0, experts)
        slots = flipped(slots_t)
        squashed = jnp.where(slots >= 0.0, jax.nn.sigmoid(logits), 0.0)
        share = squashed / jnp.sum(squashed, axis=1, keepdims=True)
        hit = dot(slots.astype(jnp.bfloat16), spread).astype(jnp.int32) == wanted
        high = share.astype(jnp.bfloat16)
        low = (share - high.astype(jnp.float32)).astype(jnp.bfloat16)
        done[i, 0] = jnp.where(hit, dot(high, spread), 0.0).astype(jnp.bfloat16)
        done[i, 1] = jnp.where(hit, dot(low, spread), 0.0).astype(jnp.bfloat16)
    finish(load_all(((done, out),), out_sem))


def rotate(projected, depth, length, spectrum, query_width):
    angles = (depth + length) * spectrum
    cosine = jnp.cos(angles)
    sine = jnp.sin(angles)
    first_half = lax.broadcasted_iota(jnp.int32, (1, HEAD_SIZE), 1) < HEAD_SIZE // 2
    sine = jnp.where(first_half, -sine, sine)
    key_width = KEY_VALUE_HEADS * HEAD_SIZE
    turned = []
    for h in range(QUERY_HEADS + KEY_VALUE_HEADS):
        part = projected[:, h * HEAD_SIZE : (h + 1) * HEAD_SIZE]
        swapped = jnp.concatenate([part[:, HEAD_SIZE // 2 :], part[:, : HEAD_SIZE // 2]], axis=1)
        turned.append((part * cosine + swapped * sine).astype(jnp.bfloat16))
    values = projected[:, query_width + key_width :].astype(jnp.bfloat16)
    return (
        jnp.concatenate(turned[:QUERY_HEADS], axis=1),
        jnp.concatenate(turned[QUERY_HEADS:] + [values], axis=1),
    )


def front_kernel(
    slot, lengths, table, hidden, parents, path, spectrum, gain, moe_gain, ids_t, w_qkv, w_out,
    pool, moved_projected, moved_reach, moved_picked, compact, staying, parcel,
    weights, tokens, lines, trees, table_row, gains, names_t, w_in, cache, kept_lines, sems,
    page_sems, out_sem,
):
    stay = 1 - slot[0]
    loads = load_all(
        (
            (hidden, tokens), (gain, gains.at[0]), (w_qkv, w_in), (moe_gain, gains.at[1]),
            (parents, lines), (path, trees), (spectrum, table_row),
            (ids_t, names_t), (w_out, weights),
        ),
        sems,
    )
    pages = load_pages(table, stay, pool, cache, page_sems)
    draft = parents.shape[1]
    query_width = w_out.shape[0]
    finish(loads[:3])
    rows = [
        tokens[pl.ds(pl.multiple_of(r * draft, draft), draft), :] for r in (stay, slot[0])
    ]
    normed = rms_scale(jnp.concatenate(rows, axis=0), gains[0])
    projected = dot(normed, w_in[...])
    names = lax.broadcasted_iota(jnp.int32, (draft, draft), 1)
    itself = names == lax.broadcasted_iota(jnp.int32, (draft, draft), 0)
    finish(loads[3:8])
    reaches = []
    for r in (stay, slot[0]):
        above = flipped(lines[pl.ds(r, 1), :].astype(jnp.float32)).astype(jnp.int32)
        reached = jnp.where((above == names) | itself, 1.0, 0.0)
        for _ in range(max(1, (draft - 1).bit_length())):
            half = reached.astype(jnp.bfloat16)
            reached = jnp.minimum(dot(half, half), 1.0)
        reaches.append(reached)
    picks = [
        one_hot(flipped(trees[pl.ds(r, 1), :].astype(jnp.float32)).astype(jnp.int32) == names)
        for r in (stay, slot[0])
    ]
    kept_lines[...] = projected[draft:]
    store = load_all(((kept_lines, moved_projected),), out_sem)
    moved_reach[...] = reaches[1]
    moved_picked[...] = picks[1]
    depth = jnp.sum(reaches[0], axis=-1, keepdims=True) - 1.0
    length = lengths[stay]
    queries, fresh = rotate(
        projected[:draft], depth, length.astype(jnp.float32), table_row[...], query_width
    )
    compact[...] = dot(picks[0], fresh).astype(jnp.bfloat16)
    finish(pages)
    attended = attend(queries, cache, fresh, reaches[0], length)
    finish(loads[8:])
    kept = (rows[0].astype(jnp.float32) + dot(attended, weights[...])).astype(jnp.bfloat16)
    staying[...] = kept
    parcel[:draft, :] = rms_scale(kept, gains[1])
    finish(store)
    ids = travel_order(slot[0], names_t[...]).astype(jnp.float32)
    blank = jnp.zeros((NOTE - ids.shape[0], ids.shape[1]), jnp.float32)
    parcel[draft:, :] = jnp.zeros((NOTE, parcel.shape[1]), jnp.bfloat16)
    parcel[draft:, : ids.shape[1]] = jnp.concatenate([ids, blank], axis=0).astype(jnp.bfloat16)


def early_kernel(
    slot, me, reach, picked, staying_compact, projected, spectrum, *rest,
):
    sources = rest[:-14]
    (
        pick, stacked, mixed, tops, totals, compact,
        cache, notes, lines, table_row, fresh, note_sems, sems, cache_sem,
    ) = rest[-14:]
    half = cache.shape[0]
    draft = projected.shape[0]
    note_loads = load_all(
        [
            (first.at[pl.ds(half, NOTE), pl.ds(0, 128)], notes.at[i])
            for i, first in enumerate(sources)
        ],
        note_sems,
    )
    loads = load_all(((projected, lines), (spectrum, table_row)), sems)
    depth = jnp.sum(reach[...], axis=-1, keepdims=True) - 1.0
    finish(note_loads)
    chosen = jnp.int32(0)
    length = jnp.int32(0)
    for i, source in enumerate(sources):
        code = jnp.sum(notes[i].astype(jnp.float32)).astype(jnp.int32)
        mine = code // (4 * half) == me[0]
        chosen = jnp.where(mine, i, chosen)
        length = jnp.where(mine, code % (4 * half), length)

        @pl.when(mine)
        def _(source=source):
            pltpu.make_async_copy(source.at[pl.ds(0, half)], cache, cache_sem).start()

    pick[0] = chosen
    pick[1] = length
    finish(loads)
    query_width = QUERY_HEADS * HEAD_SIZE
    queries, rows = rotate(
        lines[...], depth, length.astype(jnp.float32), table_row[...], query_width
    )
    fresh[...] = rows
    own = pl.ds(pl.multiple_of(slot[0] * draft, draft), draft)
    other = pl.ds(pl.multiple_of((1 - slot[0]) * draft, draft), draft)
    compact[own, :] = dot(picked[...], rows).astype(jnp.bfloat16)
    compact[other, :] = staying_compact[...]
    pltpu.make_async_copy(sources[0].at[pl.ds(0, half)], cache, cache_sem).wait()
    scale = HEAD_SIZE ** (-0.5) * LOG2E
    key_width = KEY_VALUE_HEADS * HEAD_SIZE
    in_cache = lax.broadcasted_iota(jnp.int32, (1, half), 1) < length
    cache_bias = jnp.where(in_cache, 0.0, MASKED)
    tree_bias = jnp.concatenate([jnp.where(reach[...] > 0.5, 0.0, MASKED)] * GROUP, axis=0)
    for kv in range(KEY_VALUE_HEADS):
        cols = slice(kv * HEAD_SIZE, (kv + 1) * HEAD_SIZE)
        vcols = slice(key_width + kv * HEAD_SIZE, key_width + (kv + 1) * HEAD_SIZE)
        heads = [
            queries[:, (kv * GROUP + g) * HEAD_SIZE : (kv * GROUP + g + 1) * HEAD_SIZE]
            for g in range(GROUP)
        ]
        asked = jnp.concatenate(heads, axis=0)
        stacked[kv] = asked
        first = dot(asked, cache[:, cols], ((1,), (1,))) * scale + cache_bias
        second = dot(asked, fresh[:, cols], ((1,), (1,))) * scale + tree_bias
        top = jnp.maximum(
            jnp.max(first, axis=-1, keepdims=True), jnp.max(second, axis=-1, keepdims=True)
        )
        first = jnp.exp2(first - top)
        second = jnp.exp2(second - top)
        tops[kv] = top
        totals[kv] = jnp.sum(first, axis=-1, keepdims=True) + jnp.sum(
            second, axis=-1, keepdims=True
        )
        mixed[kv] = dot(first.astype(jnp.bfloat16), cache[:, vcols]) + dot(
            second.astype(jnp.bfloat16), fresh[:, vcols]
        )


def arrival_kernel(
    slot, pick, stacked, mixed, tops, totals, hidden, gain, w_out, *rest,
):
    sources = rest[:-8]
    moved, moved_normed, cache, weights, rows, gains, sems, cache_sem = rest[-8:]
    half = cache.shape[0]
    draft = rows.shape[0]
    for i, source in enumerate(sources):

        @pl.when(pick[0] == i)
        def _(source=source):
            pltpu.make_async_copy(source, cache, cache_sem).start()

    own = pl.ds(pl.multiple_of(slot[0] * draft, draft), draft)
    loads = load_all(((hidden.at[own], rows), (gain, gains), (w_out, weights)), sems)
    scale = HEAD_SIZE ** (-0.5) * LOG2E
    key_width = KEY_VALUE_HEADS * HEAD_SIZE
    in_cache = lax.broadcasted_iota(jnp.int32, (1, half), 1) + half < pick[1]
    bias = jnp.where(in_cache, 0.0, MASKED)
    pltpu.make_async_copy(sources[0], cache, cache_sem).wait()
    outs = []
    for kv in range(KEY_VALUE_HEADS):
        cols = slice(kv * HEAD_SIZE, (kv + 1) * HEAD_SIZE)
        vcols = slice(key_width + kv * HEAD_SIZE, key_width + (kv + 1) * HEAD_SIZE)
        scores = dot(stacked[kv], cache[:, cols], ((1,), (1,))) * scale + bias
        top = jnp.maximum(jnp.max(scores, axis=-1, keepdims=True), tops[kv])
        weight = jnp.exp2(scores - top)
        factor = jnp.exp2(tops[kv] - top)
        total = totals[kv] * factor + jnp.sum(weight, axis=-1, keepdims=True)
        blend = mixed[kv] * factor + dot(weight.astype(jnp.bfloat16), cache[:, vcols])
        blend = (blend / total).astype(jnp.bfloat16)
        outs += [blend[g * draft : (g + 1) * draft] for g in range(GROUP)]
    attended = jnp.concatenate(outs, axis=1)
    finish(loads)
    kept = rows[...].astype(jnp.float32) + dot(attended, weights[...])
    kept = kept.astype(jnp.bfloat16)
    moved[...] = kept
    moved_normed[...] = rms_scale(kept, gains[...])


def pack_kernel(routes, staying, moved, out, rows, sems):
    both = jnp.concatenate([staying[: moved.shape[0], :], moved[...]], axis=0)
    group = rows.shape[0] // 2
    stores = []
    for i in range(2):
        span = pl.ds(i * group, group)
        rows[span] = dot(routes[i * group : (i + 1) * group, :], both).astype(jnp.bfloat16)
        stores += load_all(((rows.at[span], out.at[span]),), sems.at[pl.ds(i, 1)])
    finish(stores)


def expert_kernel(arrived, w_gate, w_up, w_down, out, gates, ups, downs, act, done, sems):
    count, model = out.shape
    hidden_units = gates.shape[1]
    chunk = 256 if hidden_units % 256 == 0 else hidden_units
    wide = 512 if model % 512 == 0 else model
    block = 256 if count % 256 == 0 else count
    chunks = [pl.ds(i * chunk, chunk) for i in range(hidden_units // chunk)]
    wides = [pl.ds(i * wide, wide) for i in range(model // wide)]
    loads = []
    for i, cols in enumerate(chunks):
        pairs = ((w_gate.at[0, :, cols], gates.at[:, cols]), (w_up.at[0, :, cols], ups.at[:, cols]))
        loads.append(load_all(pairs, sems.at[i]))
    down_loads = [
        load_all(((w_down.at[0, :, cols], downs.at[:, cols]),), sems.at[len(chunks) + i])
        for i, cols in enumerate(wides)
    ]
    blocks = [slice(i * block, (i + 1) * block) for i in range(count // block)]
    for load, cols in zip(loads, chunks):
        finish(load)
        for span in blocks:
            rows = arrived[span, :]
            gated = dot(rows, gates[:, cols])
            upped = dot(rows, ups[:, cols])
            act[span, cols] = (jnp.maximum(gated, 0.0) * upped).astype(jnp.bfloat16)
    stores = []
    for i, cols in enumerate(wides):
        finish(down_loads[i])
        for span in blocks:
            done[span, cols] = dot(act[span, :], downs[:, cols]).astype(jnp.bfloat16)
        stores += load_all(((done.at[:, cols], out.at[:, cols]),), sems.at[len(chunks) + i])
    finish(stores)


def partial_kernel(shares, rows, out, pair, sems):
    finish(load_all(((shares.at[1], pair),), sems))
    values = rows[...]
    out[...] = (dot(pair[0], values) + dot(pair[1], values)).astype(jnp.bfloat16)


def near_kernel(shares, staying, moved, arrived, total, pair, kept, rows, sems):
    pairs = (
        (shares.at[0], pair), (staying, kept.at[0]), (moved, kept.at[1]), (arrived, rows),
    )
    finish(load_all(pairs, sems))
    draft = staying.shape[0]
    values = rows[...]
    near = dot(pair[0], values) + dot(pair[1], values)
    total[:draft, :] = kept[0].astype(jnp.float32) + near[:draft]
    total[draft:, :] = kept[1].astype(jnp.float32) + near[draft:]


def final_kernel(slot, total, far, out):
    draft = out.shape[0] // 2
    for i, at in enumerate((1 - slot[0], slot[0])):
        at = pl.ds(pl.multiple_of(at * draft, draft), draft)
        span = slice(i * draft, (i + 1) * draft)
        out[at, :] = (total[span, :] + far[span, :].astype(jnp.float32)).astype(jnp.bfloat16)


def params(mib, rows=512):
    return pltpu.CompilerParams(vmem_limit_bytes=min(60, mib * max(rows, 512) // 512) * MIB)


def cost(flops, moved):
    return pl.CostEstimate(flops=int(flops), bytes_accessed=int(moved), transcendentals=0)


def run_experts(arrived, w_gate, w_up, w_down):
    count, model = arrived.shape
    hidden_units = w_gate.shape[2]
    return pl.pallas_call(
        expert_kernel,
        in_specs=[VMEM] + [HBM] * 3,
        out_specs=HBM,
        out_shape=pltpu.HBM((count, model), jnp.bfloat16),
        scratch_shapes=[
            pltpu.VMEM((model, hidden_units), jnp.bfloat16),
            pltpu.VMEM((model, hidden_units), jnp.bfloat16),
            pltpu.VMEM((hidden_units, model), jnp.bfloat16),
            pltpu.VMEM((count, hidden_units), jnp.bfloat16),
            pltpu.VMEM((count, model), jnp.bfloat16),
            pltpu.SemaphoreType.DMA((8, 2)),
        ],
        compiler_params=params(16 + 3 * count * model // MIB),
        cost_estimate=cost(6 * count * model * hidden_units, 6 * model * hidden_units),
        name="experts",
    )(*in_vmem(arrived), *in_hbm(w_gate, w_up, w_down))


def per_device(
    hidden, parents, path, cache_len, page_table, kv_pool, mig_slot, mig_dest,
    attn_gain, w_qkv, w_out, moe_gain, w_router, expert_ids, w_gate, w_up, w_down,
):
    bf16 = jnp.bfloat16
    requests, draft = parents.shape
    tokens, model = hidden.shape
    req_count = lax.axis_size("req")
    ep_count = lax.axis_size("ep")
    device_count = req_count * ep_count
    half_count = device_count // 2
    experts = w_router.shape[1]
    split = device_count // experts
    pages = page_table.shape[1]
    page, kv_width = kv_pool.shape[1:]
    context = pages * page
    query_width = w_out.shape[0]
    slot_rows = half_count * CAP
    req_index = lax.axis_index("req")
    ep_index = lax.axis_index("ep")
    groups = [[h * half_count + i for i in range(half_count)] for h in range(2)]
    inner = req_count // 4
    swap = [(i, (3 - i // inner) * inner + i % inner) for i in range(req_count)]
    base = (req_index // (req_count // 2) * (experts // 2)).astype(jnp.int32).reshape(1)

    def within_half(rows):
        return lax.all_to_all(rows, AXES, 0, 0, tiled=True, axis_index_groups=groups)

    f32 = jnp.float32
    half_cache = context // 2
    leaving = pl.pallas_call(
        leaving_kernel,
        in_specs=[SMEM] * 4 + [HBM],
        out_specs=[VMEM] * 2,
        out_shape=[
            pltpu.VMEM((half_cache + NOTE, kv_width), bf16),
            pltpu.VMEM((half_cache, kv_width), bf16),
        ],
        scratch_shapes=[pltpu.SemaphoreType.DMA((pages,))],
        compiler_params=params(58),
        cost_estimate=cost(0, 4 * context * kv_width),
        name="leaving",
    )(mig_slot, mig_dest, cache_len, page_table, *in_hbm(kv_pool))
    chips = ep_count // 2
    chip = ep_index // 2
    core = ep_index % 2
    pairs = [(i, i ^ 1) for i in range(ep_count)]
    sibling = [lax.ppermute(part, "ep", pairs) for part in leaving]
    sources = [*leaving, *sibling]
    payloads = []
    for k in range(1, chips):
        target = (chip + k) % chips * 2 + core
        moves = [(i, ((i // 2 + k) % chips) * 2 + i % 2) for i in range(ep_count)]
        for mine, other in zip(leaving, sibling):
            payload = jnp.where(mig_dest[0] == target, mine, other)
            payloads.append(payload)
            sources.append(lax.ppermute(payload, "ep", moves))
    me = ep_index.astype(jnp.int32).reshape(1)

    route_shapes = [
        pltpu.VMEM((slot_rows, tokens), bf16),
        pltpu.HBM((expert_ids.shape[1], tokens), jnp.int32),
    ]
    frequencies = ROPE_BASE ** (-2.0 * np.arange(HEAD_SIZE // 2) / HEAD_SIZE)
    spectrum = jnp.asarray(np.concatenate([frequencies] * 2)[None].astype(np.float32))
    row_gain = attn_gain.reshape(1, model)
    row_moe_gain = moe_gain.reshape(1, model)
    hidden, *_ = lax.optimization_barrier((hidden, *payloads))
    projected, reach, picked, staying_compact, staying, parcel = pl.pallas_call(
        front_kernel,
        in_specs=[SMEM] * 3 + [HBM] * 10,
        out_specs=[HBM] + [VMEM] * 5,
        out_shape=[
            pltpu.HBM((draft, w_qkv.shape[1]), f32),
            pltpu.VMEM((draft, draft), f32),
            pltpu.VMEM((draft, draft), bf16),
            pltpu.VMEM((draft, kv_width), bf16),
            pltpu.VMEM((draft, model), bf16),
            pltpu.VMEM((draft + NOTE, model), bf16),
        ],
        scratch_shapes=[
            pltpu.VMEM(w_out.shape, bf16),
            pltpu.VMEM((tokens, model), bf16),
            pltpu.VMEM(parents.shape, jnp.int32),
            pltpu.VMEM(path.shape, jnp.int32),
            pltpu.VMEM(spectrum.shape, f32),
            pltpu.VMEM((2, 1, model), bf16),
            pltpu.VMEM((expert_ids.shape[1], tokens), jnp.int32),
            pltpu.VMEM(w_qkv.shape, bf16),
            pltpu.VMEM((context, kv_width), bf16),
            pltpu.VMEM((draft, w_qkv.shape[1]), f32),
            pltpu.SemaphoreType.DMA((9,)),
            pltpu.SemaphoreType.DMA((pages,)),
            pltpu.SemaphoreType.DMA((1,)),
        ],
        compiler_params=params(36),
        cost_estimate=cost(3e9, 3e6),
        name="front",
    )(
        mig_slot, cache_len, page_table,
        *in_hbm(
            hidden, parents, path, spectrum, row_gain, row_moe_gain, expert_ids.T, w_qkv, w_out,
            kv_pool,
        ),
    )
    far_parcel = lax.ppermute(parcel, "req", swap)
    names_t, _ = lax.optimization_barrier((expert_ids.T, projected))
    routes, ids = pl.pallas_call(
        functools.partial(routes_kernel, split),
        in_specs=[SMEM, SMEM, HBM],
        out_specs=[VMEM] * 2,
        out_shape=route_shapes,
        scratch_shapes=[
            pltpu.VMEM((expert_ids.shape[1], tokens), jnp.int32),
            pltpu.SemaphoreType.DMA((1,)),
        ],
        compiler_params=params(6, slot_rows),
        cost_estimate=cost(1e8, 1e6),
        name="routes",
    )(base, mig_slot, *in_hbm(names_t))
    early, late = sources[0::2], sources[1::2]
    rows = GROUP * draft
    pick, stacked, mixed, tops, totals, compact = pl.pallas_call(
        early_kernel,
        in_specs=[SMEM] * 2 + [VMEM] * 3 + [HBM] * 2 + [ANY] * len(early),
        out_specs=[SMEM] + [VMEM] * 5,
        out_shape=[
            jax.ShapeDtypeStruct((2,), jnp.int32),
            pltpu.VMEM((KEY_VALUE_HEADS, rows, HEAD_SIZE), bf16),
            pltpu.VMEM((KEY_VALUE_HEADS, rows, HEAD_SIZE), f32),
            pltpu.VMEM((KEY_VALUE_HEADS, rows, 1), f32),
            pltpu.VMEM((KEY_VALUE_HEADS, rows, 1), f32),
            jax.ShapeDtypeStruct((tokens, kv_width), bf16),
        ],
        scratch_shapes=[
            pltpu.VMEM((half_cache, kv_width), bf16),
            pltpu.VMEM((len(early), NOTE, 128), bf16),
            pltpu.VMEM(projected.shape, f32),
            pltpu.VMEM(spectrum.shape, f32),
            pltpu.VMEM((draft, kv_width), bf16),
            pltpu.SemaphoreType.DMA((len(early),)),
            pltpu.SemaphoreType.DMA((2,)),
            pltpu.SemaphoreType.DMA,
        ],
        compiler_params=params(16),
        cost_estimate=cost(1e9, 2e6),
        name="early",
    )(
        mig_slot, me, *in_vmem(reach, picked, staying_compact), *in_hbm(projected, spectrum),
        *early,
    )
    far_parcel, routes, pick, *late = lax.optimization_barrier((far_parcel, routes, pick, *late))
    moved, moved_normed = pl.pallas_call(
        arrival_kernel,
        in_specs=[SMEM] * 2 + [VMEM] * 4 + [HBM] * 3 + [ANY] * len(late),
        out_specs=[VMEM] * 2,
        out_shape=[pltpu.VMEM((draft, model), bf16)] * 2,
        scratch_shapes=[
            pltpu.VMEM((half_cache, kv_width), bf16),
            pltpu.VMEM(w_out.shape, bf16),
            pltpu.VMEM((draft, model), bf16),
            pltpu.VMEM((1, model), bf16),
            pltpu.SemaphoreType.DMA((3,)),
            pltpu.SemaphoreType.DMA,
        ],
        compiler_params=params(16),
        cost_estimate=cost(2e9, 8e6),
        name="arrival",
    )(
        mig_slot, pick, *in_vmem(stacked, mixed, tops, totals),
        *in_hbm(hidden, row_moe_gain, w_out), *late,
    )
    far_moved = lax.ppermute(moved_normed, "req", swap)
    far_routes, far_ids = pl.pallas_call(
        functools.partial(far_routes_kernel, split),
        in_specs=[SMEM, VMEM],
        out_specs=[VMEM] * 2,
        out_shape=route_shapes,
        compiler_params=params(6, slot_rows),
        cost_estimate=cost(1e8, 1e6),
        name="far_routes",
    )(base, *in_vmem(far_parcel))

    def pack(table, first, second):
        return pl.pallas_call(
            pack_kernel,
            in_specs=[VMEM] * 3,
            out_specs=HBM,
            out_shape=pltpu.HBM((slot_rows, model), bf16),
            scratch_shapes=[
                pltpu.VMEM((slot_rows, model), bf16),
                pltpu.SemaphoreType.DMA((2,)),
            ],
            compiler_params=params(10, slot_rows),
            cost_estimate=cost(3e8, 2e6),
            name="pack",
        )(*in_vmem(table, first, second))

    near_packed = pack(routes, parcel, moved_normed)
    far_packed = pack(far_routes, far_parcel, far_moved)
    far_rows = within_half(far_packed)
    near_packed, far_rows = lax.optimization_barrier((near_packed, far_rows))
    near_rows = within_half(near_packed)
    shares = pl.pallas_call(
        functools.partial(shares_kernel, split),
        in_specs=[SMEM, HBM] + [VMEM] * 4 + [HBM] * 2,
        out_specs=HBM,
        out_shape=pltpu.HBM((2, 2, tokens, slot_rows), bf16),
        scratch_shapes=[
            pltpu.VMEM((experts, model), bf16),
            pltpu.VMEM((2,) + ids.shape, jnp.int32),
            pltpu.VMEM((2, 2, tokens, slot_rows), bf16),
            pltpu.SemaphoreType.DMA((3,)),
            pltpu.SemaphoreType.DMA((1,)),
        ],
        compiler_params=params(10, slot_rows),
        cost_estimate=cost(3e8, 1e6),
        name="shares",
    )(
        base, *in_hbm(w_router.T), *in_vmem(parcel, moved_normed, far_parcel, far_moved),
        *in_hbm(ids, far_ids),
    )
    far_out = run_experts(far_rows, w_gate, w_up, w_down)
    far_out, near_rows, shares = lax.optimization_barrier((far_out, near_rows, shares))
    far_back = within_half(far_out)
    near_out = run_experts(near_rows, w_gate, w_up, w_down)
    near_out, far_back = lax.optimization_barrier((near_out, far_back))
    far_sum = pl.pallas_call(
        partial_kernel,
        in_specs=[HBM, VMEM],
        out_specs=VMEM,
        out_shape=pltpu.VMEM((tokens, model), bf16),
        scratch_shapes=[
            pltpu.VMEM((2, tokens, slot_rows), bf16),
            pltpu.SemaphoreType.DMA((1,)),
        ],
        compiler_params=params(8, slot_rows),
        cost_estimate=cost(4e8, 2e6),
        name="partial",
    )(*in_hbm(shares), *in_vmem(far_back))
    own_far = lax.ppermute(far_sum, "req", swap)
    near_back = within_half(near_out)
    total = pl.pallas_call(
        near_kernel,
        in_specs=[HBM] * 3 + [ANY],
        out_specs=VMEM,
        out_shape=pltpu.VMEM((tokens, model), f32),
        scratch_shapes=[
            pltpu.VMEM((2, tokens, slot_rows), bf16),
            pltpu.VMEM((2, draft, model), bf16),
            pltpu.VMEM((slot_rows, model), bf16),
            pltpu.SemaphoreType.DMA((4,)),
        ],
        compiler_params=params(56),
        cost_estimate=cost(4e8, 2e6),
        name="near",
    )(*in_hbm(shares, staying, moved), near_back)
    layer_out = pl.pallas_call(
        final_kernel,
        in_specs=[SMEM] + [VMEM] * 2,
        out_specs=VMEM,
        out_shape=jax.ShapeDtypeStruct((tokens, model), bf16),
        compiler_params=params(8),
        cost_estimate=cost(1e6, 2e6),
        name="final",
    )(mig_slot, *in_vmem(total, own_far))
    return layer_out, compact.reshape(requests, draft, kv_width)


def solution(mesh):
    rows = P(AXES, None)
    blocks = P(AXES, None, None)
    in_specs = (
        rows, rows, rows, P(AXES), rows, blocks, P(AXES), P(AXES),
        P(), P(), P(), P(), P(), rows, blocks, blocks, blocks,
    )
    return jax.shard_map(
        per_device, mesh=mesh, in_specs=in_specs, out_specs=(rows, blocks), check_vma=False
    )
```

```python
import functools

import jax
import jax.numpy as jnp
import numpy as np
from jax import lax
from jax.experimental import pallas as pl
from jax.experimental.pallas import tpu as pltpu
from jax.sharding import PartitionSpec as P

QUERY_HEADS = 12
KEY_VALUE_HEADS = 2
HEAD_SIZE = 128
GROUP = QUERY_HEADS // KEY_VALUE_HEADS
CAP = 32
EPSILON = 1e-06
ROPE_BASE = 1000000.0
MASKED = -1e30
LOG2E = 1.4426950408889634
MIB = 1024 * 1024
NOTE = 16
NOTE_BASE = 32
NOTE_SPAN = 2048
AXES = ("req", "ep")

VMEM = pl.BlockSpec(memory_space=pltpu.VMEM)
SMEM = pl.BlockSpec(memory_space=pltpu.SMEM)
ANY = pl.BlockSpec(memory_space=pl.ANY)
HBM = pl.BlockSpec(memory_space=pltpu.HBM)


def in_hbm(*values):
    return [pltpu.with_memory_space_constraint(value, pltpu.HBM) for value in values]


def in_vmem(*values):
    return [pltpu.with_memory_space_constraint(value, pltpu.VMEM) for value in values]


def load_all(pairs, sems):
    copies = [
        pltpu.make_async_copy(source, target, sems.at[i])
        for i, (source, target) in enumerate(pairs)
    ]
    for copy in copies:
        copy.start()
    return copies


def finish(copies):
    for copy in copies:
        copy.wait()


def dot(a, b, dims=((1,), (0,))):
    return lax.dot_general(a, b, (dims, ((), ())), preferred_element_type=jnp.float32)


def rms_scale(values, scaling):
    widened = values.astype(jnp.float32)
    spread = jnp.mean(widened * widened, axis=-1, keepdims=True)
    return (widened * lax.rsqrt(spread + EPSILON) * scaling.astype(jnp.float32)).astype(
        jnp.bfloat16
    )


def attend(queries, cached, fresh, reach, length):
    scale = HEAD_SIZE ** (-0.5) * LOG2E
    key_width = KEY_VALUE_HEADS * HEAD_SIZE
    context = cached.shape[0]
    in_cache = lax.broadcasted_iota(jnp.int32, (1, context), 1) < length
    cache_bias = jnp.where(in_cache, 0.0, MASKED)
    tree_bias = jnp.concatenate([jnp.where(reach > 0.5, 0.0, MASKED)] * GROUP, axis=0)
    outs = []
    for kv in range(KEY_VALUE_HEADS):
        cols = slice(kv * HEAD_SIZE, (kv + 1) * HEAD_SIZE)
        vcols = slice(key_width + kv * HEAD_SIZE, key_width + (kv + 1) * HEAD_SIZE)
        heads = [
            queries[:, (kv * GROUP + g) * HEAD_SIZE : (kv * GROUP + g + 1) * HEAD_SIZE]
            for g in range(GROUP)
        ]
        stacked = jnp.concatenate(heads, axis=0)
        first = dot(stacked, cached[:, cols], ((1,), (1,))) * scale + cache_bias
        second = dot(stacked, fresh[:, cols], ((1,), (1,))) * scale + tree_bias
        highest = jnp.maximum(
            jnp.max(first, axis=-1, keepdims=True), jnp.max(second, axis=-1, keepdims=True)
        )
        first = jnp.exp2(first - highest)
        second = jnp.exp2(second - highest)
        total = jnp.sum(first, axis=-1, keepdims=True) + jnp.sum(second, axis=-1, keepdims=True)
        mixed = dot(first.astype(jnp.bfloat16), cached[:, vcols])
        mixed = mixed + dot(second.astype(jnp.bfloat16), fresh[:, vcols])
        mixed = (mixed / total).astype(jnp.bfloat16)
        step = queries.shape[0]
        outs += [mixed[g * step : (g + 1) * step] for g in range(GROUP)]
    return jnp.concatenate(outs, axis=1)


def load_pages(table, row, pool, target, sems):
    page = pool.shape[1]
    copies = [
        pltpu.make_async_copy(
            pool.at[table[row, i]], target.at[pl.ds(i * page, page)], sems.at[i]
        )
        for i in range(table.shape[1])
    ]
    for copy in copies:
        copy.start()
    return copies


def leaving_kernel(slot, dest, lengths, table, pool, first, second, sems):
    half, page = first.shape[0] - NOTE, pool.shape[1]
    loads = []
    for i in range(table.shape[1]):
        target = first if i * page < half else second
        span = pl.ds(i * page if i * page < half else i * page - half, page)
        loads.append(
            pltpu.make_async_copy(pool.at[table[slot[0], i]], target.at[span], sems.at[i])
        )
        loads[-1].start()
    length = lengths[slot[0]]
    row = lax.broadcasted_iota(jnp.int32, (NOTE, first.shape[1]), 0)
    lane = lax.broadcasted_iota(jnp.int32, (NOTE, first.shape[1]), 1)
    note = jnp.zeros((NOTE, first.shape[1]), jnp.int32)
    parts = (dest[0] * NOTE_SPAN, length // NOTE_BASE * NOTE_BASE, length % NOTE_BASE)
    for at, value in enumerate(parts):
        note = jnp.where((row == 0) & (lane == at), value, note)
    first[half:, :] = note.astype(jnp.float32).astype(jnp.bfloat16)
    finish(loads)


def slots_of(ids_t, first, shown):
    tokens = ids_t.shape[1]
    names = lax.broadcasted_iota(jnp.int32, (shown, tokens), 0) + first
    assigned = jnp.zeros((shown, tokens), jnp.bool_)
    for k in range(ids_t.shape[0]):
        assigned = assigned | (ids_t[k : k + 1, :] == names)
    before = lax.broadcasted_iota(jnp.int32, (tokens, tokens), 0) < lax.broadcasted_iota(
        jnp.int32, (tokens, tokens), 1
    )
    ranks = dot(one_hot(assigned), one_hot(before))
    return assigned, jnp.where(assigned, ranks, -1.0)


def one_hot(flags):
    return jnp.where(flags, 1.0, 0.0).astype(jnp.bfloat16)


def flipped(values):
    size = values.shape[1]
    same = lax.broadcasted_iota(jnp.int32, (size, size), 0) == lax.broadcasted_iota(
        jnp.int32, (size, size), 1
    )
    if values.shape[0] == 1:
        return jnp.sum(jnp.where(same, values, 0.0), axis=1, keepdims=True)
    return dot(one_hot(same), values.astype(jnp.bfloat16), ((1,), (1,)))


def write_routes(split, first, ids, table):
    shown = table.shape[0] // (split * CAP)
    _, slots = slots_of(ids, first, shown)
    wanted = lax.broadcasted_iota(jnp.int32, (shown, split * CAP, ids.shape[1]), 1) % CAP
    hot = jnp.where(slots.astype(jnp.int32)[:, None, :] == wanted, 1.0, 0.0)
    table[...] = hot.reshape(table.shape).astype(jnp.bfloat16)


def travel_order(slot, ids):
    half = ids.shape[1] // 2
    return jnp.where(slot == 0, jnp.concatenate([ids[:, half:], ids[:, :half]], axis=1), ids)


def routes_kernel(split, base, slot, ids_t, table, ordered, names, sems):
    finish(load_all(((ids_t, names),), sems))
    ids = travel_order(slot[0], names[...])
    ordered[...] = ids
    write_routes(split, base[0], ids, table)


def far_routes_kernel(split, base, parcel, table, ordered):
    draft = parcel.shape[0] - NOTE
    ids = parcel[draft:, : ordered.shape[1]].astype(jnp.float32).astype(jnp.int32)
    ids = ids[: ordered.shape[0]]
    ordered[...] = ids
    write_routes(split, base[0], ids, table)


def shares_kernel(split, base, w_router_t, *rest):
    inputs, out, (weights, names, done, sems, out_sem) = rest[:6], rest[6], rest[7:]
    finish(
        load_all(
            ((w_router_t, weights), (inputs[4], names.at[0]), (inputs[5], names.at[1])), sems
        )
    )
    experts = weights.shape[0]
    tokens, width = done.shape[2:]
    spread = one_hot(
        lax.broadcasted_iota(jnp.int32, (experts, width), 1) // (split * CAP) + base[0]
        == lax.broadcasted_iota(jnp.int32, (experts, width), 0)
    )
    wanted = lax.broadcasted_iota(jnp.int32, (tokens, width), 1) % CAP
    for i in range(2):
        staying, moved = inputs[2 * i : 2 * i + 2]
        rows = jnp.concatenate([staying[: moved.shape[0], :], moved[...]], axis=0)
        logits = dot(rows, weights[...], ((1,), (1,)))
        _, slots_t = slots_of(names.at[i], 0, experts)
        slots = flipped(slots_t)
        squashed = jnp.where(slots >= 0.0, jax.nn.sigmoid(logits), 0.0)
        share = squashed / jnp.sum(squashed, axis=1, keepdims=True)
        hit = dot(slots.astype(jnp.bfloat16), spread).astype(jnp.int32) == wanted
        high = share.astype(jnp.bfloat16)
        low = (share - high.astype(jnp.float32)).astype(jnp.bfloat16)
        done[i, 0] = jnp.where(hit, dot(high, spread), 0.0).astype(jnp.bfloat16)
        done[i, 1] = jnp.where(hit, dot(low, spread), 0.0).astype(jnp.bfloat16)
    finish(load_all(((done, out),), out_sem))


def rotate(projected, depth, length, spectrum, query_width):
    angles = (depth + length) * spectrum
    cosine = jnp.cos(angles)
    sine = jnp.sin(angles)
    first_half = lax.broadcasted_iota(jnp.int32, (1, HEAD_SIZE), 1) < HEAD_SIZE // 2
    sine = jnp.where(first_half, -sine, sine)
    key_width = KEY_VALUE_HEADS * HEAD_SIZE
    turned = []
    for h in range(QUERY_HEADS + KEY_VALUE_HEADS):
        part = projected[:, h * HEAD_SIZE : (h + 1) * HEAD_SIZE]
        swapped = jnp.concatenate([part[:, HEAD_SIZE // 2 :], part[:, : HEAD_SIZE // 2]], axis=1)
        turned.append((part * cosine + swapped * sine).astype(jnp.bfloat16))
    values = projected[:, query_width + key_width :].astype(jnp.bfloat16)
    return (
        jnp.concatenate(turned[:QUERY_HEADS], axis=1),
        jnp.concatenate(turned[QUERY_HEADS:] + [values], axis=1),
    )


def front_kernel(
    slot, lengths, table, hidden, parents, path, spectrum, gain, moe_gain, ids_t, w_qkv, w_out,
    pool, moved_projected, moved_reach, moved_picked, compact, staying, parcel,
    weights, tokens, lines, trees, table_row, gains, names_t, w_in, cache, kept_lines, sems,
    page_sems, out_sem,
):
    stay = 1 - slot[0]
    loads = load_all(
        (
            (hidden, tokens), (gain, gains.at[0]), (w_qkv, w_in), (moe_gain, gains.at[1]),
            (parents, lines), (path, trees), (spectrum, table_row),
            (ids_t, names_t), (w_out, weights),
        ),
        sems,
    )
    pages = load_pages(table, stay, pool, cache, page_sems)
    draft = parents.shape[1]
    query_width = w_out.shape[0]
    finish(loads[:3])
    rows = [
        tokens[pl.ds(pl.multiple_of(r * draft, draft), draft), :] for r in (stay, slot[0])
    ]
    normed = rms_scale(jnp.concatenate(rows, axis=0), gains[0])
    projected = dot(normed, w_in[...])
    names = lax.broadcasted_iota(jnp.int32, (draft, draft), 1)
    itself = names == lax.broadcasted_iota(jnp.int32, (draft, draft), 0)
    finish(loads[3:8])
    reaches = []
    for r in (stay, slot[0]):
        above = flipped(lines[pl.ds(r, 1), :].astype(jnp.float32)).astype(jnp.int32)
        reached = jnp.where((above == names) | itself, 1.0, 0.0)
        for _ in range(max(1, (draft - 1).bit_length())):
            half = reached.astype(jnp.bfloat16)
            reached = jnp.minimum(dot(half, half), 1.0)
        reaches.append(reached)
    picks = [
        one_hot(flipped(trees[pl.ds(r, 1), :].astype(jnp.float32)).astype(jnp.int32) == names)
        for r in (stay, slot[0])
    ]
    kept_lines[...] = projected[draft:]
    store = load_all(((kept_lines, moved_projected),), out_sem)
    moved_reach[...] = reaches[1]
    moved_picked[...] = picks[1]
    depth = jnp.sum(reaches[0], axis=-1, keepdims=True) - 1.0
    length = lengths[stay]
    queries, fresh = rotate(
        projected[:draft], depth, length.astype(jnp.float32), table_row[...], query_width
    )
    compact[...] = dot(picks[0], fresh).astype(jnp.bfloat16)
    finish(pages)
    attended = attend(queries, cache, fresh, reaches[0], length)
    finish(loads[8:])
    kept = (rows[0].astype(jnp.float32) + dot(attended, weights[...])).astype(jnp.bfloat16)
    staying[...] = kept
    parcel[:draft, :] = rms_scale(kept, gains[1])
    finish(store)
    ids = travel_order(slot[0], names_t[...]).astype(jnp.float32)
    blank = jnp.zeros((NOTE - ids.shape[0], ids.shape[1]), jnp.float32)
    parcel[draft:, :] = jnp.zeros((NOTE, parcel.shape[1]), jnp.bfloat16)
    parcel[draft:, : ids.shape[1]] = jnp.concatenate([ids, blank], axis=0).astype(jnp.bfloat16)


def early_kernel(
    slot, me, reach, picked, staying_compact, projected, spectrum, *rest,
):
    sources = rest[:-14]
    (
        pick, stacked, mixed, tops, totals, compact,
        cache, notes, lines, table_row, fresh, note_sems, sems, cache_sem,
    ) = rest[-14:]
    half = cache.shape[0]
    draft = projected.shape[0]
    note_loads = load_all(
        [
            (first.at[pl.ds(half, NOTE), pl.ds(0, 128)], notes.at[i])
            for i, first in enumerate(sources)
        ],
        note_sems,
    )
    loads = load_all(((projected, lines), (spectrum, table_row)), sems)
    depth = jnp.sum(reach[...], axis=-1, keepdims=True) - 1.0
    finish(note_loads)
    chosen = jnp.int32(0)
    length = jnp.int32(0)
    for i, source in enumerate(sources):
        code = jnp.sum(notes[i].astype(jnp.float32)).astype(jnp.int32)
        mine = code // NOTE_SPAN == me[0]
        chosen = jnp.where(mine, i, chosen)
        length = jnp.where(mine, code % NOTE_SPAN, length)

        @pl.when(mine)
        def _(source=source):
            pltpu.make_async_copy(source.at[pl.ds(0, half)], cache, cache_sem).start()

    pick[0] = chosen
    pick[1] = length
    finish(loads)
    query_width = QUERY_HEADS * HEAD_SIZE
    queries, rows = rotate(
        lines[...], depth, length.astype(jnp.float32), table_row[...], query_width
    )
    fresh[...] = rows
    own = pl.ds(pl.multiple_of(slot[0] * draft, draft), draft)
    other = pl.ds(pl.multiple_of((1 - slot[0]) * draft, draft), draft)
    compact[own, :] = dot(picked[...], rows).astype(jnp.bfloat16)
    compact[other, :] = staying_compact[...]
    pltpu.make_async_copy(sources[0].at[pl.ds(0, half)], cache, cache_sem).wait()
    scale = HEAD_SIZE ** (-0.5) * LOG2E
    key_width = KEY_VALUE_HEADS * HEAD_SIZE
    in_cache = lax.broadcasted_iota(jnp.int32, (1, half), 1) < length
    cache_bias = jnp.where(in_cache, 0.0, MASKED)
    tree_bias = jnp.concatenate([jnp.where(reach[...] > 0.5, 0.0, MASKED)] * GROUP, axis=0)
    for kv in range(KEY_VALUE_HEADS):
        cols = slice(kv * HEAD_SIZE, (kv + 1) * HEAD_SIZE)
        vcols = slice(key_width + kv * HEAD_SIZE, key_width + (kv + 1) * HEAD_SIZE)
        heads = [
            queries[:, (kv * GROUP + g) * HEAD_SIZE : (kv * GROUP + g + 1) * HEAD_SIZE]
            for g in range(GROUP)
        ]
        asked = jnp.concatenate(heads, axis=0)
        stacked[kv] = asked
        first = dot(asked, cache[:, cols], ((1,), (1,))) * scale + cache_bias
        second = dot(asked, fresh[:, cols], ((1,), (1,))) * scale + tree_bias
        top = jnp.maximum(
            jnp.max(first, axis=-1, keepdims=True), jnp.max(second, axis=-1, keepdims=True)
        )
        first = jnp.exp2(first - top)
        second = jnp.exp2(second - top)
        tops[kv] = top
        totals[kv] = jnp.sum(first, axis=-1, keepdims=True) + jnp.sum(
            second, axis=-1, keepdims=True
        )
        mixed[kv] = dot(first.astype(jnp.bfloat16), cache[:, vcols]) + dot(
            second.astype(jnp.bfloat16), fresh[:, vcols]
        )


def arrival_kernel(
    first_rows, slot, pick, stacked, mixed, tops, totals, hidden, gain, w_out, *rest,
):
    sources = rest[:-8]
    moved, moved_normed, cache, weights, rows, gains, sems, cache_sem = rest[-8:]
    half = cache.shape[0]
    draft = rows.shape[0]
    for i, source in enumerate(sources):

        @pl.when(pick[0] == i)
        def _(source=source):
            pltpu.make_async_copy(source, cache, cache_sem).start()

    own = pl.ds(pl.multiple_of(slot[0] * draft, draft), draft)
    loads = load_all(((hidden.at[own], rows), (gain, gains), (w_out, weights)), sems)
    scale = HEAD_SIZE ** (-0.5) * LOG2E
    key_width = KEY_VALUE_HEADS * HEAD_SIZE
    in_cache = lax.broadcasted_iota(jnp.int32, (1, half), 1) + first_rows < pick[1]
    bias = jnp.where(in_cache, 0.0, MASKED)
    pltpu.make_async_copy(sources[0], cache, cache_sem).wait()
    outs = []
    for kv in range(KEY_VALUE_HEADS):
        cols = slice(kv * HEAD_SIZE, (kv + 1) * HEAD_SIZE)
        vcols = slice(key_width + kv * HEAD_SIZE, key_width + (kv + 1) * HEAD_SIZE)
        scores = dot(stacked[kv], cache[:, cols], ((1,), (1,))) * scale + bias
        top = jnp.maximum(jnp.max(scores, axis=-1, keepdims=True), tops[kv])
        weight = jnp.exp2(scores - top)
        factor = jnp.exp2(tops[kv] - top)
        total = totals[kv] * factor + jnp.sum(weight, axis=-1, keepdims=True)
        blend = mixed[kv] * factor + dot(weight.astype(jnp.bfloat16), cache[:, vcols])
        blend = (blend / total).astype(jnp.bfloat16)
        outs += [blend[g * draft : (g + 1) * draft] for g in range(GROUP)]
    attended = jnp.concatenate(outs, axis=1)
    finish(loads)
    kept = rows[...].astype(jnp.float32) + dot(attended, weights[...])
    kept = kept.astype(jnp.bfloat16)
    moved[...] = kept
    moved_normed[...] = rms_scale(kept, gains[...])


def pack_kernel(routes, staying, moved, out, rows, sems):
    both = jnp.concatenate([staying[: moved.shape[0], :], moved[...]], axis=0)
    group = rows.shape[0] // 2
    stores = []
    for i in range(2):
        span = pl.ds(i * group, group)
        rows[span] = dot(routes[i * group : (i + 1) * group, :], both).astype(jnp.bfloat16)
        stores += load_all(((rows.at[span], out.at[span]),), sems.at[pl.ds(i, 1)])
    finish(stores)


def expert_kernel(arrived, w_gate, w_up, w_down, out, gates, ups, downs, act, done, sems):
    count, model = out.shape
    hidden_units = gates.shape[1]
    chunk = 256 if hidden_units % 256 == 0 else hidden_units
    wide = 512 if model % 512 == 0 else model
    block = 256 if count % 256 == 0 else count
    chunks = [pl.ds(i * chunk, chunk) for i in range(hidden_units // chunk)]
    wides = [pl.ds(i * wide, wide) for i in range(model // wide)]
    loads = []
    for i, cols in enumerate(chunks):
        pairs = ((w_gate.at[0, :, cols], gates.at[:, cols]), (w_up.at[0, :, cols], ups.at[:, cols]))
        loads.append(load_all(pairs, sems.at[i]))
    down_loads = [
        load_all(((w_down.at[0, :, cols], downs.at[:, cols]),), sems.at[len(chunks) + i])
        for i, cols in enumerate(wides)
    ]
    blocks = [slice(i * block, (i + 1) * block) for i in range(count // block)]
    for load, cols in zip(loads, chunks):
        finish(load)
        for span in blocks:
            rows = arrived[span, :]
            gated = dot(rows, gates[:, cols])
            upped = dot(rows, ups[:, cols])
            act[span, cols] = (jnp.maximum(gated, 0.0) * upped).astype(jnp.bfloat16)
    stores = []
    for i, cols in enumerate(wides):
        finish(down_loads[i])
        for span in blocks:
            done[span, cols] = dot(act[span, :], downs[:, cols]).astype(jnp.bfloat16)
        stores += load_all(((done.at[:, cols], out.at[:, cols]),), sems.at[len(chunks) + i])
    finish(stores)


def partial_kernel(shares, rows, out, pair, sems):
    finish(load_all(((shares.at[1], pair),), sems))
    values = rows[...]
    out[...] = (dot(pair[0], values) + dot(pair[1], values)).astype(jnp.bfloat16)


def near_kernel(shares, staying, moved, arrived, total, pair, kept, rows, sems):
    pairs = (
        (shares.at[0], pair), (staying, kept.at[0]), (moved, kept.at[1]), (arrived, rows),
    )
    finish(load_all(pairs, sems))
    draft = staying.shape[0]
    values = rows[...]
    near = dot(pair[0], values) + dot(pair[1], values)
    total[:draft, :] = kept[0].astype(jnp.float32) + near[:draft]
    total[draft:, :] = kept[1].astype(jnp.float32) + near[draft:]


def final_kernel(slot, total, far, out):
    draft = out.shape[0] // 2
    for i, at in enumerate((1 - slot[0], slot[0])):
        at = pl.ds(pl.multiple_of(at * draft, draft), draft)
        span = slice(i * draft, (i + 1) * draft)
        out[at, :] = (total[span, :] + far[span, :].astype(jnp.float32)).astype(jnp.bfloat16)


def params(mib, rows=512):
    return pltpu.CompilerParams(vmem_limit_bytes=min(60, mib * max(rows, 512) // 512) * MIB)


def cost(flops, moved):
    return pl.CostEstimate(flops=int(flops), bytes_accessed=int(moved), transcendentals=0)


def run_experts(arrived, w_gate, w_up, w_down):
    count, model = arrived.shape
    hidden_units = w_gate.shape[2]
    return pl.pallas_call(
        expert_kernel,
        in_specs=[VMEM] + [HBM] * 3,
        out_specs=HBM,
        out_shape=pltpu.HBM((count, model), jnp.bfloat16),
        scratch_shapes=[
            pltpu.VMEM((model, hidden_units), jnp.bfloat16),
            pltpu.VMEM((model, hidden_units), jnp.bfloat16),
            pltpu.VMEM((hidden_units, model), jnp.bfloat16),
            pltpu.VMEM((count, hidden_units), jnp.bfloat16),
            pltpu.VMEM((count, model), jnp.bfloat16),
            pltpu.SemaphoreType.DMA((8, 2)),
        ],
        compiler_params=params(16 + 3 * count * model // MIB),
        cost_estimate=cost(6 * count * model * hidden_units, 6 * model * hidden_units),
        name="experts",
    )(*in_vmem(arrived), *in_hbm(w_gate, w_up, w_down))


def per_device(
    hidden, parents, path, cache_len, page_table, kv_pool, mig_slot, mig_dest,
    attn_gain, w_qkv, w_out, moe_gain, w_router, expert_ids, w_gate, w_up, w_down,
):
    bf16 = jnp.bfloat16
    requests, draft = parents.shape
    tokens, model = hidden.shape
    req_count = lax.axis_size("req")
    ep_count = lax.axis_size("ep")
    device_count = req_count * ep_count
    half_count = device_count // 2
    experts = w_router.shape[1]
    split = device_count // experts
    pages = page_table.shape[1]
    page, kv_width = kv_pool.shape[1:]
    context = pages * page
    query_width = w_out.shape[0]
    slot_rows = half_count * CAP
    req_index = lax.axis_index("req")
    ep_index = lax.axis_index("ep")
    groups = [[h * half_count + i for i in range(half_count)] for h in range(2)]
    inner = req_count // 4
    swap = [(i, (3 - i // inner) * inner + i % inner) for i in range(req_count)]
    base = (req_index // (req_count // 2) * (experts // 2)).astype(jnp.int32).reshape(1)

    def within_half(rows):
        return lax.all_to_all(rows, AXES, 0, 0, tiled=True, axis_index_groups=groups)

    f32 = jnp.float32
    first_rows = pages * 3 // 8 * page
    last_rows = context - first_rows
    leaving = pl.pallas_call(
        leaving_kernel,
        in_specs=[SMEM] * 4 + [HBM],
        out_specs=[VMEM] * 2,
        out_shape=[
            pltpu.VMEM((first_rows + NOTE, kv_width), bf16),
            pltpu.VMEM((last_rows, kv_width), bf16),
        ],
        scratch_shapes=[pltpu.SemaphoreType.DMA((pages,))],
        compiler_params=params(58),
        cost_estimate=cost(0, 4 * context * kv_width),
        name="leaving",
    )(mig_slot, mig_dest, cache_len, page_table, *in_hbm(kv_pool))
    chips = ep_count // 2
    chip = ep_index // 2
    core = ep_index % 2
    pairs = [(i, i ^ 1) for i in range(ep_count)]
    sibling = [lax.ppermute(part, "ep", pairs) for part in leaving]
    sources = [*leaving, *sibling]
    payloads = []
    for k in range(1, chips):
        target = (chip + k) % chips * 2 + core
        moves = [(i, ((i // 2 + k) % chips) * 2 + i % 2) for i in range(ep_count)]
        for mine, other in zip(leaving, sibling):
            payload = jnp.where(mig_dest[0] == target, mine, other)
            payloads.append(payload)
            sources.append(lax.ppermute(payload, "ep", moves))
    me = ep_index.astype(jnp.int32).reshape(1)

    route_shapes = [
        pltpu.VMEM((slot_rows, tokens), bf16),
        pltpu.HBM((expert_ids.shape[1], tokens), jnp.int32),
    ]
    frequencies = ROPE_BASE ** (-2.0 * np.arange(HEAD_SIZE // 2) / HEAD_SIZE)
    spectrum = jnp.asarray(np.concatenate([frequencies] * 2)[None].astype(np.float32))
    row_gain = attn_gain.reshape(1, model)
    row_moe_gain = moe_gain.reshape(1, model)
    hidden, *_ = lax.optimization_barrier((hidden, *payloads))
    projected, reach, picked, staying_compact, staying, parcel = pl.pallas_call(
        front_kernel,
        in_specs=[SMEM] * 3 + [HBM] * 10,
        out_specs=[HBM] + [VMEM] * 5,
        out_shape=[
            pltpu.HBM((draft, w_qkv.shape[1]), f32),
            pltpu.VMEM((draft, draft), f32),
            pltpu.VMEM((draft, draft), bf16),
            pltpu.VMEM((draft, kv_width), bf16),
            pltpu.VMEM((draft, model), bf16),
            pltpu.VMEM((draft + NOTE, model), bf16),
        ],
        scratch_shapes=[
            pltpu.VMEM(w_out.shape, bf16),
            pltpu.VMEM((tokens, model), bf16),
            pltpu.VMEM(parents.shape, jnp.int32),
            pltpu.VMEM(path.shape, jnp.int32),
            pltpu.VMEM(spectrum.shape, f32),
            pltpu.VMEM((2, 1, model), bf16),
            pltpu.VMEM((expert_ids.shape[1], tokens), jnp.int32),
            pltpu.VMEM(w_qkv.shape, bf16),
            pltpu.VMEM((context, kv_width), bf16),
            pltpu.VMEM((draft, w_qkv.shape[1]), f32),
            pltpu.SemaphoreType.DMA((9,)),
            pltpu.SemaphoreType.DMA((pages,)),
            pltpu.SemaphoreType.DMA((1,)),
        ],
        compiler_params=params(36),
        cost_estimate=cost(3e9, 3e6),
        name="front",
    )(
        mig_slot, cache_len, page_table,
        *in_hbm(
            hidden, parents, path, spectrum, row_gain, row_moe_gain, expert_ids.T, w_qkv, w_out,
            kv_pool,
        ),
    )
    far_parcel = lax.ppermute(parcel, "req", swap)
    names_t, _ = lax.optimization_barrier((expert_ids.T, projected))
    routes, ids = pl.pallas_call(
        functools.partial(routes_kernel, split),
        in_specs=[SMEM, SMEM, HBM],
        out_specs=[VMEM] * 2,
        out_shape=route_shapes,
        scratch_shapes=[
            pltpu.VMEM((expert_ids.shape[1], tokens), jnp.int32),
            pltpu.SemaphoreType.DMA((1,)),
        ],
        compiler_params=params(6, slot_rows),
        cost_estimate=cost(1e8, 1e6),
        name="routes",
    )(base, mig_slot, *in_hbm(names_t))
    early, late = sources[0::2], sources[1::2]
    rows = GROUP * draft
    pick, stacked, mixed, tops, totals, compact = pl.pallas_call(
        early_kernel,
        in_specs=[SMEM] * 2 + [VMEM] * 3 + [HBM] * 2 + [ANY] * len(early),
        out_specs=[SMEM] + [VMEM] * 5,
        out_shape=[
            jax.ShapeDtypeStruct((2,), jnp.int32),
            pltpu.VMEM((KEY_VALUE_HEADS, rows, HEAD_SIZE), bf16),
            pltpu.VMEM((KEY_VALUE_HEADS, rows, HEAD_SIZE), f32),
            pltpu.VMEM((KEY_VALUE_HEADS, rows, 1), f32),
            pltpu.VMEM((KEY_VALUE_HEADS, rows, 1), f32),
            jax.ShapeDtypeStruct((tokens, kv_width), bf16),
        ],
        scratch_shapes=[
            pltpu.VMEM((first_rows, kv_width), bf16),
            pltpu.VMEM((len(early), NOTE, 128), bf16),
            pltpu.VMEM(projected.shape, f32),
            pltpu.VMEM(spectrum.shape, f32),
            pltpu.VMEM((draft, kv_width), bf16),
            pltpu.SemaphoreType.DMA((len(early),)),
            pltpu.SemaphoreType.DMA((2,)),
            pltpu.SemaphoreType.DMA,
        ],
        compiler_params=params(16),
        cost_estimate=cost(1e9, 2e6),
        name="early",
    )(
        mig_slot, me, *in_vmem(reach, picked, staying_compact), *in_hbm(projected, spectrum),
        *early,
    )
    far_parcel, routes, pick, *late = lax.optimization_barrier((far_parcel, routes, pick, *late))
    moved, moved_normed = pl.pallas_call(
        functools.partial(arrival_kernel, first_rows),
        in_specs=[SMEM] * 2 + [VMEM] * 4 + [HBM] * 3 + [ANY] * len(late),
        out_specs=[VMEM] * 2,
        out_shape=[pltpu.VMEM((draft, model), bf16)] * 2,
        scratch_shapes=[
            pltpu.VMEM((last_rows, kv_width), bf16),
            pltpu.VMEM(w_out.shape, bf16),
            pltpu.VMEM((draft, model), bf16),
            pltpu.VMEM((1, model), bf16),
            pltpu.SemaphoreType.DMA((3,)),
            pltpu.SemaphoreType.DMA,
        ],
        compiler_params=params(16),
        cost_estimate=cost(2e9, 8e6),
        name="arrival",
    )(
        mig_slot, pick, *in_vmem(stacked, mixed, tops, totals),
        *in_hbm(hidden, row_moe_gain, w_out), *late,
    )
    far_moved = lax.ppermute(moved_normed, "req", swap)
    far_routes, far_ids = pl.pallas_call(
        functools.partial(far_routes_kernel, split),
        in_specs=[SMEM, VMEM],
        out_specs=[VMEM] * 2,
        out_shape=route_shapes,
        compiler_params=params(6, slot_rows),
        cost_estimate=cost(1e8, 1e6),
        name="far_routes",
    )(base, *in_vmem(far_parcel))

    def pack(table, first, second):
        return pl.pallas_call(
            pack_kernel,
            in_specs=[VMEM] * 3,
            out_specs=HBM,
            out_shape=pltpu.HBM((slot_rows, model), bf16),
            scratch_shapes=[
                pltpu.VMEM((slot_rows, model), bf16),
                pltpu.SemaphoreType.DMA((2,)),
            ],
            compiler_params=params(10, slot_rows),
            cost_estimate=cost(3e8, 2e6),
            name="pack",
        )(*in_vmem(table, first, second))

    near_packed = pack(routes, parcel, moved_normed)
    far_packed = pack(far_routes, far_parcel, far_moved)
    far_rows = within_half(far_packed)
    near_packed, far_rows = lax.optimization_barrier((near_packed, far_rows))
    near_rows = within_half(near_packed)
    shares = pl.pallas_call(
        functools.partial(shares_kernel, split),
        in_specs=[SMEM, HBM] + [VMEM] * 4 + [HBM] * 2,
        out_specs=HBM,
        out_shape=pltpu.HBM((2, 2, tokens, slot_rows), bf16),
        scratch_shapes=[
            pltpu.VMEM((experts, model), bf16),
            pltpu.VMEM((2,) + ids.shape, jnp.int32),
            pltpu.VMEM((2, 2, tokens, slot_rows), bf16),
            pltpu.SemaphoreType.DMA((3,)),
            pltpu.SemaphoreType.DMA((1,)),
        ],
        compiler_params=params(10, slot_rows),
        cost_estimate=cost(3e8, 1e6),
        name="shares",
    )(
        base, *in_hbm(w_router.T), *in_vmem(parcel, moved_normed, far_parcel, far_moved),
        *in_hbm(ids, far_ids),
    )
    far_out = run_experts(far_rows, w_gate, w_up, w_down)
    far_out, near_rows, shares = lax.optimization_barrier((far_out, near_rows, shares))
    far_back = within_half(far_out)
    near_out = run_experts(near_rows, w_gate, w_up, w_down)
    near_out, far_back = lax.optimization_barrier((near_out, far_back))
    far_sum = pl.pallas_call(
        partial_kernel,
        in_specs=[HBM, VMEM],
        out_specs=VMEM,
        out_shape=pltpu.VMEM((tokens, model), bf16),
        scratch_shapes=[
            pltpu.VMEM((2, tokens, slot_rows), bf16),
            pltpu.SemaphoreType.DMA((1,)),
        ],
        compiler_params=params(8, slot_rows),
        cost_estimate=cost(4e8, 2e6),
        name="partial",
    )(*in_hbm(shares), *in_vmem(far_back))
    own_far = lax.ppermute(far_sum, "req", swap)
    near_back = within_half(near_out)
    total = pl.pallas_call(
        near_kernel,
        in_specs=[HBM] * 3 + [ANY],
        out_specs=VMEM,
        out_shape=pltpu.VMEM((tokens, model), f32),
        scratch_shapes=[
            pltpu.VMEM((2, tokens, slot_rows), bf16),
            pltpu.VMEM((2, draft, model), bf16),
            pltpu.VMEM((slot_rows, model), bf16),
            pltpu.SemaphoreType.DMA((4,)),
        ],
        compiler_params=params(56),
        cost_estimate=cost(4e8, 2e6),
        name="near",
    )(*in_hbm(shares, staying, moved), near_back)
    layer_out = pl.pallas_call(
        final_kernel,
        in_specs=[SMEM] + [VMEM] * 2,
        out_specs=VMEM,
        out_shape=jax.ShapeDtypeStruct((tokens, model), bf16),
        compiler_params=params(8),
        cost_estimate=cost(1e6, 2e6),
        name="final",
    )(mig_slot, *in_vmem(total, own_far))
    return layer_out, compact.reshape(requests, draft, kv_width)


def solution(mesh):
    rows = P(AXES, None)
    blocks = P(AXES, None, None)
    in_specs = (
        rows, rows, rows, P(AXES), rows, blocks, P(AXES), P(AXES),
        P(), P(), P(), P(), P(), rows, blocks, blocks, blocks,
    )
    return jax.shard_map(
        per_device, mesh=mesh, in_specs=in_specs, out_specs=(rows, blocks), check_vma=False
    )
```
